32 devices in a mesh: section: 2 (over x), dp: 4 (over y, core), seq: 4 (over z).
Axes of the slice: x: 2, y: 2, z: 4, core: 2. Of those that a mesh axis runs over, the one named last changes fastest.
Arguments:
- tokens: bfloat16 [16, 1024, 1536], P('dp', 'seq'), may hold values from -6 to 6
- cotangent: bfloat16 [16, 1024, 1536], P('dp', 'seq'), may hold values from -6 to 6
- in_proj: bfloat16 [2, 1536, 6448], P('section', ('dp', 'seq')), may hold values from -0.15625 to 0.15625
- out_proj: bfloat16 [2, 3072, 1536], P('section', ('dp', 'seq')), may hold values from -0.109375 to 0.109375
- conv_weight: bfloat16 [2, 4, 3328], P('section', None, ('dp', 'seq')), may hold values from -3 to 3
- conv_bias: bfloat16 [2, 3328], P('section', ('dp', 'seq')), may hold values from -3 to 3
- norm_gain: bfloat16 [2, 1536], P('section', ('dp', 'seq')), may hold values from 0.5 to 1.5
- gate_gain: bfloat16 [2, 3072], P('section', ('dp', 'seq')), may hold values from 0.5 to 1.5
- step_bias: float32 [2, 48], P('section'), may hold values from -7 to -2
- log_decay: float32 [2, 48], P('section'), may hold values from -1 to 2
- skip_gain: float32 [2, 48], P('section'), may hold values from 0.5 to 1.5
Outputs:
- activations: bfloat16 [2, 16, 1024, 1536], P('section', 'dp', 'seq')
- input_grads: float32 [2, 16, 1024, 1536], P('section', 'dp', 'seq')
- grad_in_proj: float32 [2, 1536, 6448], P('section', ('dp', 'seq'))
- grad_out_proj: float32 [2, 3072, 1536], P('section', ('dp', 'seq'))
- grad_conv_weight: float32 [2, 4, 3328], P('section', None, ('dp', 'seq'))
- grad_conv_bias: float32 [2, 3328], P('section', ('dp', 'seq'))
- grad_norm_gain: float32 [2, 1536], P('section', ('dp', 'seq'))
- grad_gate_gain: float32 [2, 3072], P('section', ('dp', 'seq'))
- grad_step_bias: float32 [2, 48], P('section')
- grad_log_decay: float32 [2, 48], P('section')
- grad_skip_gain: float32 [2, 48], P('section')
The draws below stay inside these ranges and needn't reach their ends.
All inputs are finite; a program needn't handle non-finite values.
Results may differ from the reference program's by a relative error of at most 0.012.
The reference program's roundings to bfloat16 on the way count: a program that leaves them out, or rounds other values in their place, can miss the bound.
Values may be sent and summed in bfloat16 or wider, within the bound.
No kernel may reach another device: no remote copies, remote signals or barrier semaphores. Data moves between devices by JAX's collectives and lax.ppermute only.
A program may use at most 448 MiB of HBM per device.

```python
import jax
import jax.numpy as jnp
from jax import lax

D = 1536
HEADS = 48
HEAD_DIM = 64
STATE = 128
CONV = 4
BLOCK = 256
DI = 3072
CH = 3328
PROJ = 6448
BATCH = 16
SEQ_LEN = 1024
N_SECTION = 2


def steps_of(rng, shape, shards, least, top_value):
    def one(dim, blocks):
        draws = jax.random.uniform(jax.random.fold_in(jax.random.fold_in(rng, 6), dim), (blocks,), jnp.float32, least / len(shards), top_value / len(shards))
        return jnp.repeat(jnp.exp(draws), shape[dim] // blocks).reshape((-1,) + (1,) * (len(shape) - dim - 1))

    factor_of = one(*shards[0])
    for cut in shards[1:]:
        factor_of = factor_of * one(*cut)
    return factor_of


def noise(rng, extent, width, reach, cuts=(), dtype=jnp.bfloat16):
    level = steps_of(rng, extent, cuts, -0.22, 0.18) if cuts else 1.0
    entries = jax.random.normal(rng, extent, jnp.float32) * width * level
    return jnp.minimum(jnp.maximum(entries, -reach), reach).astype(dtype)


def setup_inputs(seed: int = 0) -> dict:
    arg_keys = jax.random.split(jax.random.key(seed), 12)
    return {
        "tokens": noise(arg_keys[0], (BATCH, SEQ_LEN, D), 1.0, 6.0, ((0, 4), (1, 4))),
        "cotangent": noise(arg_keys[1], (BATCH, SEQ_LEN, D), 1.0, 6.0, ((0, 4), (1, 4))),
        "in_proj": noise(arg_keys[2], (N_SECTION, D, PROJ), D ** -0.5, 0.15625, ((0, 2), (1, 16))),
        "out_proj": noise(arg_keys[3], (N_SECTION, DI, D), DI ** -0.5, 0.109375, ((0, 2), (1, 16))),
        "conv_weight": noise(arg_keys[4], (N_SECTION, CONV, CH), CONV ** -0.5, 3.0, ((0, 2), (2, 16))),
        "conv_bias": noise(arg_keys[5], (N_SECTION, CH), 0.5, 3.0, ((0, 2), (1, 16))),
        "norm_gain": jnp.clip(1.0 + 0.1 * jax.random.normal(arg_keys[6], (N_SECTION, D), jnp.float32), 0.5, 1.5).astype(jnp.bfloat16),
        "gate_gain": jnp.clip(1.0 + 0.1 * jax.random.normal(arg_keys[7], (N_SECTION, DI), jnp.float32), 0.5, 1.5).astype(jnp.bfloat16),
        "step_bias": jnp.clip(-7.0 + 5.0 * jax.random.uniform(arg_keys[8], (N_SECTION, HEADS), jnp.float32) ** steps_of(arg_keys[8], (N_SECTION, HEADS), ((0, 2),), -0.2, 0.2), -7.0, -2.0),
        "log_decay": jnp.clip(-1.0 + 3.0 * jax.random.uniform(arg_keys[9], (N_SECTION, HEADS), jnp.float32) ** steps_of(arg_keys[9], (N_SECTION, HEADS), ((0, 2),), -0.2, 0.2), -1.0, 2.0),
        "skip_gain": jnp.clip(0.5 + 1.0 * jax.random.uniform(arg_keys[10], (N_SECTION, HEADS), jnp.float32) ** steps_of(arg_keys[10], (N_SECTION, HEADS), ((0, 2),), -0.2, 0.2), 0.5, 1.5),
    }


@jax.custom_vjp
def low(v):
    return lax.optimization_barrier(v.astype(jnp.bfloat16)).astype(jnp.float32)

@jax.custom_vjp
def low_back(v):
    return v

def low_keep(v):
    return (low(v), None)

def low_pass(kept, grad):
    return (grad,)

def back_keep(v):
    return (v, None)

def back_low(kept, grad):
    return (low(grad),)
low.defvjp(low_keep, low_pass)
low_back.defvjp(back_keep, back_low)
eps_norm = 1e-05
highest = lax.Precision.HIGHEST

def rms_scale(hidden, gains):
    return hidden * lax.rsqrt(lax.optimization_barrier(jnp.mean(hidden * hidden, axis=-1, keepdims=True)) + eps_norm) * gains

def block_step(carry_state, block_pieces, step_bias, log_decay, skip_gain):
    values, b_rows, c_rows, step_raw = block_pieces
    step_size = jax.nn.softplus(step_raw + step_bias)
    cumulative = jnp.cumsum(step_size * -jnp.exp(log_decay), axis=0)
    length = cumulative.shape[0]
    causal = jnp.arange(length)[:, None] >= jnp.arange(length)[None, :]
    cum_heads = cumulative.T
    segment = jnp.where(causal, cum_heads[:, :, None] - cum_heads[:, None, :], -1e+30)
    scores = jnp.einsum('qn,kn->qk', c_rows, b_rows, precision=highest)
    mixing = jnp.exp(segment) * scores[None] * step_size.T[:, None, :]
    within = jnp.einsum('hqk,khp->qhp', mixing, values, precision=highest)
    carried = jnp.einsum('qn,hpn->qhp', c_rows, carry_state, precision=highest) * jnp.exp(cumulative)[:, :, None]
    totals = cumulative[-1]
    weights_in = jnp.exp(totals[None, :] - cumulative) * step_size
    fresh_state = jnp.einsum('qh,qhp,qn->hpn', weights_in, values, b_rows, precision=highest)
    new_state = jnp.exp(totals)[:, None, None] * carry_state + fresh_state
    return (new_state, within + carried + skip_gain[:, None] * values)

def mixer_layer(hidden, params):
    in_w, out_w, conv_taps, conv_shift, gain_in, gain_gate, step_bias, log_decay, skip_gain = params
    normed = low(rms_scale(hidden, gain_in))
    projected = low_back(jnp.dot(normed, in_w, precision=highest))
    gate_part = projected[:, :DI]
    conv_in = low(projected[:, DI:2 * DI + 2 * STATE])
    step_raw = projected[:, 2 * DI + 2 * STATE:]
    length = hidden.shape[0]
    padded = jnp.concatenate([jnp.zeros((CONV - 1, conv_in.shape[1]), jnp.float32), conv_in], axis=0)
    summed = conv_shift
    for offset in range(CONV):
        summed = summed + padded[offset:offset + length] * conv_taps[offset]
    activated = low(jax.nn.silu(summed))
    blocks = length // BLOCK
    pieces = (activated[:, :DI].reshape(blocks, BLOCK, HEADS, HEAD_DIM), activated[:, DI:DI + STATE].reshape(blocks, BLOCK, STATE), activated[:, DI + STATE:].reshape(blocks, BLOCK, STATE), step_raw.reshape(blocks, BLOCK, HEADS))

    def advance(carry_state, block_pieces):
        return block_step(carry_state, block_pieces, step_bias, log_decay, skip_gain)
    final_state, outputs = lax.scan(jax.checkpoint(advance), jnp.zeros((HEADS, HEAD_DIM, STATE), jnp.float32), pieces)
    gated = outputs.reshape(length, DI) * jax.nn.silu(gate_part)
    gate_out = low(rms_scale(gated, gain_gate))
    return hidden + low_back(jnp.dot(gate_out, out_w, precision=highest))

def network(seq_tokens, mid_probe, stacked):
    first_layer = tuple((piece[0] for piece in stacked))
    second_layer = tuple((piece[1] for piece in stacked))
    middle = low(low_back(mixer_layer(seq_tokens, first_layer))) + mid_probe
    return (mixer_layer(middle, second_layer), middle)

def reference(tokens, cotangent, in_proj, out_proj, conv_weight, conv_bias, norm_gain, gate_gain, step_bias, log_decay, skip_gain):
    params = tuple((piece.astype(jnp.float32) for piece in (in_proj, out_proj, conv_weight, conv_bias, norm_gain, gate_gain, step_bias, log_decay, skip_gain)))

    def per_sequence(totals, inputs):
        seq_tokens, seq_cot = inputs
        tokens_float = seq_tokens.astype(jnp.float32)
        mid_probe = jnp.zeros_like(tokens_float)
        last_out, pull_back, middle = jax.vjp(network, tokens_float, mid_probe, params, has_aux=True)
        token_grads, probe_grads, param_grads = pull_back(seq_cot.astype(jnp.float32))
        totals = jax.tree.map(jnp.add, totals, param_grads)
        return (totals, (middle.astype(jnp.bfloat16), last_out.astype(jnp.bfloat16), token_grads, probe_grads))
    zero_grads = tuple((jnp.zeros_like(piece) for piece in params))
    totals, (mid_rows, last_rows, token_grads, probe_grads) = lax.scan(per_sequence, zero_grads, (tokens, cotangent))
    activations = jnp.stack([mid_rows, last_rows])
    input_grads = jnp.stack([token_grads, probe_grads])
    return (activations, input_grads, totals[0], totals[1], totals[2], totals[3], totals[4], totals[5], totals[6], totals[7], totals[8])
```

```python
import jax
import jax.numpy as jnp
import numpy as np
from jax import lax
from jax.experimental import pallas as pl
from jax.experimental.pallas import tpu as pltpu
from jax.sharding import PartitionSpec as P

D = 1536
HEADS = 48
HEAD_DIM = 64
STATE = 128
CONV = 4
DI = 3072
BC = 2 * STATE
TAIL = BC + 128
GROUP = 8
WIDTH = GROUP * HEAD_DIM
GROUPS = HEADS // GROUP
OUT_TILE = 256
LANES = 128
EPS = 1e-05
f32 = jnp.float32
bf16 = jnp.bfloat16
VMEM_LIMIT = 56 * 2**20
NN = ((1,), (0,))
NT = ((1,), (1,))
TN = ((0,), (0,))


def dot(a, b, dims, precision=None):
    return lax.dot_general(a, b, (dims, ((), ())), preferred_element_type=f32, precision=precision)


def halves(value):
    top = value.astype(bf16)
    rest = (value - top.astype(f32)).astype(bf16)
    return jnp.concatenate([top, rest], axis=1)


def lower_mask(rows, cols):
    return lax.broadcasted_iota(jnp.int32, (rows, cols), 0) >= lax.broadcasted_iota(
        jnp.int32, (rows, cols), 1
    )


def sigmoid(v):
    return 1.0 / (1.0 + jnp.exp(-v))


def head_steps(step_raw, head_rows):
    biased = step_raw + head_rows[0:1]
    return jnp.maximum(biased, 0.0) + jnp.log1p(jnp.exp(-jnp.abs(biased)))


def running_sum(value):
    length = value.shape[0]
    ones = jnp.where(lower_mask(length, length), 1.0, 0.0).astype(f32)
    return dot(ones, value, NN, lax.Precision.HIGHEST)


def conv_pre(ext_ref, taps, length, width):
    summed = taps[CONV : CONV + 1]
    for j in range(CONV):
        summed = summed + ext_ref[5 + j : 5 + j + length, 0:width] * taps[j : j + 1]
    return summed


def fill_ext(ext_ref, tail, rows, length, width):
    ext_ref[0:8, 0:width] = tail[8:16].astype(f32)
    ext_ref[8 : 8 + length, 0:width] = rows


def fwd_body(
    h_ref, h_tile, ngain, wg, wc, wbc, wo, taps, taps_bc, head_rows, skip, gate_gain, spread, tail_in,
    tail_bc_in, state_in,
    normed_o, gate_o, cin_o, cin_bc_o, step_o, ssm_o, state_o, gout_o, r_o, branch_o, out_o,
    tail_o, tail_bc_o,
    u_s, ssq_s, k_s, c_s, bt_s, dt_s, ec_s, w_s, cum_s, cumt_s, ext_s,
):
    step = pl.program_id(0)
    length = h_ref.shape[0]
    half = length // 2

    @pl.when(step == 0)
    def _():
        h = h_ref[...].astype(f32)
        scale = lax.rsqrt(jnp.mean(h * h, axis=1, keepdims=True) + EPS)
        normed = (h * scale * ngain[...]).astype(bf16)
        normed_o[...] = normed
        projected = dot(normed, wbc[...], NN)
        step_raw = projected[:, BC:]
        step_o[...] = step_raw
        conv_in = projected[:, :BC].astype(bf16)
        cin_bc_o[...] = conv_in
        tail_bc_o[...] = conv_in[length - 16 :]
        fill_ext(ext_s, tail_bc_in[...], conv_in.astype(f32), length, BC)
        pre = conv_pre(ext_s, taps_bc[...], length, BC)
        act = (pre * sigmoid(pre)).astype(bf16)
        b_rows, c_rows = act[:, :STATE], act[:, STATE:]
        c_s[...] = c_rows
        bt_s[...] = b_rows.astype(f32).T.astype(bf16)
        k_s[...] = dot(c_rows, b_rows, NT)
        dt = head_steps(step_raw, head_rows[...])
        cum = running_sum(dt * head_rows[1:2])
        total = cum[length - 1 : length]
        dt_s[...] = halves(dt)
        ec_s[...] = halves(jnp.exp(cum))
        w_s[...] = halves(dt * jnp.exp(total - cum))
        for g in range(GROUPS):
            cum_s[g] = cum[:, g * GROUP : (g + 1) * GROUP]
        cumt_s[...] = cum.T
        ssq_s[...] = jnp.zeros_like(ssq_s)

    @pl.when(step < GROUPS)
    def _():
        normed = normed_o[...]
        gate = dot(normed, wg[...], NN)
        gate_o[...] = gate
        conv_in = dot(normed, wc[...], NN).astype(bf16)
        cin_o[...] = conv_in
        tail_o[...] = conv_in[length - 16 :]
        fill_ext(ext_s, tail_in[...], conv_in.astype(f32), length, WIDTH)
        pre = conv_pre(ext_s, taps[...], length, WIDTH)
        act = (pre * sigmoid(pre)).astype(bf16).astype(f32)
        where = spread[...]
        x_dt = (act * dot(dt_s[...], where, NN)).astype(bf16)
        x_w = (act * dot(w_s[...], where, NN)).astype(bf16)
        ec = dot(ec_s[...], where, NN)
        state = state_in[...]
        state_o[...] = ec[length - 1 : length] * state + dot(bt_s[...], x_w, NN)
        carried = dot(c_s[...], state.astype(bf16), NN) * ec
        cum = cum_s[step]
        cumt = cumt_s[pl.ds(pl.multiple_of(step * GROUP, GROUP), GROUP), :]
        k = k_s[...]
        mask = lower_mask(half, half)
        left_lane = lax.broadcasted_iota(jnp.int32, (length, LANES), 1) < HEAD_DIM
        pieces = []
        for pair in range(GROUP // 2):
            x_pair = x_dt[:, pair * LANES : (pair + 1) * LANES]
            results = []
            for i in (2 * pair, 2 * pair + 1):
                col, row = cum[:, i : i + 1], cumt[i : i + 1, :]
                top = jnp.exp(jnp.where(mask, col[:half] - row[:, :half], -1e30))
                low_left = jnp.exp(col[half:] - row[:, :half])
                low_right = jnp.exp(jnp.where(mask, col[half:] - row[:, half:], -1e30))
                top = (top * k[:half, :half]).astype(bf16)
                low = jnp.concatenate(
                    [
                        (low_left * k[half:, :half]).astype(bf16),
                        (low_right * k[half:, half:]).astype(bf16),
                    ],
                    axis=1,
                )
                results.append(
                    jnp.concatenate([dot(top, x_pair[:half], NN), dot(low, x_pair, NN)], axis=0)
                )
            pieces.append(jnp.where(left_lane, results[0], results[1]))
        within = jnp.concatenate(pieces, axis=1)
        ssm = within + carried + skip[...] * act
        ssm_o[...] = ssm
        u = ssm * (gate * sigmoid(gate))
        u_s[:, pl.ds(pl.multiple_of(step * WIDTH, WIDTH), WIDTH)] = u
        ssq_s[...] += jnp.sum(u * u, axis=1, keepdims=True)

    @pl.when(step == GROUPS)
    def _():
        r = lax.rsqrt(ssq_s[...] * (1.0 / DI) + EPS)
        r_o[...] = r
        for g in range(GROUPS):
            cols = slice(g * WIDTH, (g + 1) * WIDTH)
            gout_o[:, cols] = (u_s[:, cols] * r[:, 0:1] * gate_gain[:, cols]).astype(bf16)

    @pl.when(step >= GROUPS)
    def _():
        branch = dot(gout_o[...], wo[...], NN)
        branch_o[...] = branch
        out_o[...] = (h_tile[...].astype(f32) + branch).astype(bf16)


def bwd_body(
    h_ref, gout_ref, ngain, branch, r_ref, wo, wg, wc, wbc, taps, taps_bc, head_rows, skip,
    gate_gain, spread, gather, gate_ref, ssm_ref, cin, cin_bc, step_ref, tail_in, tail_bc_in,
    state_in, adj_in, next_in, next_bc_in,
    gg_o, gc_o, gbc_o, gin_o, gin_low_o, adj_o, next_o, next_bc_o, chan_o, chan_bc_o, ngrad_o,
    head_o,
    acc_s, kt_s, wt_s, b_s, c_s, ct_s, dt_s, ec_s, w_s, cum_s, cumt_s, db_s, dc_s, rows_s, cols_s,
    direct_s, fresh_s, carry_s, edge_s, dsilu_s, q_s, ext_s, ext2_s,
):
    step = pl.program_id(0)
    length = h_ref.shape[0]
    half = length // 2

    @pl.when(step == 0)
    def _():
        fill_ext(ext_s, tail_bc_in[...], cin_bc[...].astype(f32), length, BC)
        pre = conv_pre(ext_s, taps_bc[...], length, BC)
        sig = sigmoid(pre)
        dsilu_s[...] = sig * (1.0 + pre * (1.0 - sig))
        act = (pre * sig).astype(bf16)
        b_rows, c_rows = act[:, :STATE], act[:, STATE:]
        b_s[...] = b_rows
        c_s[...] = c_rows
        ct_s[...] = c_rows.astype(f32).T.astype(bf16)
        kt_s[...] = dot(b_rows, c_rows, NT)
        dt = head_steps(step_ref[...], head_rows[...])
        cum = running_sum(dt * head_rows[1:2])
        total = cum[length - 1 : length]
        dt_s[...] = halves(dt)
        ec_s[...] = halves(jnp.exp(cum))
        w_s[...] = halves(jnp.exp(total - cum))
        for g in range(GROUPS):
            cum_s[g] = cum[:, g * GROUP : (g + 1) * GROUP]
        cumt_s[...] = cum.T
        for ref in (acc_s, wt_s, db_s, dc_s, rows_s, cols_s, direct_s, fresh_s, carry_s, edge_s):
            ref[...] = jnp.zeros_like(ref)
        rowdot = jnp.sum(branch[...] * gout_ref[...].astype(f32), axis=1, keepdims=True)
        q_s[...] = jnp.broadcast_to(rowdot * (1.0 / DI), q_s.shape) * r_ref[...] * r_ref[...]

    @pl.when(step < GROUPS)
    def _():
        grad_gated = dot(gout_ref[...], wo[...], NT)
        gate, ssm = gate_ref[...], ssm_ref[...]
        sig = sigmoid(gate)
        silu = gate * sig
        u = ssm * silu
        scaled = r_ref[:, 0:1] * grad_gated
        gain_grad = jnp.sum(scaled * u, axis=0, keepdims=True)
        grad_u = scaled * gate_gain[...] - u * q_s[:, 0:1]
        grad_ssm = grad_u * silu
        grad_gate = (grad_u * ssm * (sig * (1.0 + gate * (1.0 - sig)))).astype(bf16)
        gg_o[...] = grad_gate
        conv_in = cin[...].astype(f32)
        fill_ext(ext_s, tail_in[...], conv_in, length, WIDTH)
        pre = conv_pre(ext_s, taps[...], length, WIDTH)
        sig = sigmoid(pre)
        act = (pre * sig).astype(bf16).astype(f32)
        dsilu = sig * (1.0 + pre * (1.0 - sig))
        where, pick = spread[...], gather[...]
        dt, ec, w = (dot(ref[...], where, NN) for ref in (dt_s, ec_s, w_s))
        skip_grad = jnp.sum(act * grad_ssm, axis=0, keepdims=True)
        x_dt = act * dt
        x_low, g_low = x_dt.astype(bf16), grad_ssm.astype(bf16)
        g_ec = (grad_ssm * ec).astype(bf16)
        state, adj = state_in[...], adj_in[...]
        state_low, adj_low = state.astype(bf16), adj.astype(bf16)
        from_adj = w * dot(b_s[...], adj_low, NN)
        carried = ec * dot(c_s[...], state_low, NN)
        db_s[...] += dot((x_dt * w).astype(bf16), adj_low, NT)
        dc_s[...] += dot(g_ec, state_low, NT)
        last = ec[length - 1 : length]
        adj_o[...] = last * adj + dot(ct_s[...], g_ec, NN)
        edge = last * jnp.sum(state * adj, axis=0, keepdims=True)
        edge_s[...] += dot(halves(edge), pick, NN)
        cum = cum_s[step]
        start = pl.multiple_of(step * GROUP, GROUP)
        cumt = cumt_s[pl.ds(start, GROUP), :]
        kt = kt_s[...]
        mask = lax.broadcasted_iota(jnp.int32, (half, half), 0) <= lax.broadcasted_iota(
            jnp.int32, (half, half), 1
        )
        left_lane = lax.broadcasted_iota(jnp.int32, (length, LANES), 1) < HEAD_DIM
        lane_id = lax.broadcasted_iota(jnp.int32, (1, LANES), 1)
        pieces, col_sums = [], []
        row_sums = rows_s[...]
        w_tl, w_tr, w_br = wt_s[:half, :half], wt_s[:half, half:], wt_s[half:, half:]
        for pair in range(GROUP // 2):
            lanes = slice(pair * LANES, (pair + 1) * LANES)
            x_pair, g_pair = x_low[:, lanes], g_low[:, lanes]
            results = []
            for i in (2 * pair, 2 * pair + 1):
                col, row = cum[:, i : i + 1], cumt[i : i + 1, :]
                mine = left_lane if i % 2 == 0 else jnp.logical_not(left_lane)
                x_head = jnp.where(mine, x_pair, jnp.zeros_like(x_pair))
                l_tl = jnp.exp(jnp.where(mask, row[:, :half] - col[:half], -1e30))
                l_tr = jnp.exp(row[:, half:] - col[:half])
                l_br = jnp.exp(jnp.where(mask, row[:, half:] - col[half:], -1e30))
                lk_tl, lk_tr, lk_br = (
                    l_tl * kt[:half, :half],
                    l_tr * kt[:half, half:],
                    l_br * kt[half:, half:],
                )
                mixed = jnp.concatenate([lk_tl.astype(bf16), lk_tr.astype(bf16)], axis=1)
                results.append(
                    jnp.concatenate(
                        [dot(mixed, g_pair, NN), dot(lk_br.astype(bf16), g_pair[half:], NN)], axis=0
                    )
                )
                p_top = dot(x_head[:half], g_pair, NT)
                p_br = dot(x_head[half:], g_pair[half:], NT)
                p_tl, p_tr = p_top[:, :half], p_top[:, half:]
                w_tl, w_tr, w_br = w_tl + l_tl * p_tl, w_tr + l_tr * p_tr, w_br + l_br * p_br
                z_tl, z_tr, z_br = lk_tl * p_tl, lk_tr * p_tr, lk_br * p_br
                sums = jnp.concatenate(
                    [
                        jnp.sum(z_tl + z_tr, axis=1, keepdims=True),
                        jnp.sum(z_br, axis=1, keepdims=True),
                    ],
                    axis=0,
                )
                row_sums = row_sums + jnp.where(lane_id == start + i, sums, 0.0)
                col_sums.append(
                    jnp.concatenate(
                        [
                            jnp.sum(z_tl, axis=0, keepdims=True),
                            jnp.sum(z_tr, axis=0, keepdims=True)
                            + jnp.sum(z_br, axis=0, keepdims=True),
                        ],
                        axis=1,
                    )
                )
            pieces.append(jnp.where(left_lane, results[0], results[1]))
        wt_s[:half, :half] = w_tl
        wt_s[:half, half:] = w_tr
        wt_s[half:, half:] = w_br
        rows_s[...] = row_sums
        cols_s[pl.ds(start, GROUP), :] = jnp.concatenate(col_sums, axis=0)
        mixed_grad = jnp.concatenate(pieces, axis=1) + from_adj
        direct_s[...] += dot(halves(act * mixed_grad), pick, NN)
        fresh_s[...] += dot(halves(x_dt * from_adj), pick, NN)
        carry_s[...] += dot(halves(grad_ssm * carried), pick, NN)
        grad_pre = (dt * mixed_grad + skip[...] * grad_ssm) * dsilu
        next_o[...] = grad_pre[0:8]
        ext2_s[0:length] = grad_pre
        ext2_s[length : length + 8] = next_in[...]
        tap_rows = taps[...]
        grad_conv = grad_pre * tap_rows[CONV - 1 : CONV]
        for j in range(CONV - 1):
            shift = CONV - 1 - j
            grad_conv = grad_conv + ext2_s[shift : shift + length] * tap_rows[j : j + 1]
        grad_conv = grad_conv.astype(bf16)
        gc_o[...] = grad_conv
        sums = [
            jnp.sum(grad_pre * ext_s[5 + j : 5 + j + length], axis=0, keepdims=True)
            for j in range(CONV)
        ]
        sums += [jnp.sum(grad_pre, axis=0, keepdims=True), gain_grad, skip_grad]
        chan_o[...] = jnp.concatenate(sums + [jnp.zeros_like(skip_grad)], axis=0)
        acc_s[...] += dot(grad_gate, wg[...], NT) + dot(grad_conv, wc[...], NT)

    @pl.when(step == GROUPS)
    def _():
        wt = wt_s[...].astype(bf16)
        grad_b = db_s[...] + dot(wt, c_s[...], NN)
        grad_c = dc_s[...] + dot(wt, b_s[...], TN)
        grad_pre = jnp.concatenate([grad_b, grad_c], axis=1) * dsilu_s[...]
        next_bc_o[...] = grad_pre[0:8]
        ext2_s[0:length, 0:BC] = grad_pre
        ext2_s[length : length + 8, 0:BC] = next_bc_in[...]
        fill_ext(ext_s, tail_bc_in[...], cin_bc[...].astype(f32), length, BC)
        tap_rows = taps_bc[...]
        grad_conv = grad_pre * tap_rows[CONV - 1 : CONV]
        for j in range(CONV - 1):
            shift = CONV - 1 - j
            grad_conv = grad_conv + ext2_s[shift : shift + length, 0:BC] * tap_rows[j : j + 1]
        sums = [
            jnp.sum(grad_pre * ext_s[5 + j : 5 + j + length, 0:BC], axis=0, keepdims=True)
            for j in range(CONV)
        ]
        sums += [jnp.sum(grad_pre, axis=0, keepdims=True)]
        chan_bc_o[...] = jnp.concatenate(sums + [jnp.zeros((3, BC), f32)], axis=0)
        dt = head_steps(step_ref[...], head_rows[...])
        rate = head_rows[1:2]
        ones = jnp.where(lower_mask(length, length), 1.0, 0.0).astype(f32)
        fresh = fresh_s[...]
        from_here = cols_s[...].T - rows_s[...] + carry_s[...]
        suffix = (
            dot(ones, from_here, TN, lax.Precision.HIGHEST)
            + dot(ones, fresh, NN, lax.Precision.HIGHEST)
            - fresh
            + edge_s[0:1]
        )
        decayed = rate * suffix
        grad_step = (direct_s[...] + decayed) * sigmoid(step_ref[...] + head_rows[0:1])
        head_o[...] = jnp.concatenate(
            [
                jnp.sum(grad_step, axis=0, keepdims=True),
                jnp.sum(dt * decayed, axis=0, keepdims=True),
                jnp.zeros((6, LANES), f32),
            ],
            axis=0,
        )
        low = jnp.concatenate([grad_conv.astype(bf16), grad_step.astype(bf16)], axis=1)
        gbc_o[...] = low
        grad_normed = acc_s[...] + dot(low, wbc[...], NT)
        h = h_ref[...].astype(f32)
        scale = lax.rsqrt(jnp.mean(h * h, axis=1, keepdims=True) + EPS)
        ngrad_o[...] = jnp.sum(grad_normed * h * scale, axis=0, keepdims=True)
        weighted = grad_normed * ngain[...]
        mean = jnp.mean(h * weighted, axis=1, keepdims=True)
        grad_in = gout_ref[...].astype(f32) + scale * weighted - h * (scale * scale * scale * mean)
        gin_o[...] = grad_in
        gin_low_o[...] = grad_in.astype(bf16)


def spread_table():
    table = np.zeros((2 * LANES, DI), np.float32)
    for head in range(HEADS):
        table[head, head * HEAD_DIM : (head + 1) * HEAD_DIM] = 1.0
        table[LANES + head, head * HEAD_DIM : (head + 1) * HEAD_DIM] = 1.0
    return table


def whole(shape):
    return pl.BlockSpec(shape, lambda i: (0,) * len(shape))


def by_group(rows, width=WIDTH):
    return pl.BlockSpec((rows, width), lambda i: (0, jnp.minimum(i, GROUPS - 1)))


def tail_of(rows, width):
    return pl.BlockSpec((rows, width), lambda i: (0, DI // width))


def gather_table():
    table = np.zeros((GROUPS, 2, WIDTH, LANES), np.float32)
    for group in range(GROUPS):
        for column in range(WIDTH):
            table[group, :, column, group * GROUP + column // HEAD_DIM] = 1.0
    return table.reshape(-1, LANES)


def fwd_call(h, params, weights, state, tail, tail_bc):
    length = h.shape[0]
    wg, wc, wo = weights
    out_tiles = D // OUT_TILE
    by_out = pl.BlockSpec((length, OUT_TILE), lambda i: (0, jnp.maximum(i - GROUPS, 0)))
    in_specs = [
        whole((length, D)), by_out, whole((1, D)), by_group(D), by_group(D), tail_of(D, TAIL),
        pl.BlockSpec((DI, OUT_TILE), lambda i: (0, jnp.maximum(i - GROUPS, 0))),
        by_group(8), tail_of(8, BC), whole((8, LANES)), by_group(1), whole((1, DI)),
        by_group(2 * LANES), by_group(16), whole((16, BC)), by_group(STATE),
    ]
    out = [
        ((length, D), bf16, whole((length, D))),
        ((length, DI), f32, by_group(length)),
        ((length, DI), bf16, by_group(length)),
        ((length, BC), bf16, whole((length, BC))),
        ((length, LANES), f32, whole((length, LANES))),
        ((length, DI), f32, by_group(length)),
        ((STATE, DI), f32, by_group(STATE)),
        ((length, DI), bf16, whole((length, DI))),
        ((length, LANES), f32, whole((length, LANES))),
        ((length, D), f32, by_out),
        ((length, D), bf16, by_out),
        ((16, DI), bf16, by_group(16)),
        ((16, BC), bf16, whole((16, BC))),
    ]
    scratch = [
        ((length, DI), f32), ((length, LANES), f32), ((length, length), f32),
        ((length, STATE), bf16), ((STATE, length), bf16), ((length, 2 * LANES), bf16),
        ((length, 2 * LANES), bf16), ((length, 2 * LANES), bf16), ((GROUPS, length, GROUP), f32),
        ((LANES, length), f32), ((length + 8, WIDTH), f32),
    ]
    return pl.pallas_call(
        fwd_body,
        grid=(GROUPS + out_tiles,),
        in_specs=in_specs,
        out_specs=[spec for _, _, spec in out],
        out_shape=[jax.ShapeDtypeStruct(shape, dtype) for shape, dtype, _ in out],
        scratch_shapes=[pltpu.VMEM(shape, dtype) for shape, dtype in scratch],
        compiler_params=pltpu.CompilerParams(
            dimension_semantics=("arbitrary",), vmem_limit_bytes=VMEM_LIMIT
        ),
        cost_estimate=pl.CostEstimate(flops=12 * 10**9, bytes_accessed=45 * 10**6, transcendentals=5 * 10**6),
        name="layer_forward",
    )(
        h, h, params["norm_gain"], wg, wc, wc, wo, params["taps"], params["taps"],
        params["heads"], params["skip"], params["gate_gain"], params["spread"], tail, tail_bc, state,
    )


def bwd_call(h, grad_out, kept, params, weights, adj, ahead, ahead_bc):
    length = h.shape[0]
    wg, wc, wo = weights
    rows_of_wo = pl.BlockSpec((WIDTH, D), lambda i: (jnp.minimum(i, GROUPS - 1), 0))
    pick = pl.BlockSpec((2 * WIDTH, LANES), lambda i: (jnp.minimum(i, GROUPS - 1), 0))
    in_specs = [
        whole((length, D)), whole((length, D)), whole((1, D)), whole((length, D)),
        whole((length, LANES)), rows_of_wo, by_group(D), by_group(D), tail_of(D, TAIL),
        by_group(8), tail_of(8, BC), whole((8, LANES)), by_group(1), by_group(1),
        by_group(2 * LANES), pick, by_group(length), by_group(length), by_group(length),
        whole((length, BC)), whole((length, LANES)), by_group(16), whole((16, BC)),
        by_group(STATE), by_group(STATE), by_group(8), whole((8, BC)),
    ]
    out = [
        ((length, DI), bf16, by_group(length)),
        ((length, DI), bf16, by_group(length)),
        ((length, TAIL), bf16, whole((length, TAIL))),
        ((length, D), f32, whole((length, D))),
        ((length, D), bf16, whole((length, D))),
        ((STATE, DI), f32, by_group(STATE)),
        ((8, DI), f32, by_group(8)),
        ((8, BC), f32, whole((8, BC))),
        ((8, DI), f32, by_group(8)),
        ((8, BC), f32, whole((8, BC))),
        ((1, D), f32, whole((1, D))),
        ((8, LANES), f32, whole((8, LANES))),
    ]
    scratch = [
        ((length, D), f32), ((length, length), f32), ((length, length), f32),
        ((length, STATE), bf16), ((length, STATE), bf16), ((STATE, length), bf16),
        ((length, 2 * LANES), bf16), ((length, 2 * LANES), bf16), ((length, 2 * LANES), bf16),
        ((GROUPS, length, GROUP), f32), ((LANES, length), f32), ((length, STATE), f32),
        ((length, STATE), f32), ((length, LANES), f32), ((LANES, length), f32),
        ((length, LANES), f32), ((length, LANES), f32), ((length, LANES), f32), ((1, LANES), f32),
        ((length, BC), f32), ((length, LANES), f32), ((length + 8, WIDTH), f32),
        ((length + 8, WIDTH), f32),
    ]
    return pl.pallas_call(
        bwd_body,
        grid=(GROUPS + 1,),
        in_specs=in_specs,
        out_specs=[spec for _, _, spec in out],
        out_shape=[jax.ShapeDtypeStruct(shape, dtype) for shape, dtype, _ in out],
        scratch_shapes=[pltpu.VMEM(shape, dtype) for shape, dtype in scratch],
        compiler_params=pltpu.CompilerParams(
            dimension_semantics=("arbitrary",), vmem_limit_bytes=VMEM_LIMIT
        ),
        cost_estimate=pl.CostEstimate(flops=25 * 10**9, bytes_accessed=55 * 10**6, transcendentals=8 * 10**6),
        name="layer_backward",
    )(
        h, grad_out, params["norm_gain"], kept["branch"], kept["r"], wo, wg, wc, wc,
        params["taps"], params["taps"], params["heads"], params["skip"], params["gate_gain"],
        params["spread"], params["gather"], kept["gate"], kept["ssm"], kept["cin"], kept["cin_bc"],
        kept["step"], kept["tail"], kept["tail_bc"], kept["state"], adj, ahead, ahead_bc,
    )


def xor_route(size, bit):
    return [(i, i ^ bit) for i in range(size)]


def bits_of(size):
    return [1 << b for b in range(size.bit_length() - 1)]


def gather_small(row):
    for axis in ("seq", "dp"):
        size, position = lax.axis_size(axis), lax.axis_index(axis)
        for bit in bits_of(size):
            other = lax.ppermute(row, axis, xor_route(size, bit))
            row = jnp.where(
                (position & bit) == 0,
                jnp.concatenate([row, other], axis=0),
                jnp.concatenate([other, row], axis=0),
            )
    return row


def sum_small(value):
    for axis in ("dp", "seq"):
        size = lax.axis_size(axis)
        for bit in bits_of(size):
            value = value + lax.ppermute(value, axis, xor_route(size, bit))
    return value


def direct_paths():
    return lax.axis_size("dp") == 4 and lax.axis_size("seq") == 4


def pair_route(allowed):
    return [(d * 4 + z, (d ^ 2) * 4 + z) for d in range(4) for z in range(4) if allowed(z)]


def gather_rows(shard):
    if not direct_paths():
        return lax.all_gather(shard, ("dp", "seq"), axis=0, tiled=True)
    rows, cols = shard.shape
    dp, z = lax.axis_index("dp"), lax.axis_index("seq")
    y, core = dp // 2, dp % 2
    held = jnp.zeros((2, 4, rows, cols), shard.dtype)

    def place(held, piece, at_y, at_z):
        return lax.dynamic_update_slice(held, piece[None, None], (at_y, at_z, 0, 0))

    up, down = shard, shard
    beside = lax.ppermute(shard, "dp", xor_route(4, 2))
    arrivals = []
    for hop in range(1, 4):
        up = lax.ppermute(up, "seq", [(i, i + 1) for i in range(hop - 1, 3)])
        down = lax.ppermute(down, "seq", [(i, i - 1) for i in range(1, 5 - hop)])
        up_beside = lax.ppermute(up, ("dp", "seq"), pair_route(lambda i: i >= hop))
        down_beside = lax.ppermute(down, ("dp", "seq"), pair_route(lambda i: i <= 3 - hop))
        arrivals.append((up, up_beside, jnp.where(z >= hop, z - hop, z)))
        arrivals.append((down, down_beside, jnp.where(z + hop <= 3, z + hop, z)))
    for piece, piece_beside, at in arrivals:
        held = place(held, piece, y, at)
        held = place(held, piece_beside, 1 - y, at)
    held = place(place(held, beside, 1 - y, z), shard, y, z)
    other = lax.ppermute(held, "dp", xor_route(4, 1))
    full = jnp.where(
        core == 0, jnp.stack([held, other], axis=1), jnp.stack([other, held], axis=1)
    )
    return full.reshape(16 * rows, cols)


def reduce_rows(mine, rest):
    dp, z = lax.axis_index("dp"), lax.axis_index("seq")
    y = dp // 2
    from_core = lax.ppermute(rest(), "dp", xor_route(4, 1))
    chip = mine(from_core)
    order = jnp.array([[3, 2, 1, 0], [3, 2, 0, 1], [0, 1, 3, 2], [0, 1, 2, 3]], jnp.int32)[z]
    sums = []
    for j in range(4):
        at = order[j]

        def pick(at_y):
            return lax.dynamic_slice(chip, (at_y, at, 0, 0), (1, 1) + chip.shape[2:])[0, 0]

        arrived = lax.ppermute(pick(1 - y), "dp", xor_route(4, 2))
        sums.append(pick(y).astype(f32) + arrived.astype(f32))

    def up(value, hop):
        return lax.ppermute(value.astype(bf16), "seq", [(i, i + 1) for i in range(hop)]).astype(f32)

    def down(value, hop):
        return lax.ppermute(
            value.astype(bf16), "seq", [(i, i - 1) for i in range(4 - hop, 4)]
        ).astype(f32)

    up_1, down_1 = up(sums[0], 1), down(sums[0], 1)
    up_2 = up(jnp.where(z == 0, sums[1], sums[0]) + up_1, 2)
    down_2 = down(jnp.where(z == 3, sums[1], sums[0]) + down_1, 2)
    up_3 = up(jnp.where(z == 1, sums[1], sums[2]) + up_2, 3)
    down_3 = down(jnp.where(z == 2, sums[1], sums[2]) + down_2, 3)
    return sums[3] + up_3 + down_3


def weight_grad(left, right):
    def term(columns):
        return jnp.einsum("td,te->de", columns, right, preferred_element_type=f32)

    dp, seq = lax.axis_size("dp"), lax.axis_size("seq")
    if not direct_paths():
        return lax.optimization_barrier(
            lax.psum_scatter(term(left), ("dp", "seq"), scatter_dimension=0, tiled=True)
        )
    rows = left.shape[1] // (dp * seq)
    core = lax.axis_index("dp") % 2
    by_core = left.reshape(left.shape[0], 2, 2, 4 * rows)
    shape = (2, 4, rows, right.shape[1])

    def owned(which):
        chosen = jnp.where(which == 0, by_core[:, :, 0], by_core[:, :, 1])
        return term(chosen.reshape(left.shape[0], 8 * rows))

    return reduce_rows(
        lambda arrived: (owned(core).reshape(shape) + arrived.astype(f32)).astype(bf16),
        lambda: owned(1 - core).astype(bf16).reshape(shape),
    )


def turn(value, shift, parts):
    size = lax.axis_size("seq")
    route = [(i, i - i % parts + (i % parts + shift) % parts) for i in range(size)]
    return lax.ppermute(value, "seq", route)


def to_sequences(rows):
    parts = rows.shape[0]
    rank = lax.axis_index("seq") % parts
    arrived = []
    for shift in range(parts):
        piece = lax.dynamic_index_in_dim(rows, (rank + shift) % parts, 0, keepdims=False)
        arrived.append(piece if shift == 0 else turn(piece, shift, parts))
    arrived = jnp.stack(arrived)
    return [
        lax.dynamic_index_in_dim(arrived, (rank - k) % parts, 0, keepdims=False)
        for k in range(parts)
    ]


def to_pieces(blocks, sent_type):
    parts = len(blocks)
    rank = lax.axis_index("seq") % parts
    stacked = jnp.stack(blocks)
    held = stacked
    for shift in range(parts):
        piece = lax.dynamic_index_in_dim(stacked, (rank + shift) % parts, 0, keepdims=False)
        if shift:
            piece = turn(piece.astype(sent_type), shift, parts).astype(piece.dtype)
        held = lax.dynamic_update_slice(held, piece[None], ((rank - shift) % parts, 0, 0))
    return held


KEPT = (
    "normed", "gate", "cin", "cin_bc", "step", "ssm", "state_out", "gout", "r", "branch", "out",
    "tail_out", "tail_bc_out",
)
SKEW = 2


def shards(
    tokens, cotangent, in_proj, out_proj, conv_weight, conv_bias, norm_gain, gate_gain, step_bias,
    log_decay, skip_gain,
):
    first = lax.axis_index("section") == 0
    seq = lax.axis_size("seq")
    parts, length = tokens.shape[0], tokens.shape[1]
    owned = in_proj.shape[1]
    blocks_in = to_sequences(jnp.where(first, tokens, cotangent))

    shard = in_proj[0]
    shard_conv = jnp.pad(shard[:, DI:], ((0, 0), (0, TAIL - BC - HEADS)))
    w_conv = gather_rows(shard_conv)
    w_gate = gather_rows(shard[:, :DI])
    w_out = gather_rows(out_proj[0])
    weights = (w_gate, w_conv, w_out)

    sizes = [CONV * conv_bias.shape[1], conv_bias.shape[1], norm_gain.shape[1], gate_gain.shape[1]]
    packed = jnp.concatenate([conv_weight[0].reshape(-1), conv_bias[0], norm_gain[0], gate_gain[0]])
    packed = gather_small(packed[None]).astype(f32)
    ends = np.cumsum(sizes)
    taps, shift, gain_in, gain_gate = (
        packed[:, end - size : end] for end, size in zip(ends, sizes)
    )
    taps = jnp.swapaxes(taps.reshape(-1, CONV, conv_bias.shape[1]), 0, 1).reshape(CONV, -1)
    taps = jnp.concatenate([taps, shift.reshape(1, -1), jnp.zeros((3, taps.shape[1]), f32)], axis=0)
    lanes = ((0, 0), (0, LANES - HEADS))
    params = {
        "norm_gain": gain_in.reshape(1, -1),
        "gate_gain": gain_gate.reshape(1, -1),
        "taps": taps,
        "heads": jnp.pad(
            jnp.concatenate([step_bias, -jnp.exp(log_decay), jnp.zeros((6, HEADS), f32)], axis=0),
            lanes,
        ),
        "skip": jnp.repeat(skip_gain, HEAD_DIM, axis=1),
        "spread": jnp.asarray(spread_table(), bf16),
        "gather": jnp.asarray(gather_table(), bf16),
    }

    ticks = parts + SKEW
    hops = seq // parts

    def forward(start):
        kept, received = [], [jnp.zeros((length, D), bf16)] * SKEW
        carry = start
        for tick in range(ticks):
            if tick == SKEW:
                carry = tuple(jnp.where(first, now, at) for now, at in zip(carry, start))
            h = jnp.where(first, blocks_in[min(tick, parts - 1)], received[tick])
            values = dict(zip(KEPT, fwd_call(h, params, weights, *carry)))
            values.update(h=h, state=carry[0], tail=carry[1], tail_bc=carry[2])
            carry = (values["state_out"], values["tail_out"], values["tail_bc_out"])
            kept.append(values)
            if tick < parts:
                received.append(lax.ppermute(values["out"], "section", [(0, 1)]))
        return kept

    def backward(kept, start):
        zeros = tuple(jnp.zeros_like(part) for part in start)
        carry = tuple(jnp.where(first, zero, at) for zero, at in zip(zeros, start))
        grads, received = [None] * ticks, [jnp.zeros((length, D), bf16)] * SKEW
        for tick in range(ticks):
            if tick == SKEW and hops > 1:
                carry = tuple(jnp.where(first, at, now) for now, at in zip(carry, start))
            if tick == parts:
                carry = tuple(jnp.where(first, now, zero) for now, zero in zip(carry, zeros))
            from_loss = blocks_in[parts - 1 - tick] if tick < parts else zeros_low
            grad_out = jnp.where(first, received[tick], from_loss)
            at = ticks - 1 - tick
            names = (
                "gate", "conv", "tail", "in", "in_low", "adj", "next", "next_bc", "chan", "chan_bc",
                "norm", "head",
            )
            values = dict(
                zip(names, bwd_call(kept[at]["h"], grad_out, kept[at], params, weights, *carry))
            )
            values["out"] = grad_out
            carry = (values["adj"], values["next"], values["next_bc"])
            grads[at] = values
            if tick < parts:
                received.append(lax.ppermute(values["in_low"], "section", [(1, 0)]))
        return grads

    zeros_low = jnp.zeros((length, D), bf16)
    start = (jnp.zeros((STATE, DI), f32), jnp.zeros((16, DI), bf16), jnp.zeros((16, BC), bf16))
    if hops > 1:

        def onward(_, start):
            kept = forward(start)
            ends = (
                tuple(kept[parts - 1][name] for name in ("state_out", "tail_out", "tail_bc_out")),
                tuple(kept[ticks - 1][name] for name in ("state_out", "tail_out", "tail_bc_out")),
            )
            route = [(i, i + parts) for i in range(seq - parts)]
            return tuple(
                lax.ppermute(jnp.where(first, a, b), "seq", route) for a, b in zip(*ends)
            )

        start = lax.fori_loop(0, hops - 1, onward, start)
    kept = forward(start)
    activations = to_pieces(
        [jnp.where(first, kept[k]["out"], kept[k + SKEW]["out"]) for k in range(parts)], bf16
    )[None]

    start = (jnp.zeros((STATE, DI), f32), jnp.zeros((8, DI), f32), jnp.zeros((8, BC), f32))
    if hops > 1:

        def back(_, start):
            grads = backward(kept, start)
            ends = (
                tuple(grads[0][name] for name in ("adj", "next", "next_bc")),
                tuple(grads[SKEW][name] for name in ("adj", "next", "next_bc")),
            )
            route = [(i, i - parts) for i in range(parts, seq)]
            return tuple(
                lax.ppermute(jnp.where(first, a, b), "seq", route) for a, b in zip(*ends)
            )

        start = lax.fori_loop(0, hops - 1, back, start)
    grads = backward(kept, start)

    def select(values, name):
        return jnp.concatenate(
            [jnp.where(first, values[k][name], values[k + SKEW][name]) for k in range(parts)], axis=0
        )

    normed, gate_out = select(kept, "normed"), select(kept, "gout")
    grad_out_proj = weight_grad(gate_out, select(grads, "out"))[None]
    grad_gate = weight_grad(normed, select(grads, "gate"))
    grad_conv = weight_grad(
        normed, jnp.concatenate([select(grads, "conv"), select(grads, "tail")], axis=1)
    )
    grad_in_proj = jnp.concatenate([grad_gate, grad_conv[:, : DI + BC + HEADS]], axis=1)[None]
    input_grads = to_pieces(
        [jnp.where(first, grads[k]["in"], grads[k + SKEW]["in"]) for k in range(parts)], bf16
    )[None]

    def total(name):
        return sum(values[name] for values in grads)

    channels = jnp.concatenate([total("chan"), total("chan_bc")], axis=1)
    norm = total("norm")
    head = total("head")
    skip = channels[6, :DI].reshape(HEADS, HEAD_DIM).sum(axis=1)
    small = jnp.concatenate(
        [
            channels[: CONV + 1].reshape(-1), channels[5, :DI], norm[0], head[0], head[1],
            jnp.pad(skip, (0, LANES - HEADS)),
        ]
    )
    small = sum_small(small.reshape(-1, LANES)).reshape(-1)
    place = lax.axis_index("dp") * seq + lax.axis_index("seq")

    def mine(flat, width):
        return lax.dynamic_slice_in_dim(flat, place * width, width, axis=flat.ndim - 1)

    width = conv_bias.shape[1]
    full = CONV * (DI + BC)
    grad_taps = small[:full].reshape(CONV, -1)
    grad_shift = small[full : full + DI + BC]
    rest = small[full + DI + BC :]
    return (
        activations,
        input_grads,
        grad_in_proj,
        grad_out_proj,
        mine(grad_taps, width)[None],
        mine(grad_shift, width)[None],
        mine(rest[DI : DI + D], owned)[None],
        mine(rest[:DI], gate_gain.shape[1])[None],
        rest[DI + D : DI + D + HEADS][None],
        rest[DI + D + LANES : DI + D + LANES + HEADS][None],
        rest[DI + D + 2 * LANES : DI + D + 2 * LANES + HEADS][None],
    )


def solution(mesh):
    placed = (
        P("dp", "seq", None),
        P("dp", "seq", None),
        P("section", ("dp", "seq"), None),
        P("section", ("dp", "seq"), None),
        P("section", None, ("dp", "seq")),
        P("section", ("dp", "seq")),
        P("section", ("dp", "seq")),
        P("section", ("dp", "seq")),
        P("section", None),
        P("section", None),
        P("section", None),
    )
    return jax.shard_map(
        shards,
        mesh=mesh,
        in_specs=placed,
        out_specs=(
            P("section", "dp", "seq", None),
            P("section", "dp", "seq", None),
        )
        + placed[2:],
        check_vma=False,
    )
```

```python
import jax
import jax.numpy as jnp
import numpy as np
from jax import lax
from jax.experimental import pallas as pl
from jax.experimental.pallas import tpu as pltpu
from jax.sharding import PartitionSpec as P

D = 1536
HEADS = 48
HEAD_DIM = 64
STATE = 128
CONV = 4
DI = 3072
BC = 2 * STATE
TAIL = BC + 128
GROUP = 8
WIDTH = GROUP * HEAD_DIM
GROUPS = HEADS // GROUP
LANES = 128
EPS = 1e-05
LOG2_E = 1.4426950408889634
f32 = jnp.float32
bf16 = jnp.bfloat16
VMEM_LIMIT = 56 * 2**20
NN = ((1,), (0,))
NT = ((1,), (1,))
TN = ((0,), (0,))


def dot(a, b, dims, precision=None):
    return lax.dot_general(a, b, (dims, ((), ())), preferred_element_type=f32, precision=precision)


def halves(value):
    top = value.astype(bf16)
    rest = (value - top.astype(f32)).astype(bf16)
    return jnp.concatenate([top, rest], axis=1)


def lower_mask(rows, cols):
    return lax.broadcasted_iota(jnp.int32, (rows, cols), 0) >= lax.broadcasted_iota(
        jnp.int32, (rows, cols), 1
    )


def sigmoid(v):
    return 0.5 * jnp.tanh(0.5 * v) + 0.5


def head_steps(step_raw, head_rows):
    biased = step_raw + head_rows[0:1]
    return jnp.maximum(biased, 0.0) + jnp.log1p(jnp.exp(-jnp.abs(biased)))


def running_sum(value):
    length = value.shape[0]
    ones = jnp.where(lower_mask(length, length), 1.0, 0.0).astype(f32)
    return dot(ones, value, NN, lax.Precision.HIGHEST)


def earlier_rows(tail, rows):
    joined = jnp.concatenate([tail[8:16].astype(f32), rows], axis=0)
    shifted = [pltpu.roll(joined, shift, 0)[8:] for shift in range(CONV - 1, 0, -1)]
    return shifted + [rows]


def later_rows(rows, head):
    length = rows.shape[0]
    joined = jnp.concatenate([rows, head], axis=0)
    shifted = [pltpu.roll(joined, length + 8 - shift, 0)[:length] for shift in range(CONV - 1, 0, -1)]
    return shifted + [rows]


def conv_sum(taps, shifted, start=0.0):
    for j in range(CONV):
        start = start + shifted[j] * taps[j : j + 1]
    return start


def chosen(flag, own, other):
    return jnp.where(flag == 1, own[...].astype(f32), other[...].astype(f32))


def chosen_grad(flag, own, other):
    other_or_zero = jnp.where(flag == 0, other[...].astype(f32), 0.0)
    return jnp.where(flag == 1, own[...].astype(f32), other_or_zero)


def fwd_body(
    flag, own_ref, other_ref, ngain, wg, wc, wbc, wo, taps, taps_bc, head_rows, skip, gate_gain, spread, tail_in,
    tail_bc_in, state_in,
    normed_o, gate_o, cin_o, cin_bc_o, step_o, ssm_o, state_o, gout_o, r_o, branch_o, out_o,
    tail_o, tail_bc_o,
    u_s, ssq_s, k_s, c_s, bt_s, dt_s, ec_s, w_s, cum_s, cumt_s,
):
    step = pl.program_id(0)
    length = own_ref.shape[0]
    half = length // 2

    @pl.when(step == 0)
    def _():
        h = chosen(flag[0, 0], own_ref, other_ref)
        scale = lax.rsqrt(jnp.mean(h * h, axis=1, keepdims=True) + EPS)
        normed = (h * scale * ngain[...]).astype(bf16)
        normed_o[...] = normed
        projected = dot(normed, wbc[...], NN)
        step_raw = projected[:, BC:]
        step_o[...] = step_raw
        conv_in = projected[:, :BC].astype(bf16)
        cin_bc_o[...] = conv_in
        tail_bc_o[...] = conv_in[length - 16 :]
        tap_rows = taps_bc[...]
        shifted = earlier_rows(tail_bc_in[...], conv_in.astype(f32))
        pre = conv_sum(tap_rows, shifted, tap_rows[CONV : CONV + 1])
        act = (pre * sigmoid(pre)).astype(bf16)
        b_rows, c_rows = act[:, :STATE], act[:, STATE:]
        c_s[...] = c_rows
        bt_s[...] = b_rows.astype(f32).T.astype(bf16)
        k_s[...] = dot(c_rows, b_rows, NT)
        dt = head_steps(step_raw, head_rows[...])
        cum = running_sum(dt * head_rows[1:2])
        total = cum[length - 1 : length]
        dt_s[...] = halves(dt)
        ec_s[...] = halves(jnp.exp(cum))
        w_s[...] = halves(dt * jnp.exp(total - cum))
        for g in range(GROUPS):
            cum_s[g] = cum[:, g * GROUP : (g + 1) * GROUP] * LOG2_E
        cumt_s[...] = (cum * LOG2_E).T
        ssq_s[...] = jnp.zeros_like(ssq_s)
        branch_o[...] = jnp.zeros_like(branch_o)

    @pl.when(step < GROUPS)
    def _():
        normed = normed_o[...]
        gate = dot(normed, wg[...], NN)
        gate_o[...] = gate
        conv_in = dot(normed, wc[...], NN).astype(bf16)
        cin_o[...] = conv_in
        tail_o[...] = conv_in[length - 16 :]
        tap_rows = taps[...]
        shifted = earlier_rows(tail_in[...], conv_in.astype(f32))
        pre = conv_sum(tap_rows, shifted, tap_rows[CONV : CONV + 1])
        act = (pre * sigmoid(pre)).astype(bf16).astype(f32)
        where = spread[...]
        x_dt = (act * dot(dt_s[...], where, NN)).astype(bf16)
        x_w = (act * dot(w_s[...], where, NN)).astype(bf16)
        ec = dot(ec_s[...], where, NN)
        state = state_in[...]
        state_o[...] = ec[length - 1 : length] * state + dot(bt_s[...], x_w, NN)
        carried = dot(c_s[...], state.astype(bf16), NN) * ec
        cum = cum_s[step]
        cumt = cumt_s[pl.ds(pl.multiple_of(step * GROUP, GROUP), GROUP), :]
        k = k_s[...]
        mask = lower_mask(half, half)
        left_lane = lax.broadcasted_iota(jnp.int32, (length, LANES), 1) < HEAD_DIM
        pieces = []
        for pair in range(GROUP // 2):
            x_pair = x_dt[:, pair * LANES : (pair + 1) * LANES]
            results = []
            for i in (2 * pair, 2 * pair + 1):
                col, row = cum[:, i : i + 1], cumt[i : i + 1, :]
                top = jnp.exp2(jnp.where(mask, col[:half] - row[:, :half], -1e30))
                low_left = jnp.exp2(col[half:] - row[:, :half])
                low_right = jnp.exp2(jnp.where(mask, col[half:] - row[:, half:], -1e30))
                top = (top * k[:half, :half]).astype(bf16)
                low = jnp.concatenate(
                    [
                        (low_left * k[half:, :half]).astype(bf16),
                        (low_right * k[half:, half:]).astype(bf16),
                    ],
                    axis=1,
                )
                results.append(
                    jnp.concatenate([dot(top, x_pair[:half], NN), dot(low, x_pair, NN)], axis=0)
                )
            pieces.append(jnp.where(left_lane, results[0], results[1]))
        within = jnp.concatenate(pieces, axis=1)
        ssm = within + carried + skip[...] * act
        ssm_o[...] = ssm
        u = ssm * (gate * sigmoid(gate))
        gained = u * gate_gain[...]
        u_s[:, pl.ds(pl.multiple_of(step * WIDTH, WIDTH), WIDTH)] = gained
        ssq_s[...] += jnp.sum(u * u, axis=1, keepdims=True)
        branch_o[...] += dot(gained.astype(bf16), wo[...], NN)

    @pl.when(step == GROUPS)
    def _():
        r = lax.rsqrt(ssq_s[...] * (1.0 / DI) + EPS)
        r_o[...] = r
        r = r[:, 0:1]
        for g in range(GROUPS):
            cols = slice(g * WIDTH, (g + 1) * WIDTH)
            gout_o[:, cols] = (u_s[:, cols] * r).astype(bf16)
        branch = branch_o[...] * r
        branch_o[...] = branch
        out_o[...] = (chosen(flag[0, 0], own_ref, other_ref) + branch).astype(bf16)


def bwd_body(
    flag, own_ref, other_ref, own_grad, other_grad, ngain, branch, r_ref, wo, wg, wc, wbc, taps, taps_bc, head_rows, skip,
    gate_gain, spread, gather, gate_ref, ssm_ref, cin, cin_bc, step_ref, tail_in, tail_bc_in,
    state_in, adj_in, next_in, next_bc_in,
    gout_ref, gg_o, gc_o, gin_o, gin_low_o, adj_o, next_o, next_bc_o, chan_o, chan_bc_o, ngrad_o,
    head_o,
    acc_s, kt_s, wt_s, b_s, c_s, ct_s, dt_s, ec_s, w_s, cum_s, cumt_s, db_s, dc_s, rows_s, cols_s,
    direct_s, fresh_s, carry_s, edge_s, dsilu_s, q_s,
):
    step = pl.program_id(0)
    length = own_ref.shape[0]
    half = length // 2

    @pl.when(step == 0)
    def _():
        gout_ref[...] = chosen_grad(flag[0, 1], own_grad, other_grad).astype(bf16)
        tap_rows = taps_bc[...]
        shifted = earlier_rows(tail_bc_in[...], cin_bc[...].astype(f32))
        pre = conv_sum(tap_rows, shifted, tap_rows[CONV : CONV + 1])
        sig = sigmoid(pre)
        dsilu_s[...] = sig * (1.0 + pre * (1.0 - sig))
        act = (pre * sig).astype(bf16)
        b_rows, c_rows = act[:, :STATE], act[:, STATE:]
        b_s[...] = b_rows
        c_s[...] = c_rows
        ct_s[...] = c_rows.astype(f32).T.astype(bf16)
        kt_s[...] = dot(b_rows, c_rows, NT)
        dt = head_steps(step_ref[...], head_rows[...])
        cum = running_sum(dt * head_rows[1:2])
        total = cum[length - 1 : length]
        dt_s[...] = halves(dt)
        ec_s[...] = halves(jnp.exp(cum))
        w_s[...] = halves(jnp.exp(total - cum))
        for g in range(GROUPS):
            cum_s[g] = cum[:, g * GROUP : (g + 1) * GROUP] * LOG2_E
        cumt_s[...] = (cum * LOG2_E).T
        for ref in (acc_s, wt_s, db_s, dc_s, rows_s, cols_s, direct_s, fresh_s, carry_s, edge_s):
            ref[...] = jnp.zeros_like(ref)
        rowdot = jnp.sum(branch[...] * gout_ref[...].astype(f32), axis=1, keepdims=True)
        q_s[...] = jnp.broadcast_to(rowdot * (1.0 / DI), q_s.shape) * r_ref[...] * r_ref[...]

    @pl.when(step < GROUPS)
    def _():
        grad_gated = dot(gout_ref[...], wo[...], NT)
        gate, ssm = gate_ref[...], ssm_ref[...]
        sig = sigmoid(gate)
        silu = gate * sig
        u = ssm * silu
        scaled = r_ref[:, 0:1] * grad_gated
        gain_grad = jnp.sum(scaled * u, axis=0, keepdims=True)
        grad_u = scaled * gate_gain[...] - u * q_s[:, 0:1]
        grad_ssm = grad_u * silu
        grad_gate = (grad_u * ssm * (sig * (1.0 + gate * (1.0 - sig)))).astype(bf16)
        gg_o[...] = grad_gate
        tap_rows = taps[...]
        shifted = earlier_rows(tail_in[...], cin[...].astype(f32))
        pre = conv_sum(tap_rows, shifted, tap_rows[CONV : CONV + 1])
        sig = sigmoid(pre)
        act = (pre * sig).astype(bf16).astype(f32)
        dsilu = sig * (1.0 + pre * (1.0 - sig))
        where, pick = spread[...], gather[...]
        dt, ec, w = (dot(ref[...], where, NN) for ref in (dt_s, ec_s, w_s))
        skip_grad = jnp.sum(act * grad_ssm, axis=0, keepdims=True)
        x_dt = act * dt
        x_low, g_low = x_dt.astype(bf16), grad_ssm.astype(bf16)
        g_ec = (grad_ssm * ec).astype(bf16)
        state, adj = state_in[...], adj_in[...]
        state_low, adj_low = state.astype(bf16), adj.astype(bf16)
        from_adj = w * dot(b_s[...], adj_low, NN)
        carried = ec * dot(c_s[...], state_low, NN)
        db_s[...] += dot((x_dt * w).astype(bf16), adj_low, NT)
        dc_s[...] += dot(g_ec, state_low, NT)
        last = ec[length - 1 : length]
        adj_o[...] = last * adj + dot(ct_s[...], g_ec, NN)
        edge = last * jnp.sum(state * adj, axis=0, keepdims=True)
        edge_s[...] += dot(edge.astype(bf16), pick, NN)
        cum = cum_s[step]
        start = pl.multiple_of(step * GROUP, GROUP)
        cumt = cumt_s[pl.ds(start, GROUP), :]
        kt = kt_s[...]
        mask = lax.broadcasted_iota(jnp.int32, (half, half), 0) <= lax.broadcasted_iota(
            jnp.int32, (half, half), 1
        )
        left_lane = lax.broadcasted_iota(jnp.int32, (length, LANES), 1) < HEAD_DIM
        lane_id = lax.broadcasted_iota(jnp.int32, (1, LANES), 1)
        pieces, col_sums = [], []
        row_sums = rows_s[...]
        w_tl, w_tr, w_br = wt_s[:half, :half], wt_s[:half, half:], wt_s[half:, half:]
        for pair in range(GROUP // 2):
            lanes = slice(pair * LANES, (pair + 1) * LANES)
            x_pair, g_pair = x_low[:, lanes], g_low[:, lanes]
            results = []
            for i in (2 * pair, 2 * pair + 1):
                col, row = cum[:, i : i + 1], cumt[i : i + 1, :]
                mine = left_lane if i % 2 == 0 else jnp.logical_not(left_lane)
                x_head = jnp.where(mine, x_pair, jnp.zeros_like(x_pair))
                l_tl = jnp.exp2(jnp.where(mask, row[:, :half] - col[:half], -1e30))
                l_tr = jnp.exp2(row[:, half:] - col[:half])
                l_br = jnp.exp2(jnp.where(mask, row[:, half:] - col[half:], -1e30))
                lk_tl, lk_tr, lk_br = (
                    l_tl * kt[:half, :half],
                    l_tr * kt[:half, half:],
                    l_br * kt[half:, half:],
                )
                mixed = jnp.concatenate([lk_tl.astype(bf16), lk_tr.astype(bf16)], axis=1)
                results.append(
                    jnp.concatenate(
                        [dot(mixed, g_pair, NN), dot(lk_br.astype(bf16), g_pair[half:], NN)], axis=0
                    )
                )
                p_top = dot(x_head[:half], g_pair, NT)
                p_br = dot(x_head[half:], g_pair[half:], NT)
                p_tl, p_tr = p_top[:, :half], p_top[:, half:]
                w_tl, w_tr, w_br = w_tl + l_tl * p_tl, w_tr + l_tr * p_tr, w_br + l_br * p_br
                z_tl, z_tr, z_br = lk_tl * p_tl, lk_tr * p_tr, lk_br * p_br
                sums = jnp.concatenate(
                    [
                        jnp.sum(z_tl + z_tr, axis=1, keepdims=True),
                        jnp.sum(z_br, axis=1, keepdims=True),
                    ],
                    axis=0,
                )
                row_sums = row_sums + jnp.where(lane_id == start + i, sums, 0.0)
                col_sums.append(
                    jnp.concatenate(
                        [
                            jnp.sum(z_tl, axis=0, keepdims=True),
                            jnp.sum(z_tr, axis=0, keepdims=True)
                            + jnp.sum(z_br, axis=0, keepdims=True),
                        ],
                        axis=1,
                    )
                )
            pieces.append(jnp.where(left_lane, results[0], results[1]))
        wt_s[:half, :half] = w_tl
        wt_s[:half, half:] = w_tr
        wt_s[half:, half:] = w_br
        rows_s[...] = row_sums
        cols_s[pl.ds(start, GROUP), :] = jnp.concatenate(col_sums, axis=0)
        mixed_grad = jnp.concatenate(pieces, axis=1) + from_adj
        direct_s[...] += dot((act * mixed_grad).astype(bf16), pick, NN)
        fresh_s[...] += dot((x_dt * from_adj).astype(bf16), pick, NN)
        carry_s[...] += dot((grad_ssm * carried).astype(bf16), pick, NN)
        grad_pre = (dt * mixed_grad + skip[...] * grad_ssm) * dsilu
        next_o[...] = grad_pre[0:8]
        grad_conv = conv_sum(tap_rows, later_rows(grad_pre, next_in[...]))
        grad_conv = grad_conv.astype(bf16)
        gc_o[:, pl.ds(pl.multiple_of(step * WIDTH, WIDTH), WIDTH)] = grad_conv
        sums = [
            jnp.sum(grad_pre * rows, axis=0, keepdims=True) for rows in shifted
        ]
        sums += [jnp.sum(grad_pre, axis=0, keepdims=True), gain_grad, skip_grad]
        chan_o[...] = jnp.concatenate(sums + [jnp.zeros_like(skip_grad)], axis=0)
        acc_s[...] += dot(grad_gate, wg[...], NT) + dot(grad_conv, wc[...], NT)

    @pl.when(step == GROUPS)
    def _():
        wt = wt_s[...].astype(bf16)
        grad_b = db_s[...] + dot(wt, c_s[...], NN)
        grad_c = dc_s[...] + dot(wt, b_s[...], TN)
        grad_pre = jnp.concatenate([grad_b, grad_c], axis=1) * dsilu_s[...]
        next_bc_o[...] = grad_pre[0:8]
        tap_rows = taps_bc[...]
        grad_conv = conv_sum(tap_rows, later_rows(grad_pre, next_bc_in[...]))
        shifted = earlier_rows(tail_bc_in[...], cin_bc[...].astype(f32))
        sums = [
            jnp.sum(grad_pre * rows, axis=0, keepdims=True) for rows in shifted
        ]
        sums += [jnp.sum(grad_pre, axis=0, keepdims=True)]
        chan_bc_o[...] = jnp.concatenate(sums + [jnp.zeros((3, BC), f32)], axis=0)
        dt = head_steps(step_ref[...], head_rows[...])
        rate = head_rows[1:2]
        ones = jnp.where(lower_mask(length, length), 1.0, 0.0).astype(f32)
        fresh = fresh_s[...]
        from_here = cols_s[...].T - rows_s[...] + carry_s[...]
        suffix = (
            dot(ones, from_here, TN, lax.Precision.HIGHEST)
            + dot(ones, fresh, NN, lax.Precision.HIGHEST)
            - fresh
            + edge_s[0:1]
        )
        decayed = rate * suffix
        grad_step = (direct_s[...] + decayed) * sigmoid(step_ref[...] + head_rows[0:1])
        head_o[...] = jnp.concatenate(
            [
                jnp.sum(grad_step, axis=0, keepdims=True),
                jnp.sum(dt * decayed, axis=0, keepdims=True),
                jnp.zeros((6, LANES), f32),
            ],
            axis=0,
        )
        low = jnp.concatenate([grad_conv.astype(bf16), grad_step.astype(bf16)], axis=1)
        gc_o[:, DI:] = low
        grad_normed = acc_s[...] + dot(low, wbc[...], NT)
        h = chosen(flag[0, 0], own_ref, other_ref)
        scale = lax.rsqrt(jnp.mean(h * h, axis=1, keepdims=True) + EPS)
        ngrad_o[...] = jnp.sum(grad_normed * h * scale, axis=0, keepdims=True)
        weighted = grad_normed * ngain[...]
        mean = jnp.mean(h * weighted, axis=1, keepdims=True)
        grad_in = gout_ref[...].astype(f32) + scale * weighted - h * (scale * scale * scale * mean)
        gin_o[...] = grad_in
        gin_low_o[...] = grad_in.astype(bf16)


def spread_table():
    table = np.zeros((2 * LANES, DI), np.float32)
    for head in range(HEADS):
        table[head, head * HEAD_DIM : (head + 1) * HEAD_DIM] = 1.0
        table[LANES + head, head * HEAD_DIM : (head + 1) * HEAD_DIM] = 1.0
    return table


def whole(shape):
    return pl.BlockSpec(shape, lambda i: (0,) * len(shape))


def by_group(rows, width=WIDTH, skip=0):
    return pl.BlockSpec((rows, width), lambda i: (0, jnp.minimum(i, GROUPS - 1) + skip))


def tail_of(rows, width, at):
    return pl.BlockSpec((rows, width), lambda i: (0, at // width))


def gather_table():
    table = np.zeros((GROUPS, WIDTH, LANES), np.float32)
    for group in range(GROUPS):
        for column in range(WIDTH):
            table[group, column, group * GROUP + column // HEAD_DIM] = 1.0
    return table.reshape(-1, LANES)


FLAGS = pl.BlockSpec(memory_space=pltpu.SMEM)


def fwd_call(flag, own, other, params, weights, state, tail, tail_bc):
    length = own.shape[0]
    win, wo = weights
    in_specs = [
        FLAGS, whole((length, D)), whole((length, D)), whole((1, D)), by_group(D), by_group(D, WIDTH, GROUPS), tail_of(D, TAIL, 2 * DI),
        pl.BlockSpec((WIDTH, D), lambda i: (jnp.minimum(i, GROUPS - 1), 0)),
        by_group(8), tail_of(8, BC, DI), whole((8, LANES)), by_group(1), by_group(1),
        by_group(2 * LANES), by_group(16), whole((16, BC)), by_group(STATE),
    ]
    out = [
        ((length, D), bf16, whole((length, D))),
        ((length, DI), f32, by_group(length)),
        ((length, DI), bf16, by_group(length)),
        ((length, BC), bf16, whole((length, BC))),
        ((length, LANES), f32, whole((length, LANES))),
        ((length, DI), f32, by_group(length)),
        ((STATE, DI), f32, by_group(STATE)),
        ((length, DI), bf16, whole((length, DI))),
        ((length, LANES), f32, whole((length, LANES))),
        ((length, D), f32, whole((length, D))),
        ((length, D), bf16, whole((length, D))),
        ((16, DI), bf16, by_group(16)),
        ((16, BC), bf16, whole((16, BC))),
    ]
    scratch = [
        ((length, DI), f32), ((length, LANES), f32), ((length, length), f32),
        ((length, STATE), bf16), ((STATE, length), bf16), ((length, 2 * LANES), bf16),
        ((length, 2 * LANES), bf16), ((length, 2 * LANES), bf16), ((GROUPS, length, GROUP), f32),
        ((LANES, length), f32),
    ]
    return pl.pallas_call(
        fwd_body,
        grid=(GROUPS + 1,),
        in_specs=in_specs,
        out_specs=[spec for _, _, spec in out],
        out_shape=[jax.ShapeDtypeStruct(shape, dtype) for shape, dtype, _ in out],
        scratch_shapes=[pltpu.VMEM(shape, dtype) for shape, dtype in scratch],
        compiler_params=pltpu.CompilerParams(
            dimension_semantics=("arbitrary",), vmem_limit_bytes=VMEM_LIMIT
        ),
        cost_estimate=pl.CostEstimate(flops=12 * 10**9, bytes_accessed=45 * 10**6, transcendentals=5 * 10**6),
        name="layer_forward",
    )(
        flag, own, other, params["norm_gain"], win, win, win, wo, params["taps"], params["taps"],
        params["heads"], params["skip"], params["gate_gain"], params["spread"], tail, tail_bc, state,
    )


def bwd_call(flag, own_grad, other_grad, kept, params, weights, adj, ahead, ahead_bc):
    length = own_grad.shape[0]
    win, wo = weights
    rows_of_wo = pl.BlockSpec((WIDTH, D), lambda i: (jnp.minimum(i, GROUPS - 1), 0))
    pick = pl.BlockSpec((WIDTH, LANES), lambda i: (jnp.minimum(i, GROUPS - 1), 0))
    in_specs = [
        FLAGS, whole((length, D)), whole((length, D)), whole((length, D)), whole((length, D)),
        whole((1, D)), whole((length, D)),
        whole((length, LANES)), rows_of_wo, by_group(D), by_group(D, WIDTH, GROUPS), tail_of(D, TAIL, 2 * DI),
        by_group(8), tail_of(8, BC, DI), whole((8, LANES)), by_group(1), by_group(1),
        by_group(2 * LANES), pick, by_group(length), by_group(length), by_group(length),
        whole((length, BC)), whole((length, LANES)), by_group(16), whole((16, BC)),
        by_group(STATE), by_group(STATE), by_group(8), whole((8, BC)),
    ]
    out = [
        ((length, D), bf16, whole((length, D))),
        ((length, DI), bf16, by_group(length)),
        ((length, DI + TAIL), bf16, whole((length, DI + TAIL))),
        ((length, D), f32, whole((length, D))),
        ((length, D), bf16, whole((length, D))),
        ((STATE, DI), f32, by_group(STATE)),
        ((8, DI), f32, by_group(8)),
        ((8, BC), f32, whole((8, BC))),
        ((8, DI), f32, by_group(8)),
        ((8, BC), f32, whole((8, BC))),
        ((1, D), f32, whole((1, D))),
        ((8, LANES), f32, whole((8, LANES))),
    ]
    scratch = [
        ((length, D), f32), ((length, length), f32), ((length, length), f32),
        ((length, STATE), bf16), ((length, STATE), bf16), ((STATE, length), bf16),
        ((length, 2 * LANES), bf16), ((length, 2 * LANES), bf16), ((length, 2 * LANES), bf16),
        ((GROUPS, length, GROUP), f32), ((LANES, length), f32), ((length, STATE), f32),
        ((length, STATE), f32), ((length, LANES), f32), ((LANES, length), f32),
        ((length, LANES), f32), ((length, LANES), f32), ((length, LANES), f32), ((1, LANES), f32),
        ((length, BC), f32), ((length, LANES), f32),
    ]
    return pl.pallas_call(
        bwd_body,
        grid=(GROUPS + 1,),
        in_specs=in_specs,
        out_specs=[spec for _, _, spec in out],
        out_shape=[jax.ShapeDtypeStruct(shape, dtype) for shape, dtype, _ in out],
        scratch_shapes=[pltpu.VMEM(shape, dtype) for shape, dtype in scratch],
        compiler_params=pltpu.CompilerParams(
            dimension_semantics=("arbitrary",), vmem_limit_bytes=VMEM_LIMIT
        ),
        cost_estimate=pl.CostEstimate(flops=25 * 10**9, bytes_accessed=55 * 10**6, transcendentals=8 * 10**6),
        name="layer_backward",
    )(
        flag, kept["own"], kept["other"], own_grad, other_grad, params["norm_gain"], kept["branch"], kept["r"], wo, win, win, win,
        params["taps"], params["taps"], params["heads"], params["skip"], params["gate_gain"],
        params["spread"], params["gather"], kept["gate"], kept["ssm"], kept["cin"], kept["cin_bc"],
        kept["step"], kept["tail"], kept["tail_bc"], kept["state"], adj, ahead, ahead_bc,
    )


def xor_route(size, bit):
    return [(i, i ^ bit) for i in range(size)]


def bits_of(size):
    return [1 << b for b in range(size.bit_length() - 1)]


def gather_small(row):
    for axis in ("seq", "dp"):
        size, position = lax.axis_size(axis), lax.axis_index(axis)
        for bit in bits_of(size):
            other = lax.ppermute(row, axis, xor_route(size, bit))
            row = jnp.where(
                (position & bit) == 0,
                jnp.concatenate([row, other], axis=0),
                jnp.concatenate([other, row], axis=0),
            )
    return row


def exchanges():
    return [(axis, bit) for axis in ("dp", "seq") for bit in bits_of(lax.axis_size(axis))]


def exchange(value, axis, bit):
    return value + lax.ppermute(value, axis, xor_route(lax.axis_size(axis), bit))


def sum_small(value):
    for axis, bit in exchanges():
        value = exchange(value, axis, bit)
    return value


def direct_paths():
    return lax.axis_size("dp") == 4 and lax.axis_size("seq") == 4


RING = 8


def ring_place(position):
    return jnp.where(position < 4, position, 11 - position)


def ring_route(step):
    def device(position, core):
        y, z = (0, position) if position < 4 else (1, 7 - position)
        return (y * 2 + core) * 4 + z

    return [
        (device(p, core), device((p + step) % RING, core)) for p in range(RING) for core in range(2)
    ]


def around(value, step):
    return lax.ppermute(value, ("dp", "seq"), ring_route(step))


def across(value):
    return lax.ppermute(value, "dp", xor_route(4, 1))


def own_position():
    dp, z = lax.axis_index("dp"), lax.axis_index("seq")
    y = dp // 2
    return jnp.where(y == 0, z, 7 - z), dp % 2


def together(up, down):
    pairs = [lax.optimization_barrier(pair) for pair in zip(up, down)]
    return [a for a, _ in pairs], [b for _, b in pairs]


def gather_rows(shards):
    if not direct_paths():
        return [lax.all_gather(shard, ("dp", "seq"), axis=0, tiled=True) for shard in shards]
    position, core = own_position()
    held = [jnp.zeros((16,) + shard.shape, shard.dtype) for shard in shards]

    def place(held, pieces, offset, start=0):
        at = ring_place((position + offset) % RING)
        at = (at // 4) * 8 + at % 4
        others = [across(piece) for piece in pieces]
        for of_core, values in ((core, pieces), (1 - core, others)):
            held = [
                lax.dynamic_update_slice(whole, value[None], (at + of_core * 4, start * rows, 0))
                for whole, value, rows in zip(held, values, halves_of)
            ]
        return held

    halves_of = [shard.shape[0] // 2 for shard in shards]
    up, down = shards, shards
    held = place(held, shards, 0)
    for hop in range(1, 4):
        up, down = [around(v, 1) for v in up], [around(v, -1) for v in down]
        up, down = together(up, down)
        held = place(place(held, up, -hop), down, hop)
    up = [around(v[:rows], 1) for v, rows in zip(up, halves_of)]
    down = [around(v[rows:], -1) for v, rows in zip(down, halves_of)]
    held = place(place(held, up, 4), down, 4, 1)
    return [whole.reshape((-1,) + whole.shape[2:]) for whole in held]


def reduce_rows(chips, small, early):
    position, _ = own_position()
    hops = exchanges()

    def term(chip, offset):
        at = ring_place((position + offset) % RING)
        return lax.dynamic_index_in_dim(chip, at, 0, keepdims=False)

    half = [chip.shape[1] // 2 for chip in chips]
    up = [around(term(chip, 4)[:rows], 1) for chip, rows in zip(chips, half)]
    down = [around(term(chip, -4)[rows:], -1) for chip, rows in zip(chips, half)]
    small = exchange(small, *hops[0])
    up, down = together(up, down)
    up[0], small, early = lax.optimization_barrier((up[0], small, early))
    up = [jnp.pad(v, ((0, rows), (0, 0))) for v, rows in zip(up, half)]
    down = [jnp.pad(v, ((rows, 0), (0, 0))) for v, rows in zip(down, half)]
    for hop, offset in enumerate((3, 2, 1), 1):
        up = [
            around((term(chip, offset).astype(f32) + v.astype(f32)).astype(bf16), 1)
            for chip, v in zip(chips, up)
        ]
        down = [
            around((term(chip, -offset).astype(f32) + v.astype(f32)).astype(bf16), -1)
            for chip, v in zip(chips, down)
        ]
        small = exchange(small, *hops[hop])
        up, down = together(up, down)
        up[0], small = lax.optimization_barrier((up[0], small))
    sums = [
        term(chip, 0).astype(f32) + a.astype(f32) + b.astype(f32)
        for chip, a, b in zip(chips, up, down)
    ]
    return sums, small, early


def weight_grads(pairs, small, early, ready):
    def term(columns, right):
        return jnp.einsum("td,te->de", columns, right, preferred_element_type=f32)

    if not direct_paths():
        sums = [
            lax.optimization_barrier(
                lax.psum_scatter(term(left, right), ("dp", "seq"), scatter_dimension=0, tiled=True)
            )
            for left, right in pairs
        ]
        return sums, sum_small(small), early, ready
    core = lax.axis_index("dp") % 2

    def owned(left, right, which):
        quarter = left.shape[1] // 4
        parts = [left[:, i * quarter : (i + 1) * quarter] for i in range(4)]
        chosen = jnp.concatenate(
            [jnp.where(which == 0, parts[0], parts[1]), jnp.where(which == 0, parts[2], parts[3])],
            axis=1,
        )
        return term(chosen, right).astype(bf16).reshape(RING, quarter // 4, right.shape[1])

    arrived = [across(owned(left, right, 1 - core)) for left, right in pairs]
    left, ready = lax.optimization_barrier((pairs[0][0], ready))
    chips = [
        (owned(left, right, core).astype(f32) + other.astype(f32)).astype(bf16)
        for (_, right), other in zip(pairs, arrived)
    ]
    return *reduce_rows(chips, small, early), ready


def turn(value, shift, parts):
    size = lax.axis_size("seq")
    route = [(i, i - i % parts + (i % parts + shift) % parts) for i in range(size)]
    return lax.ppermute(value, "seq", route)


def to_sequences(rows):
    parts = rows.shape[0]
    rank = lax.axis_index("seq") % parts
    arrived = []
    for shift in range(parts):
        piece = lax.dynamic_index_in_dim(rows, (rank + shift) % parts, 0, keepdims=False)
        arrived.append(piece if shift == 0 else turn(piece, shift, parts))
    arrived = jnp.stack(arrived)
    return [
        lax.dynamic_index_in_dim(arrived, (rank - k) % parts, 0, keepdims=False)
        for k in range(parts)
    ]


def to_pieces(blocks, sent_type):
    parts = len(blocks)
    rank = lax.axis_index("seq") % parts
    stacked = jnp.stack(blocks)
    held = stacked
    pieces = []
    for shift in range(parts):
        piece = lax.dynamic_index_in_dim(stacked, (rank + shift) % parts, 0, keepdims=False)
        if shift:
            piece = turn(piece.astype(sent_type), shift, parts)
        pieces.append(piece)
    return stacked, pieces


def laid_out(held, pieces):
    parts = len(pieces)
    rank = lax.axis_index("seq") % parts
    for shift, piece in enumerate(pieces):
        piece = piece.astype(held.dtype)
        held = lax.dynamic_update_slice(held, piece[None], ((rank - shift) % parts, 0, 0))
    return held


KEPT = (
    "normed", "gate", "cin", "cin_bc", "step", "ssm", "state_out", "gout", "r", "branch", "out",
    "tail_out", "tail_bc_out",
)
SKEW = 2


def flags(first, grad):
    return jnp.stack([jnp.where(first, 1, 0), jnp.asarray(grad, jnp.int32)]).astype(jnp.int32)[None]


def shards(
    tokens, cotangent, in_proj, out_proj, conv_weight, conv_bias, norm_gain, gate_gain, step_bias,
    log_decay, skip_gain,
):
    first = lax.axis_index("section") == 0
    seq = lax.axis_size("seq")
    parts, length = tokens.shape[0], tokens.shape[1]
    owned = in_proj.shape[1]
    blocks_in = to_sequences(jnp.where(first, tokens, cotangent))

    shard = jnp.pad(in_proj[0], ((0, 0), (0, TAIL - BC - HEADS)))
    weights = (
        lax.all_gather(shard, ("dp", "seq"), axis=0, tiled=True),
        gather_rows([out_proj[0]])[0],
    )

    sizes = [CONV * conv_bias.shape[1], conv_bias.shape[1], norm_gain.shape[1], gate_gain.shape[1]]
    packed = jnp.concatenate([conv_weight[0].reshape(-1), conv_bias[0], norm_gain[0], gate_gain[0]])
    packed = gather_small(packed[None]).astype(f32)
    ends = np.cumsum(sizes)
    taps, shift, gain_in, gain_gate = (
        packed[:, end - size : end] for end, size in zip(ends, sizes)
    )
    taps = jnp.swapaxes(taps.reshape(-1, CONV, conv_bias.shape[1]), 0, 1).reshape(CONV, -1)
    taps = jnp.concatenate([taps, shift.reshape(1, -1), jnp.zeros((3, taps.shape[1]), f32)], axis=0)
    lanes = ((0, 0), (0, LANES - HEADS))
    params = {
        "norm_gain": gain_in.reshape(1, -1),
        "gate_gain": gain_gate.reshape(1, -1),
        "taps": taps,
        "heads": jnp.pad(
            jnp.concatenate([step_bias, -jnp.exp(log_decay), jnp.zeros((6, HEADS), f32)], axis=0),
            lanes,
        ),
        "skip": jnp.repeat(skip_gain, HEAD_DIM, axis=1),
        "spread": jnp.asarray(spread_table(), bf16),
        "gather": jnp.asarray(gather_table(), bf16),
    }

    ticks = parts + SKEW
    hops = seq // parts

    def forward(start):
        kept, received = [], [jnp.zeros((length, D), bf16)] * SKEW
        carry = start
        for tick in range(ticks):
            if tick == SKEW:
                carry = tuple(jnp.where(first, now, at) for now, at in zip(carry, start))
            own, other = blocks_in[min(tick, parts - 1)], received[tick]
            values = dict(zip(KEPT, fwd_call(flags(first, 0), own, other, params, weights, *carry)))
            values.update(own=own, other=other, state=carry[0], tail=carry[1], tail_bc=carry[2])
            carry = (values["state_out"], values["tail_out"], values["tail_bc_out"])
            kept.append(values)
            if tick < parts:
                received.append(lax.ppermute(values["out"], "section", [(0, 1)]))
        return kept

    def backward(kept, start, before_last=None):
        early = None
        zeros = tuple(jnp.zeros_like(part) for part in start)
        carry = tuple(jnp.where(first, zero, at) for zero, at in zip(zeros, start))
        grads, received = [None] * ticks, [jnp.zeros((length, D), bf16)] * SKEW
        for tick in range(ticks):
            if tick == SKEW and hops > 1:
                carry = tuple(jnp.where(first, at, now) for now, at in zip(carry, start))
            if tick == parts:
                carry = tuple(jnp.where(first, now, zero) for now, zero in zip(carry, zeros))
            from_loss = blocks_in[max(parts - 1 - tick, 0)]
            late = jnp.int32(2 if tick >= parts else 1)
            if before_last is not None and tick == ticks - 1:
                early = before_last(grads, received[tick])
                from_loss, early = lax.optimization_barrier((from_loss, early))
            at = ticks - 1 - tick
            names = (
                "out", "gate", "conv", "in", "in_low", "adj", "next", "next_bc", "chan", "chan_bc",
                "norm", "head",
            )
            values = dict(
                zip(
                    names,
                    bwd_call(
                        flags(first, jnp.where(first, 0, late)),
                        from_loss,
                        received[tick],
                        kept[at],
                        params,
                        weights,
                        *carry,
                    ),
                )
            )
            carry = (values["adj"], values["next"], values["next_bc"])
            grads[at] = values
            if tick < parts:
                sent, received[-1] = lax.optimization_barrier((values["in_low"], received[-1]))
                received.append(lax.ppermute(sent, "section", [(1, 0)]))
        return grads, early

    start = (jnp.zeros((STATE, DI), f32), jnp.zeros((16, DI), bf16), jnp.zeros((16, BC), bf16))
    if hops > 1:

        def onward(_, start):
            kept = forward(start)
            ends = (
                tuple(kept[parts - 1][name] for name in ("state_out", "tail_out", "tail_bc_out")),
                tuple(kept[ticks - 1][name] for name in ("state_out", "tail_out", "tail_bc_out")),
            )
            route = [(i, i + parts) for i in range(seq - parts)]
            return tuple(
                lax.ppermute(jnp.where(first, a, b), "seq", route) for a, b in zip(*ends)
            )

        start = lax.fori_loop(0, hops - 1, onward, start)
    kept = forward(start)
    activations = laid_out(
        *to_pieces(
            [jnp.where(first, kept[k]["out"], kept[k + SKEW]["out"]) for k in range(parts)], bf16
        )
    )[None]

    start = (jnp.zeros((STATE, DI), f32), jnp.zeros((8, DI), f32), jnp.zeros((8, BC), f32))
    if hops > 1:

        def back(_, start):
            grads, _ = backward(kept, start)
            ends = (
                tuple(grads[0][name] for name in ("adj", "next", "next_bc")),
                tuple(grads[SKEW][name] for name in ("adj", "next", "next_bc")),
            )
            route = [(i, i - parts) for i in range(parts, seq)]
            return tuple(
                lax.ppermute(jnp.where(first, a, b), "seq", route) for a, b in zip(*ends)
            )

        start = lax.fori_loop(0, hops - 1, back, start)
    def select(values, name):
        return jnp.concatenate(
            [jnp.where(first, values[k][name], values[k + SKEW][name]) for k in range(parts)], axis=0
        )

    def out_term(grads, received):
        branch_grads = [jnp.where(first, received, blocks_in[0])] + [
            jnp.where(first, grads[k]["out"], grads[k + SKEW]["out"]) for k in range(1, parts)
        ]
        return jnp.einsum(
            "td,te->de",
            select(kept, "gout"),
            jnp.concatenate(branch_grads, axis=0),
            preferred_element_type=f32,
        ).astype(bf16)

    grads, term = backward(kept, start, out_term)
    grad_out_proj = lax.psum_scatter(
        term, ("dp", "seq"), scatter_dimension=0, tiled=True
    ).astype(f32)
    normed = select(kept, "normed")
    def total(name):
        return sum(values[name] for values in grads)

    channels = jnp.concatenate([total("chan"), total("chan_bc")], axis=1)
    head = total("head")
    last_row = jnp.concatenate([total("norm"), head[0:1], head[1:2]], axis=1)
    fill = channels.shape[1] - last_row.shape[1]
    small = (channels + jnp.pad(last_row, ((7, 0), (0, fill))))
    held, pieces = to_pieces(
        [jnp.where(first, grads[k]["in"], grads[k + SKEW]["in"]) for k in range(parts)], bf16
    )
    near = [pieces[1], pieces[-1]]
    (grad_gate, grad_conv), small, grad_out_proj, near = weight_grads(
        [(normed, select(grads, "gate")), (normed, select(grads, "conv"))],
        small,
        grad_out_proj,
        near,
    )
    pieces[1], pieces[-1] = near
    pieces, grad_gate = lax.optimization_barrier((pieces, grad_gate))
    input_grads = laid_out(held, pieces)[None]
    grad_in_proj = jnp.concatenate([grad_gate, grad_conv[:, : DI + BC + HEADS]], axis=1)[None]

    place = lax.axis_index("dp") * seq + lax.axis_index("seq")

    def mine(flat, width):
        return lax.dynamic_slice_in_dim(flat, place * width, width, axis=flat.ndim - 1)

    width = conv_bias.shape[1]
    return (
        activations,
        input_grads,
        grad_in_proj,
        grad_out_proj[None],
        mine(small[:CONV], width)[None],
        mine(small[CONV], width)[None],
        mine(small[7, :D], owned)[None],
        mine(small[5, :DI], gate_gain.shape[1])[None],
        small[7:8, D : D + HEADS],
        small[7:8, D + LANES : D + LANES + HEADS],
        small[6, :DI].reshape(HEADS, HEAD_DIM).sum(axis=1)[None],
    )


def solution(mesh):
    placed = (
        P("dp", "seq", None),
        P("dp", "seq", None),
        P("section", ("dp", "seq"), None),
        P("section", ("dp", "seq"), None),
        P("section", None, ("dp", "seq")),
        P("section", ("dp", "seq")),
        P("section", ("dp", "seq")),
        P("section", ("dp", "seq")),
        P("section", None),
        P("section", None),
        P("section", None),
    )
    return jax.shard_map(
        shards,
        mesh=mesh,
        in_specs=placed,
        out_specs=(
            P("section", "dp", "seq", None),
            P("section", "dp", "seq", None),
        )
        + placed[2:],
        check_vma=False,
    )
```

```python
import jax
import jax.numpy as jnp
import numpy as np
from jax import lax
from jax.experimental import pallas as pl
from jax.experimental.pallas import tpu as pltpu
from jax.sharding import PartitionSpec as P

D = 1536
HEADS = 48
HEAD_DIM = 64
STATE = 128
CONV = 4
DI = 3072
BC = 2 * STATE
TAIL = BC + 128
GROUP = 8
WIDTH = GROUP * HEAD_DIM
GROUPS = HEADS // GROUP
LANES = 128
EPS = 1e-05
LOG2_E = 1.4426950408889634
f32 = jnp.float32
bf16 = jnp.bfloat16
VMEM_LIMIT = 56 * 2**20
NN = ((1,), (0,))
NT = ((1,), (1,))
TN = ((0,), (0,))


def dot(a, b, dims, precision=None):
    return lax.dot_general(a, b, (dims, ((), ())), preferred_element_type=f32, precision=precision)


def halves(value):
    top = value.astype(bf16)
    rest = (value - top.astype(f32)).astype(bf16)
    return jnp.concatenate([top, rest], axis=1)


def lower_mask(rows, cols):
    return lax.broadcasted_iota(jnp.int32, (rows, cols), 0) >= lax.broadcasted_iota(
        jnp.int32, (rows, cols), 1
    )


def sigmoid(v):
    return 0.5 * jnp.tanh(0.5 * v) + 0.5


def head_steps(step_raw, head_rows):
    biased = step_raw + head_rows[0:1]
    return jnp.maximum(biased, 0.0) + jnp.log1p(jnp.exp(-jnp.abs(biased)))


def running_sum(value):
    length = value.shape[0]
    ones = jnp.where(lower_mask(length, length), 1.0, 0.0).astype(f32)
    return dot(ones, value, NN, lax.Precision.HIGHEST)


def earlier_rows(tail, rows):
    joined = jnp.concatenate([tail[8:16].astype(f32), rows], axis=0)
    shifted = [pltpu.roll(joined, shift, 0)[8:] for shift in range(CONV - 1, 0, -1)]
    return shifted + [rows]


def later_rows(rows, head):
    length = rows.shape[0]
    joined = jnp.concatenate([rows, head], axis=0)
    shifted = [pltpu.roll(joined, length + 8 - shift, 0)[:length] for shift in range(CONV - 1, 0, -1)]
    return shifted + [rows]


def conv_sum(taps, shifted, start=0.0):
    for j in range(CONV):
        start = start + shifted[j] * taps[j : j + 1]
    return start


def chosen(flag, own, other):
    return jnp.where(flag == 1, own[...].astype(f32), other[...].astype(f32))


def chosen_grad(flag, own, other):
    other_or_zero = jnp.where(flag == 0, other[...].astype(f32), 0.0)
    return jnp.where(flag == 1, own[...].astype(f32), other_or_zero)


def fwd_body(
    flag, own_ref, other_ref, ngain, wg, wc, wbc, wo, taps, taps_bc, head_rows, skip, gate_gain, spread, tail_in,
    tail_bc_in, state_in,
    normed_o, cin_o, act_o, slope_o, cin_bc_o, step_o, silu_o, turned_o, u_o, state_o, gout_o, r_o, branch_o, out_o,
    tail_o, tail_bc_o,
    u_s, ssq_s, k_s, c_s, bt_s, sp_s, cum_s, cumt_s,
):
    step = pl.program_id(0)
    length = own_ref.shape[0]
    half = length // 2

    @pl.when(step == 0)
    def _():
        h = chosen(flag[0, 0], own_ref, other_ref)
        scale = lax.rsqrt(jnp.mean(h * h, axis=1, keepdims=True) + EPS)
        normed = (h * scale * ngain[...]).astype(bf16)
        normed_o[...] = normed
        projected = dot(normed, wbc[...], NN)
        step_raw = projected[:, BC:]
        step_o[...] = step_raw
        conv_in = projected[:, :BC].astype(bf16)
        cin_bc_o[...] = conv_in
        tail_bc_o[...] = conv_in[length - 16 :]
        tap_rows = taps_bc[...]
        shifted = earlier_rows(tail_bc_in[...], conv_in.astype(f32))
        pre = conv_sum(tap_rows, shifted, tap_rows[CONV : CONV + 1])
        act = (pre * sigmoid(pre)).astype(bf16)
        b_rows, c_rows = act[:, :STATE], act[:, STATE:]
        c_s[...] = c_rows
        bt_s[...] = b_rows.astype(f32).T.astype(bf16)
        k_s[...] = dot(c_rows, b_rows, NT)
        dt = head_steps(step_raw, head_rows[...])
        cum = running_sum(dt * head_rows[1:2])
        total = cum[length - 1 : length]
        sp_s[0:length] = halves(dt)
        sp_s[length : 2 * length] = halves(jnp.exp(cum))
        sp_s[2 * length :] = halves(dt * jnp.exp(total - cum))
        for g in range(GROUPS):
            cum_s[g] = cum[:, g * GROUP : (g + 1) * GROUP] * LOG2_E
        cumt_s[...] = (cum * LOG2_E).T
        ssq_s[...] = jnp.zeros_like(ssq_s)
        branch_o[...] = jnp.zeros_like(branch_o)

    @pl.when(step < GROUPS)
    def _():
        normed = normed_o[...]
        gate = dot(normed, wg[...], NN)
        conv_in = dot(normed, wc[...], NN).astype(bf16)
        cin_o[...] = conv_in
        tail_o[...] = conv_in[length - 16 :]
        tap_rows = taps[...]
        shifted = earlier_rows(tail_in[...], conv_in.astype(f32))
        pre = conv_sum(tap_rows, shifted, tap_rows[CONV : CONV + 1])
        sig = sigmoid(pre)
        act = pre * sig
        slope_o[...] = (sig + act * (1.0 - sig)).astype(bf16)
        act_o[...] = act.astype(bf16)
        act = act_o[...].astype(f32)
        where = spread[...]
        spreads = dot(sp_s[...], where, NN)
        x_dt = (act * spreads[:length]).astype(bf16)
        x_w = (act * spreads[2 * length :]).astype(bf16)
        ec = spreads[length : 2 * length]
        state = state_in[...]
        state_o[...] = ec[length - 1 : length] * state + dot(bt_s[...], x_w, NN)
        carried = dot(c_s[...], state.astype(bf16), NN) * ec
        cum = cum_s[step]
        cumt = cumt_s[pl.ds(pl.multiple_of(step * GROUP, GROUP), GROUP), :]
        k = k_s[...]
        mask = lower_mask(half, half)
        left_lane = lax.broadcasted_iota(jnp.int32, (half, LANES), 1) < HEAD_DIM
        pieces = []
        for pair in range(GROUP // 2):
            x_pair = x_dt[:, pair * LANES : (pair + 1) * LANES]
            tops, lows = [], []
            for i in (2 * pair, 2 * pair + 1):
                col, row = cum[:, i : i + 1], cumt[i : i + 1, :]
                top = jnp.exp2(jnp.where(mask, col[:half] - row[:, :half], -1e30))
                low_left = jnp.exp2(col[half:] - row[:, :half])
                low_right = jnp.exp2(jnp.where(mask, col[half:] - row[:, half:], -1e30))
                tops.append((top * k[:half, :half]).astype(bf16))
                low = jnp.concatenate(
                    [
                        (low_left * k[half:, :half]).astype(bf16),
                        (low_right * k[half:, half:]).astype(bf16),
                    ],
                    axis=1,
                )
                lows.append(low)
            tops = dot(jnp.concatenate(tops, axis=0), x_pair[:half], NN)
            lows = dot(jnp.concatenate(lows, axis=0), x_pair, NN)
            pieces.append(
                jnp.concatenate(
                    [jnp.where(left_lane, both[:half], both[half:]) for both in (tops, lows)],
                    axis=0,
                )
            )
        within = jnp.concatenate(pieces, axis=1)
        ssm = within + carried + skip[...] * act
        sig = sigmoid(gate)
        silu = gate * sig
        silu_o[...] = silu.astype(bf16)
        turned_o[...] = (ssm * (sig + silu * (1.0 - sig))).astype(bf16)
        u = ssm * silu
        u_o[...] = u.astype(bf16)
        gained = u * gate_gain[...]
        u_s[:, pl.ds(pl.multiple_of(step * WIDTH, WIDTH), WIDTH)] = gained
        ssq_s[...] += jnp.sum(u * u, axis=1, keepdims=True)
        branch_o[...] += dot(gained.astype(bf16), wo[...], NN)

    @pl.when(step == GROUPS)
    def _():
        r = lax.rsqrt(ssq_s[...] * (1.0 / DI) + EPS)
        r_o[...] = r
        r = r[:, 0:1]
        for g in range(GROUPS):
            cols = slice(g * WIDTH, (g + 1) * WIDTH)
            gout_o[:, cols] = (u_s[:, cols] * r).astype(bf16)
        branch = branch_o[...] * r
        branch_o[...] = branch
        out_o[...] = (chosen(flag[0, 0], own_ref, other_ref) + branch).astype(bf16)


def bwd_body(
    flag, own_ref, other_ref, own_grad, other_grad, ngain, branch, r_ref, wo, wg, wc, wbc, taps, taps_bc, head_rows, skip,
    gate_gain, spread, gather, silu_ref, turned_ref, u_ref, act_ref, slope_ref, cin, cin_bc, step_ref,
    tail_bc_in,
    state_in, adj_in, next_in, next_bc_in,
    gout_ref, gg_o, gc_o, gin_o, gin_low_o, adj_o, next_o, next_bc_o, chan_o, chan_bc_o, ngrad_o,
    head_o,
    acc_s, kt_s, wt_s, b_s, c_s, ct_s, sp_s, cum_s, cumt_s, db_s, dc_s, rows_s, cols_s,
    direct_s, fresh_s, carry_s, edge_s, dsilu_s, q_s,
):
    step = pl.program_id(0)
    length = own_ref.shape[0]
    half = length // 2

    @pl.when(step == 0)
    def _():
        gout_ref[...] = chosen_grad(flag[0, 1], own_grad, other_grad).astype(bf16)
        tap_rows = taps_bc[...]
        shifted = earlier_rows(tail_bc_in[...], cin_bc[...].astype(f32))
        pre = conv_sum(tap_rows, shifted, tap_rows[CONV : CONV + 1])
        sig = sigmoid(pre)
        dsilu_s[...] = sig * (1.0 + pre * (1.0 - sig))
        act = (pre * sig).astype(bf16)
        b_rows, c_rows = act[:, :STATE], act[:, STATE:]
        b_s[...] = b_rows
        c_s[...] = c_rows
        ct_s[...] = c_rows.astype(f32).T.astype(bf16)
        kt_s[...] = dot(b_rows, c_rows, NT)
        dt = head_steps(step_ref[...], head_rows[...])
        cum = running_sum(dt * head_rows[1:2])
        total = cum[length - 1 : length]
        sp_s[0:length] = halves(dt)
        sp_s[length : 2 * length] = halves(jnp.exp(cum))
        sp_s[2 * length :] = halves(jnp.exp(total - cum))
        for g in range(GROUPS):
            cum_s[g] = cum[:, g * GROUP : (g + 1) * GROUP] * LOG2_E
        cumt_s[...] = (cum * LOG2_E).T
        for ref in (acc_s, wt_s, db_s, dc_s, rows_s, cols_s, direct_s, fresh_s, carry_s, edge_s):
            ref[...] = jnp.zeros_like(ref)
        rowdot = jnp.sum(branch[...] * gout_ref[...].astype(f32), axis=1, keepdims=True)
        q_s[...] = jnp.broadcast_to(rowdot * (1.0 / DI), q_s.shape) * r_ref[...] * r_ref[...]

    @pl.when(step < GROUPS)
    def _():
        grad_gated = dot(gout_ref[...], wo[...], NT)
        u = u_ref[...].astype(f32)
        scaled = r_ref[:, 0:1] * grad_gated
        gain_grad = jnp.sum(scaled * u, axis=0, keepdims=True)
        grad_u = scaled * gate_gain[...] - u * q_s[:, 0:1]
        grad_ssm = grad_u * silu_ref[...].astype(f32)
        grad_gate = (grad_u * turned_ref[...].astype(f32)).astype(bf16)
        gg_o[...] = grad_gate
        act = act_ref[...].astype(f32)
        where, pick = spread[...], gather[...]
        spreads = dot(sp_s[...], where, NN)
        dt, ec, w = (spreads[i * length : (i + 1) * length] for i in range(3))
        skip_grad = jnp.sum(act * grad_ssm, axis=0, keepdims=True)
        x_dt = act * dt
        x_low, g_low = x_dt.astype(bf16), grad_ssm.astype(bf16)
        g_ec = (grad_ssm * ec).astype(bf16)
        state, adj = state_in[...], adj_in[...]
        state_low, adj_low = state.astype(bf16), adj.astype(bf16)
        from_adj = w * dot(b_s[...], adj_low, NN)
        carried = ec * dot(c_s[...], state_low, NN)
        db_s[...] += dot((x_dt * w).astype(bf16), adj_low, NT)
        dc_s[...] += dot(g_ec, state_low, NT)
        last = ec[length - 1 : length]
        adj_o[...] = last * adj + dot(ct_s[...], g_ec, NN)
        edge = last * jnp.sum(state * adj, axis=0, keepdims=True)
        edge_s[...] += dot(edge.astype(bf16), pick, NN)
        cum = cum_s[step]
        start = pl.multiple_of(step * GROUP, GROUP)
        cumt = cumt_s[pl.ds(start, GROUP), :]
        kt = kt_s[...]
        mask = lax.broadcasted_iota(jnp.int32, (half, half), 0) <= lax.broadcasted_iota(
            jnp.int32, (half, half), 1
        )
        left_lane = lax.broadcasted_iota(jnp.int32, (half, LANES), 1) < HEAD_DIM
        lane_id = lax.broadcasted_iota(jnp.int32, (1, LANES), 1)
        pieces, col_sums = [], []
        row_sums = rows_s[...]
        w_tl, w_tr, w_br = wt_s[:half, :half], wt_s[:half, half:], wt_s[half:, half:]
        for pair in range(GROUP // 2):
            lanes = slice(pair * LANES, (pair + 1) * LANES)
            x_pair, g_pair = x_low[:, lanes], g_low[:, lanes]
            x_heads = [
                jnp.where(mine, x_pair[rows], jnp.zeros_like(x_pair[rows]))
                for rows in (slice(0, half), slice(half, length))
                for mine in (left_lane, jnp.logical_not(left_lane))
            ]
            p_top = dot(jnp.concatenate(x_heads[:2], axis=0), g_pair, NT)
            p_low = dot(jnp.concatenate(x_heads[2:], axis=0), g_pair[half:], NT)
            tops, lows = [], []
            for i in (2 * pair, 2 * pair + 1):
                col, row = cum[:, i : i + 1], cumt[i : i + 1, :]
                l_tl = jnp.exp2(jnp.where(mask, row[:, :half] - col[:half], -1e30))
                l_tr = jnp.exp2(row[:, half:] - col[:half])
                l_br = jnp.exp2(jnp.where(mask, row[:, half:] - col[half:], -1e30))
                lk_tl, lk_tr, lk_br = (
                    l_tl * kt[:half, :half],
                    l_tr * kt[:half, half:],
                    l_br * kt[half:, half:],
                )
                tops.append(jnp.concatenate([lk_tl.astype(bf16), lk_tr.astype(bf16)], axis=1))
                lows.append(lk_br.astype(bf16))
                of_head = slice((i % 2) * half, (i % 2 + 1) * half)
                p_tl, p_tr, p_br = p_top[of_head, :half], p_top[of_head, half:], p_low[of_head]
                w_tl, w_tr, w_br = w_tl + l_tl * p_tl, w_tr + l_tr * p_tr, w_br + l_br * p_br
                z_tl, z_tr, z_br = lk_tl * p_tl, lk_tr * p_tr, lk_br * p_br
                sums = jnp.concatenate(
                    [
                        jnp.sum(z_tl + z_tr, axis=1, keepdims=True),
                        jnp.sum(z_br, axis=1, keepdims=True),
                    ],
                    axis=0,
                )
                row_sums = row_sums + jnp.where(lane_id == start + i, sums, 0.0)
                col_sums.append(
                    jnp.concatenate(
                        [
                            jnp.sum(z_tl, axis=0, keepdims=True),
                            jnp.sum(z_tr + z_br, axis=0, keepdims=True),
                        ],
                        axis=1,
                    )
                )
            tops = dot(jnp.concatenate(tops, axis=0), g_pair, NN)
            lows = dot(jnp.concatenate(lows, axis=0), g_pair[half:], NN)
            pieces.append(
                jnp.concatenate(
                    [jnp.where(left_lane, both[:half], both[half:]) for both in (tops, lows)],
                    axis=0,
                )
            )
        wt_s[:half, :half] = w_tl
        wt_s[:half, half:] = w_tr
        wt_s[half:, half:] = w_br
        rows_s[...] = row_sums
        cols_s[pl.ds(start, GROUP), :] = jnp.concatenate(col_sums, axis=0)
        mixed_grad = jnp.concatenate(pieces, axis=1) + from_adj
        products = [act * mixed_grad, x_dt * from_adj, grad_ssm * carried]
        picked = dot(jnp.concatenate([v.astype(bf16) for v in products], axis=0), pick, NN)
        direct_s[...] += picked[:length]
        fresh_s[...] += picked[length : 2 * length]
        carry_s[...] += picked[2 * length :]
        grad_pre = (dt * mixed_grad + skip[...] * grad_ssm) * slope_ref[...].astype(f32)
        next_o[...] = grad_pre[0:8]
        later = later_rows(grad_pre, next_in[...])
        grad_conv = conv_sum(taps[...], later)
        grad_conv = grad_conv.astype(bf16)
        gc_o[:, pl.ds(pl.multiple_of(step * WIDTH, WIDTH), WIDTH)] = grad_conv
        conv_in = cin[...].astype(f32)
        sums = [jnp.sum(conv_in * rows, axis=0, keepdims=True) for rows in later]
        sums += [jnp.sum(grad_pre, axis=0, keepdims=True), gain_grad, skip_grad]
        chan_o[...] = jnp.concatenate(sums + [jnp.zeros_like(skip_grad)], axis=0)
        acc_s[...] += dot(grad_gate, wg[...], NT) + dot(grad_conv, wc[...], NT)

    @pl.when(step == GROUPS)
    def _():
        wt = wt_s[...].astype(bf16)
        grad_b = db_s[...] + dot(wt, c_s[...], NN)
        grad_c = dc_s[...] + dot(wt, b_s[...], TN)
        grad_pre = jnp.concatenate([grad_b, grad_c], axis=1) * dsilu_s[...]
        next_bc_o[...] = grad_pre[0:8]
        tap_rows = taps_bc[...]
        later = later_rows(grad_pre, next_bc_in[...])
        grad_conv = conv_sum(tap_rows, later)
        conv_in = cin_bc[...].astype(f32)
        sums = [jnp.sum(conv_in * rows, axis=0, keepdims=True) for rows in later]
        sums += [jnp.sum(grad_pre, axis=0, keepdims=True)]
        chan_bc_o[...] = jnp.concatenate(sums + [jnp.zeros((3, BC), f32)], axis=0)
        dt = head_steps(step_ref[...], head_rows[...])
        rate = head_rows[1:2]
        ones = jnp.where(lower_mask(length, length), 1.0, 0.0).astype(f32)
        fresh = fresh_s[...]
        from_here = cols_s[...].T - rows_s[...] + carry_s[...]
        suffix = (
            dot(ones, from_here, TN, lax.Precision.HIGHEST)
            + dot(ones, fresh, NN, lax.Precision.HIGHEST)
            - fresh
            + edge_s[0:1]
        )
        decayed = rate * suffix
        grad_step = (direct_s[...] + decayed) * sigmoid(step_ref[...] + head_rows[0:1])
        head_o[...] = jnp.concatenate(
            [
                jnp.sum(grad_step, axis=0, keepdims=True),
                jnp.sum(dt * decayed, axis=0, keepdims=True),
                jnp.zeros((6, LANES), f32),
            ],
            axis=0,
        )
        low = jnp.concatenate([grad_conv.astype(bf16), grad_step.astype(bf16)], axis=1)
        gc_o[:, DI:] = low
        grad_normed = acc_s[...] + dot(low, wbc[...], NT)
        h = chosen(flag[0, 0], own_ref, other_ref)
        scale = lax.rsqrt(jnp.mean(h * h, axis=1, keepdims=True) + EPS)
        ngrad_o[...] = jnp.sum(grad_normed * h * scale, axis=0, keepdims=True)
        weighted = grad_normed * ngain[...]
        mean = jnp.mean(h * weighted, axis=1, keepdims=True)
        grad_in = gout_ref[...].astype(f32) + scale * weighted - h * (scale * scale * scale * mean)
        gin_o[...] = grad_in
        gin_low_o[...] = grad_in.astype(bf16)


def spread_table():
    table = np.zeros((2 * LANES, DI), np.float32)
    for head in range(HEADS):
        table[head, head * HEAD_DIM : (head + 1) * HEAD_DIM] = 1.0
        table[LANES + head, head * HEAD_DIM : (head + 1) * HEAD_DIM] = 1.0
    return table


def whole(shape):
    return pl.BlockSpec(shape, lambda i: (0,) * len(shape))


def by_group(rows, width=WIDTH, skip=0):
    return pl.BlockSpec((rows, width), lambda i: (0, jnp.minimum(i, GROUPS - 1) + skip))


def tail_of(rows, width, at):
    return pl.BlockSpec((rows, width), lambda i: (0, at // width))


def gather_table():
    table = np.zeros((GROUPS, WIDTH, LANES), np.float32)
    for group in range(GROUPS):
        for column in range(WIDTH):
            table[group, column, group * GROUP + column // HEAD_DIM] = 1.0
    return table.reshape(-1, LANES)


FLAGS = pl.BlockSpec(memory_space=pltpu.SMEM)


def fwd_call(flag, own, other, params, weights, state, tail, tail_bc):
    length = own.shape[0]
    win, wo = weights
    in_specs = [
        FLAGS, whole((length, D)), whole((length, D)), whole((1, D)), by_group(D), by_group(D, WIDTH, GROUPS), tail_of(D, TAIL, 2 * DI),
        pl.BlockSpec((WIDTH, D), lambda i: (jnp.minimum(i, GROUPS - 1), 0)),
        by_group(8), tail_of(8, BC, DI), whole((8, LANES)), by_group(1), by_group(1),
        by_group(2 * LANES), by_group(16), whole((16, BC)), by_group(STATE),
    ]
    out = [
        ((length, D), bf16, whole((length, D))),
        ((length, DI), bf16, by_group(length)),
        ((length, DI), bf16, by_group(length)),
        ((length, DI), bf16, by_group(length)),
        ((length, BC), bf16, whole((length, BC))),
        ((length, LANES), f32, whole((length, LANES))),
        ((length, DI), bf16, by_group(length)),
        ((length, DI), bf16, by_group(length)),
        ((length, DI), bf16, by_group(length)),
        ((STATE, DI), f32, by_group(STATE)),
        ((length, DI), bf16, whole((length, DI))),
        ((length, LANES), f32, whole((length, LANES))),
        ((length, D), f32, whole((length, D))),
        ((length, D), bf16, whole((length, D))),
        ((16, DI), bf16, by_group(16)),
        ((16, BC), bf16, whole((16, BC))),
    ]
    scratch = [
        ((length, DI), f32), ((length, LANES), f32), ((length, length), f32),
        ((length, STATE), bf16), ((STATE, length), bf16), ((3 * length, 2 * LANES), bf16),
        ((GROUPS, length, GROUP), f32),
        ((LANES, length), f32),
    ]
    return pl.pallas_call(
        fwd_body,
        grid=(GROUPS + 1,),
        in_specs=in_specs,
        out_specs=[spec for _, _, spec in out],
        out_shape=[jax.ShapeDtypeStruct(shape, dtype) for shape, dtype, _ in out],
        scratch_shapes=[pltpu.VMEM(shape, dtype) for shape, dtype in scratch],
        compiler_params=pltpu.CompilerParams(
            dimension_semantics=("arbitrary",), vmem_limit_bytes=VMEM_LIMIT
        ),
        cost_estimate=pl.CostEstimate(flops=12 * 10**9, bytes_accessed=45 * 10**6, transcendentals=5 * 10**6),
        name="layer_forward",
    )(
        flag, own, other, params["norm_gain"], win, win, win, wo, params["taps"], params["taps"],
        params["heads"], params["skip"], params["gate_gain"], params["spread"], tail, tail_bc, state,
    )


def bwd_call(flag, own_grad, other_grad, kept, params, weights, adj, ahead, ahead_bc):
    length = own_grad.shape[0]
    win, wo = weights
    rows_of_wo = pl.BlockSpec((WIDTH, D), lambda i: (jnp.minimum(i, GROUPS - 1), 0))
    pick = pl.BlockSpec((WIDTH, LANES), lambda i: (jnp.minimum(i, GROUPS - 1), 0))
    in_specs = [
        FLAGS, whole((length, D)), whole((length, D)), whole((length, D)), whole((length, D)),
        whole((1, D)), whole((length, D)),
        whole((length, LANES)), rows_of_wo, by_group(D), by_group(D, WIDTH, GROUPS), tail_of(D, TAIL, 2 * DI),
        by_group(8), tail_of(8, BC, DI), whole((8, LANES)), by_group(1), by_group(1),
        by_group(2 * LANES), pick, by_group(length), by_group(length), by_group(length),
        by_group(length), by_group(length), by_group(length), whole((length, BC)),
        whole((length, LANES)), whole((16, BC)),
        by_group(STATE), by_group(STATE), by_group(8), whole((8, BC)),
    ]
    out = [
        ((length, D), bf16, whole((length, D))),
        ((length, DI), bf16, by_group(length)),
        ((length, DI + TAIL), bf16, whole((length, DI + TAIL))),
        ((length, D), f32, whole((length, D))),
        ((length, D), bf16, whole((length, D))),
        ((STATE, DI), f32, by_group(STATE)),
        ((8, DI), f32, by_group(8)),
        ((8, BC), f32, whole((8, BC))),
        ((8, DI), f32, by_group(8)),
        ((8, BC), f32, whole((8, BC))),
        ((1, D), f32, whole((1, D))),
        ((8, LANES), f32, whole((8, LANES))),
    ]
    scratch = [
        ((length, D), f32), ((length, length), f32), ((length, length), f32),
        ((length, STATE), bf16), ((length, STATE), bf16), ((STATE, length), bf16),
        ((3 * length, 2 * LANES), bf16),
        ((GROUPS, length, GROUP), f32), ((LANES, length), f32), ((length, STATE), f32),
        ((length, STATE), f32), ((length, LANES), f32), ((LANES, length), f32),
        ((length, LANES), f32), ((length, LANES), f32), ((length, LANES), f32), ((1, LANES), f32),
        ((length, BC), f32), ((length, LANES), f32),
    ]
    return pl.pallas_call(
        bwd_body,
        grid=(GROUPS + 1,),
        in_specs=in_specs,
        out_specs=[spec for _, _, spec in out],
        out_shape=[jax.ShapeDtypeStruct(shape, dtype) for shape, dtype, _ in out],
        scratch_shapes=[pltpu.VMEM(shape, dtype) for shape, dtype in scratch],
        compiler_params=pltpu.CompilerParams(
            dimension_semantics=("arbitrary",), vmem_limit_bytes=VMEM_LIMIT
        ),
        cost_estimate=pl.CostEstimate(flops=25 * 10**9, bytes_accessed=55 * 10**6, transcendentals=8 * 10**6),
        name="layer_backward",
    )(
        flag, kept["own"], kept["other"], own_grad, other_grad, params["norm_gain"], kept["branch"], kept["r"], wo, win, win, win,
        params["taps"], params["taps"], params["heads"], params["skip"], params["gate_gain"],
        params["spread"], params["gather"], kept["silu"], kept["turned"], kept["u"], kept["act"],
        kept["slope"], kept["cin"], kept["cin_bc"], kept["step"], kept["tail_bc"], kept["state"], adj, ahead, ahead_bc,
    )


def xor_route(size, bit):
    return [(i, i ^ bit) for i in range(size)]


def bits_of(size):
    return [1 << b for b in range(size.bit_length() - 1)]


def gather_small(row):
    for axis in ("seq", "dp"):
        size, position = lax.axis_size(axis), lax.axis_index(axis)
        for bit in bits_of(size):
            other = lax.ppermute(row, axis, xor_route(size, bit))
            row = jnp.where(
                (position & bit) == 0,
                jnp.concatenate([row, other], axis=0),
                jnp.concatenate([other, row], axis=0),
            )
    return row


def exchanges():
    return [(axis, bit) for axis in ("dp", "seq") for bit in bits_of(lax.axis_size(axis))]


def exchange(value, axis, bit):
    return value + lax.ppermute(value, axis, xor_route(lax.axis_size(axis), bit))


def sum_small(value):
    for axis, bit in exchanges():
        value = exchange(value, axis, bit)
    return value


def direct_paths():
    return lax.axis_size("dp") == 4 and lax.axis_size("seq") == 4


RING = 8


def ring_place(position):
    return jnp.where(position < 4, position, 11 - position)


def ring_route(step):
    def device(position, core):
        y, z = (0, position) if position < 4 else (1, 7 - position)
        return (y * 2 + core) * 4 + z

    return [
        (device(p, core), device((p + step) % RING, core)) for p in range(RING) for core in range(2)
    ]


def around(value, step):
    return lax.ppermute(value, ("dp", "seq"), ring_route(step))


def across(value):
    return lax.ppermute(value, "dp", xor_route(4, 1))


def own_position():
    dp, z = lax.axis_index("dp"), lax.axis_index("seq")
    y = dp // 2
    return jnp.where(y == 0, z, 7 - z), dp % 2


def together(up, down):
    pairs = [lax.optimization_barrier(pair) for pair in zip(up, down)]
    return [a for a, _ in pairs], [b for _, b in pairs]


def gather_rows(shards):
    if not direct_paths():
        return [lax.all_gather(shard, ("dp", "seq"), axis=0, tiled=True) for shard in shards]
    position, core = own_position()
    held = [jnp.zeros((16,) + shard.shape, shard.dtype) for shard in shards]

    def place(held, pieces, offset, start=0):
        at = ring_place((position + offset) % RING)
        at = (at // 4) * 8 + at % 4
        others = [across(piece) for piece in pieces]
        for of_core, values in ((core, pieces), (1 - core, others)):
            held = [
                lax.dynamic_update_slice(whole, value[None], (at + of_core * 4, start * rows, 0))
                for whole, value, rows in zip(held, values, halves_of)
            ]
        return held

    halves_of = [shard.shape[0] // 2 for shard in shards]
    up, down = shards, shards
    held = place(held, shards, 0)
    for hop in range(1, 4):
        up, down = [around(v, 1) for v in up], [around(v, -1) for v in down]
        up, down = together(up, down)
        held = place(place(held, up, -hop), down, hop)
    up = [around(v[:rows], 1) for v, rows in zip(up, halves_of)]
    down = [around(v[rows:], -1) for v, rows in zip(down, halves_of)]
    held = place(place(held, up, 4), down, 4, 1)
    return [whole.reshape((-1,) + whole.shape[2:]) for whole in held]


def reduce_rows(chips, small, early):
    position, _ = own_position()
    hops = exchanges()

    def term(chip, offset):
        at = ring_place((position + offset) % RING)
        return lax.dynamic_index_in_dim(chip, at, 0, keepdims=False)

    half = [chip.shape[1] // 2 for chip in chips]
    up = [around(term(chip, 4)[:rows], 1) for chip, rows in zip(chips, half)]
    down = [around(term(chip, -4)[rows:], -1) for chip, rows in zip(chips, half)]
    small = exchange(small, *hops[0])
    up, down = together(up, down)
    up[0], small, early = lax.optimization_barrier((up[0], small, early))
    up = [jnp.pad(v, ((0, rows), (0, 0))) for v, rows in zip(up, half)]
    down = [jnp.pad(v, ((rows, 0), (0, 0))) for v, rows in zip(down, half)]
    for hop, offset in enumerate((3, 2, 1), 1):
        up = [
            around((term(chip, offset).astype(f32) + v.astype(f32)).astype(bf16), 1)
            for chip, v in zip(chips, up)
        ]
        down = [
            around((term(chip, -offset).astype(f32) + v.astype(f32)).astype(bf16), -1)
            for chip, v in zip(chips, down)
        ]
        small = exchange(small, *hops[hop])
        up, down = together(up, down)
        up[0], small = lax.optimization_barrier((up[0], small))
    sums = [
        term(chip, 0).astype(f32) + a.astype(f32) + b.astype(f32)
        for chip, a, b in zip(chips, up, down)
    ]
    return sums, small, early


def weight_grads(pairs, small, early, ready):
    def term(columns, right):
        return jnp.einsum("td,te->de", columns, right, preferred_element_type=f32)

    if not direct_paths():
        sums = [
            lax.optimization_barrier(
                lax.psum_scatter(term(left, right), ("dp", "seq"), scatter_dimension=0, tiled=True)
            )
            for left, right in pairs
        ]
        return sums, sum_small(small), early, ready
    core = lax.axis_index("dp") % 2

    def owned(left, right, which):
        quarter = left.shape[1] // 4
        parts = [left[:, i * quarter : (i + 1) * quarter] for i in range(4)]
        chosen = jnp.concatenate(
            [jnp.where(which == 0, parts[0], parts[1]), jnp.where(which == 0, parts[2], parts[3])],
            axis=1,
        )
        return term(chosen, right).astype(bf16).reshape(RING, quarter // 4, right.shape[1])

    arrived = [across(owned(left, right, 1 - core)) for left, right in pairs]
    left, ready = lax.optimization_barrier((pairs[0][0], ready))
    chips = [
        (owned(left, right, core).astype(f32) + other.astype(f32)).astype(bf16)
        for (_, right), other in zip(pairs, arrived)
    ]
    return *reduce_rows(chips, small, early), ready


def turn(value, shift, parts):
    size = lax.axis_size("seq")
    route = [(i, i - i % parts + (i % parts + shift) % parts) for i in range(size)]
    return lax.ppermute(value, "seq", route)


def in_order(arrived):
    parts = len(arrived)
    rank = lax.axis_index("seq") % parts
    arrived = jnp.stack(arrived)
    return [
        lax.dynamic_index_in_dim(arrived, (rank - k) % parts, 0, keepdims=False)
        for k in range(parts)
    ]


def token_blocks(tokens):
    parts, length = tokens.shape[0], tokens.shape[1]
    rank, section = lax.axis_index("seq") % parts, lax.axis_index("section")
    half = length // 2
    arrived = []
    for shift in range(1, parts):
        at = ((rank + shift) % parts, section * half, 0)
        piece = lax.dynamic_slice(tokens, at, (1, half, tokens.shape[2]))[0]
        arrived.append(turn(piece, shift, parts))
    handed = lax.ppermute(jnp.concatenate(arrived, axis=0), "section", [(1, 0)])
    blocks = [lax.dynamic_index_in_dim(tokens, rank, 0, keepdims=False)]
    for i, low in enumerate(arrived):
        blocks.append(jnp.concatenate([low, handed[i * half : (i + 1) * half]], axis=0))
    return in_order(blocks)


def cotangent_blocks(rows):
    parts = rows.shape[0]
    size = lax.axis_size("seq")
    rank = lax.axis_index("seq") % parts
    arrived = [lax.dynamic_index_in_dim(rows, rank, 0, keepdims=False)]
    for shift in range(1, parts):
        piece = lax.dynamic_index_in_dim(rows, (rank + shift) % parts, 0, keepdims=False)
        route = [
            (size + i, size + i - i % parts + (i % parts + shift) % parts) for i in range(size)
        ]
        arrived.append(lax.ppermute(piece, ("section", "seq"), route))
    return in_order(arrived)


def to_pieces(blocks, sent_type):
    parts = len(blocks)
    rank = lax.axis_index("seq") % parts
    stacked = jnp.stack(blocks)
    held = stacked
    pieces = []
    for shift in range(parts):
        piece = lax.dynamic_index_in_dim(stacked, (rank + shift) % parts, 0, keepdims=False)
        if shift:
            piece = turn(piece.astype(sent_type), shift, parts)
        pieces.append(piece)
    return stacked, pieces


def laid_out(held, pieces):
    parts = len(pieces)
    rank = lax.axis_index("seq") % parts
    for shift, piece in enumerate(pieces):
        piece = piece.astype(held.dtype)
        held = lax.dynamic_update_slice(held, piece[None], ((rank - shift) % parts, 0, 0))
    return held


KEPT = (
    "normed", "cin", "act", "slope", "cin_bc", "step", "silu", "turned", "u", "state_out", "gout", "r",
    "branch", "out",
    "tail_out", "tail_bc_out",
)
SKEW = 2


def flags(first, grad):
    return jnp.stack([jnp.where(first, 1, 0), jnp.asarray(grad, jnp.int32)]).astype(jnp.int32)[None]


def shards(
    tokens, cotangent, in_proj, out_proj, conv_weight, conv_bias, norm_gain, gate_gain, step_bias,
    log_decay, skip_gain,
):
    first = lax.axis_index("section") == 0
    seq = lax.axis_size("seq")
    parts, length = tokens.shape[0], tokens.shape[1]
    owned = in_proj.shape[1]
    tokens_in = token_blocks(tokens)

    shard = jnp.pad(in_proj[0], ((0, 0), (0, TAIL - BC - HEADS)))
    weights = (
        lax.all_gather(shard, ("dp", "seq"), axis=0, tiled=True),
        gather_rows([out_proj[0]])[0],
    )

    sizes = [CONV * conv_bias.shape[1], conv_bias.shape[1], norm_gain.shape[1], gate_gain.shape[1]]
    packed = jnp.concatenate([conv_weight[0].reshape(-1), conv_bias[0], norm_gain[0], gate_gain[0]])
    packed = gather_small(packed[None]).astype(f32)
    ends = np.cumsum(sizes)
    taps, shift, gain_in, gain_gate = (
        packed[:, end - size : end] for end, size in zip(ends, sizes)
    )
    taps = jnp.swapaxes(taps.reshape(-1, CONV, conv_bias.shape[1]), 0, 1).reshape(CONV, -1)
    taps = jnp.concatenate([taps, shift.reshape(1, -1), jnp.zeros((3, taps.shape[1]), f32)], axis=0)
    lanes = ((0, 0), (0, LANES - HEADS))
    params = {
        "norm_gain": gain_in.reshape(1, -1),
        "gate_gain": gain_gate.reshape(1, -1),
        "taps": taps,
        "heads": jnp.pad(
            jnp.concatenate([step_bias, -jnp.exp(log_decay), jnp.zeros((6, HEADS), f32)], axis=0),
            lanes,
        ),
        "skip": jnp.repeat(skip_gain, HEAD_DIM, axis=1),
        "spread": jnp.asarray(spread_table(), bf16),
        "gather": jnp.asarray(gather_table(), bf16),
    }

    ticks = parts + SKEW
    hops = seq // parts

    def forward(start):
        kept, received = [], [jnp.zeros((length, D), bf16)] * SKEW
        carry = start
        for tick in range(ticks):
            if tick == SKEW:
                carry = tuple(jnp.where(first, now, at) for now, at in zip(carry, start))
            own, other = tokens_in[min(tick, parts - 1)], received[tick]
            values = dict(zip(KEPT, fwd_call(flags(first, 0), own, other, params, weights, *carry)))
            values.update(own=own, other=other, state=carry[0], tail=carry[1], tail_bc=carry[2])
            carry = (values["state_out"], values["tail_out"], values["tail_bc_out"])
            kept.append(values)
            if tick < parts:
                received.append(lax.ppermute(values["out"], "section", [(0, 1)]))
        return kept

    def backward(kept, start, before_last=None):
        early = None
        zeros = tuple(jnp.zeros_like(part) for part in start)
        carry = tuple(jnp.where(first, zero, at) for zero, at in zip(zeros, start))
        grads, received = [None] * ticks, [jnp.zeros((length, D), bf16)] * SKEW
        for tick in range(ticks):
            if tick == SKEW and hops > 1:
                carry = tuple(jnp.where(first, at, now) for now, at in zip(carry, start))
            if tick == parts:
                carry = tuple(jnp.where(first, now, zero) for now, zero in zip(carry, zeros))
            from_loss = loss_in[max(parts - 1 - tick, 0)]
            late = jnp.int32(2 if tick >= parts else 1)
            if before_last is not None and tick == ticks - 1:
                early = before_last(grads, received[tick])
                from_loss, early = lax.optimization_barrier((from_loss, early))
            at = ticks - 1 - tick
            names = (
                "out", "gate", "conv", "in", "in_low", "adj", "next", "next_bc", "chan", "chan_bc",
                "norm", "head",
            )
            values = dict(
                zip(
                    names,
                    bwd_call(
                        flags(first, jnp.where(first, 0, late)),
                        from_loss,
                        received[tick],
                        kept[at],
                        params,
                        weights,
                        *carry,
                    ),
                )
            )
            carry = (values["adj"], values["next"], values["next_bc"])
            grads[at] = values
            if tick < parts:
                sent, received[-1] = lax.optimization_barrier((values["in_low"], received[-1]))
                received.append(lax.ppermute(sent, "section", [(1, 0)]))
        return grads, early

    start = (jnp.zeros((STATE, DI), f32), jnp.zeros((16, DI), bf16), jnp.zeros((16, BC), bf16))
    if hops > 1:

        def onward(_, start):
            kept = forward(start)
            ends = (
                tuple(kept[parts - 1][name] for name in ("state_out", "tail_out", "tail_bc_out")),
                tuple(kept[ticks - 1][name] for name in ("state_out", "tail_out", "tail_bc_out")),
            )
            route = [(i, i + parts) for i in range(seq - parts)]
            return tuple(
                lax.ppermute(jnp.where(first, a, b), "seq", route) for a, b in zip(*ends)
            )

        start = lax.fori_loop(0, hops - 1, onward, start)
    kept = forward(start)
    cotangent, _ = lax.optimization_barrier((cotangent, kept[0]["r"]))
    loss_in = cotangent_blocks(cotangent)
    activations = laid_out(
        *to_pieces(
            [jnp.where(first, kept[k]["out"], kept[k + SKEW]["out"]) for k in range(parts)], bf16
        )
    )[None]

    start = (jnp.zeros((STATE, DI), f32), jnp.zeros((8, DI), f32), jnp.zeros((8, BC), f32))
    if hops > 1:

        def back(_, start):
            grads, _ = backward(kept, start)
            ends = (
                tuple(grads[0][name] for name in ("adj", "next", "next_bc")),
                tuple(grads[SKEW][name] for name in ("adj", "next", "next_bc")),
            )
            route = [(i, i - parts) for i in range(parts, seq)]
            return tuple(
                lax.ppermute(jnp.where(first, a, b), "seq", route) for a, b in zip(*ends)
            )

        start = lax.fori_loop(0, hops - 1, back, start)
    def select(values, name):
        return jnp.concatenate(
            [jnp.where(first, values[k][name], values[k + SKEW][name]) for k in range(parts)], axis=0
        )

    def out_term(grads, received):
        branch_grads = [jnp.where(first, received, loss_in[0])] + [
            jnp.where(first, grads[k]["out"], grads[k + SKEW]["out"]) for k in range(1, parts)
        ]
        return jnp.einsum(
            "td,te->de",
            select(kept, "gout"),
            jnp.concatenate(branch_grads, axis=0),
            preferred_element_type=f32,
        ).astype(bf16)

    grads, term = backward(kept, start, out_term)
    grad_out_proj = lax.psum_scatter(
        term, ("dp", "seq"), scatter_dimension=0, tiled=True
    ).astype(f32)
    normed = select(kept, "normed")
    def total(name):
        return sum(values[name] for values in grads)

    channels = jnp.concatenate([total("chan"), total("chan_bc")], axis=1)
    head = total("head")
    last_row = jnp.concatenate([total("norm"), head[0:1], head[1:2]], axis=1)
    fill = channels.shape[1] - last_row.shape[1]
    small = (channels + jnp.pad(last_row, ((7, 0), (0, fill))))
    held, pieces = to_pieces(
        [jnp.where(first, grads[k]["in"], grads[k + SKEW]["in"]) for k in range(parts)], bf16
    )
    near = [pieces[1], pieces[-1]]
    (grad_gate, grad_conv), small, grad_out_proj, near = weight_grads(
        [(normed, select(grads, "gate")), (normed, select(grads, "conv"))],
        small,
        grad_out_proj,
        near,
    )
    pieces[1], pieces[-1] = near
    pieces, grad_gate = lax.optimization_barrier((pieces, grad_gate))
    input_grads = laid_out(held, pieces)[None]
    grad_in_proj = jnp.concatenate([grad_gate, grad_conv[:, : DI + BC + HEADS]], axis=1)[None]

    place = lax.axis_index("dp") * seq + lax.axis_index("seq")

    def mine(flat, width):
        return lax.dynamic_slice_in_dim(flat, place * width, width, axis=flat.ndim - 1)

    width = conv_bias.shape[1]
    return (
        activations,
        input_grads,
        grad_in_proj,
        grad_out_proj[None],
        mine(small[:CONV], width)[None],
        mine(small[CONV], width)[None],
        mine(small[7, :D], owned)[None],
        mine(small[5, :DI], gate_gain.shape[1])[None],
        small[7:8, D : D + HEADS],
        small[7:8, D + LANES : D + LANES + HEADS],
        small[6, :DI].reshape(HEADS, HEAD_DIM).sum(axis=1)[None],
    )


def solution(mesh):
    placed = (
        P("dp", "seq", None),
        P("dp", "seq", None),
        P("section", ("dp", "seq"), None),
        P("section", ("dp", "seq"), None),
        P("section", None, ("dp", "seq")),
        P("section", ("dp", "seq")),
        P("section", ("dp", "seq")),
        P("section", ("dp", "seq")),
        P("section", None),
        P("section", None),
        P("section", None),
    )
    return jax.shard_map(
        shards,
        mesh=mesh,
        in_specs=placed,
        out_specs=(
            P("section", "dp", "seq", None),
            P("section", "dp", "seq", None),
        )
        + placed[2:],
        check_vma=False,
    )
```

```python
import jax
import jax.numpy as jnp
import numpy as np
from jax import lax
from jax.experimental import pallas as pl
from jax.experimental.pallas import tpu as pltpu
from jax.sharding import PartitionSpec as P

D = 1536
HEADS = 48
HEAD_DIM = 64
STATE = 128
CONV = 4
DI = 3072
BC = 2 * STATE
TAIL = BC + 128
GROUP = 8
WIDTH = GROUP * HEAD_DIM
GROUPS = HEADS // GROUP
LANES = 128
EPS = 1e-05
LOG2_E = 1.4426950408889634
f32 = jnp.float32
bf16 = jnp.bfloat16
VMEM_LIMIT = 56 * 2**20
NN = ((1,), (0,))
NT = ((1,), (1,))
TN = ((0,), (0,))


def dot(a, b, dims, precision=None):
    return lax.dot_general(a, b, (dims, ((), ())), preferred_element_type=f32, precision=precision)


def halves(value):
    top = value.astype(bf16)
    rest = (value - top.astype(f32)).astype(bf16)
    return jnp.concatenate([top, rest], axis=1)


def lower_mask(rows, cols):
    return lax.broadcasted_iota(jnp.int32, (rows, cols), 0) >= lax.broadcasted_iota(
        jnp.int32, (rows, cols), 1
    )


def sigmoid(v):
    return 0.5 * jnp.tanh(0.5 * v) + 0.5


def head_steps(step_raw, head_rows):
    biased = step_raw + head_rows[0:1]
    return jnp.maximum(biased, 0.0) + jnp.log1p(jnp.exp(-jnp.abs(biased)))


def running_sum(value):
    length = value.shape[0]
    ones = jnp.where(lower_mask(length, length), 1.0, 0.0).astype(f32)
    return dot(ones, value, NN, lax.Precision.HIGHEST)


def earlier_rows(tail, rows):
    joined = jnp.concatenate([tail[8:16].astype(f32), rows], axis=0)
    shifted = [pltpu.roll(joined, shift, 0)[8:] for shift in range(CONV - 1, 0, -1)]
    return shifted + [rows]


def later_rows(rows, head):
    length = rows.shape[0]
    joined = jnp.concatenate([rows, head], axis=0)
    shifted = [pltpu.roll(joined, length + 8 - shift, 0)[:length] for shift in range(CONV - 1, 0, -1)]
    return shifted + [rows]


def conv_sum(taps, shifted, start=0.0):
    for j in range(CONV):
        start = start + shifted[j] * taps[j : j + 1]
    return start


def chosen(flag, own, other):
    return jnp.where(flag == 1, own[...].astype(f32), other[...].astype(f32))


def chosen_grad(flag, own, other):
    other_or_zero = jnp.where(flag == 0, other[...].astype(f32), 0.0)
    return jnp.where(flag == 1, own[...].astype(f32), other_or_zero)


def fwd_body(
    flag, own_ref, other_ref, ngain, wg, wc, wbc, wo, taps, taps_bc, head_rows, skip, gate_gain, spread, tail_in,
    tail_bc_in, state_in,
    normed_o, cin_o, act_o, slope_o, cin_bc_o, step_o, silu_o, turned_o, u_o, state_o, gout_o, r_o, branch_o, out_o,
    tail_o, tail_bc_o,
    u_s, ssq_s, k_s, c_s, bt_s, sp_s, cum_s, cumt_s,
):
    step = pl.program_id(0)
    length = own_ref.shape[0]
    half = length // 2
    valid = flag[0, 2] == 1

    @pl.when(jnp.logical_and(step == 0, valid))
    def _():
        h = chosen(flag[0, 0], own_ref, other_ref)
        scale = lax.rsqrt(jnp.mean(h * h, axis=1, keepdims=True) + EPS)
        normed = (h * scale * ngain[...]).astype(bf16)
        normed_o[...] = normed
        projected = dot(normed, wbc[...], NN)
        step_raw = projected[:, BC:]
        step_o[...] = step_raw
        conv_in = projected[:, :BC].astype(bf16)
        cin_bc_o[...] = conv_in
        tail_bc_o[...] = conv_in[length - 16 :]
        tap_rows = taps_bc[...]
        shifted = earlier_rows(tail_bc_in[...], conv_in.astype(f32))
        pre = conv_sum(tap_rows, shifted, tap_rows[CONV : CONV + 1])
        act = (pre * sigmoid(pre)).astype(bf16)
        b_rows, c_rows = act[:, :STATE], act[:, STATE:]
        c_s[...] = c_rows
        bt_s[...] = b_rows.astype(f32).T.astype(bf16)
        k_s[...] = dot(c_rows, b_rows, NT)
        dt = head_steps(step_raw, head_rows[...])
        cum = running_sum(dt * head_rows[1:2])
        total = cum[length - 1 : length]
        sp_s[0:length] = halves(dt)
        sp_s[length : 2 * length] = halves(jnp.exp(cum))
        sp_s[2 * length :] = halves(dt * jnp.exp(total - cum))
        for g in range(GROUPS):
            cum_s[g] = cum[:, g * GROUP : (g + 1) * GROUP] * LOG2_E
        cumt_s[...] = (cum * LOG2_E).T
        ssq_s[...] = jnp.zeros_like(ssq_s)
        branch_o[...] = jnp.zeros_like(branch_o)

    @pl.when(jnp.logical_and(step < GROUPS, valid))
    def _():
        normed = normed_o[...]
        gate = dot(normed, wg[...], NN)
        conv_in = dot(normed, wc[...], NN).astype(bf16)
        cin_o[...] = conv_in
        tail_o[...] = conv_in[length - 16 :]
        tap_rows = taps[...]
        shifted = earlier_rows(tail_in[...], conv_in.astype(f32))
        pre = conv_sum(tap_rows, shifted, tap_rows[CONV : CONV + 1])
        sig = sigmoid(pre)
        act = pre * sig
        slope_o[...] = (sig + act * (1.0 - sig)).astype(bf16)
        act_o[...] = act.astype(bf16)
        act = act_o[...].astype(f32)
        where = spread[...]
        spreads = dot(sp_s[...], where, NN)
        x_dt = (act * spreads[:length]).astype(bf16)
        x_w = (act * spreads[2 * length :]).astype(bf16)
        ec = spreads[length : 2 * length]
        state = state_in[...]
        state_o[...] = ec[length - 1 : length] * state + dot(bt_s[...], x_w, NN)
        carried = dot(c_s[...], state.astype(bf16), NN) * ec
        cum = cum_s[step]
        cumt = cumt_s[pl.ds(pl.multiple_of(step * GROUP, GROUP), GROUP), :]
        k = k_s[...]
        mask = lower_mask(half, half)
        left_lane = lax.broadcasted_iota(jnp.int32, (half, LANES), 1) < HEAD_DIM
        pieces = []
        for pair in range(GROUP // 2):
            x_pair = x_dt[:, pair * LANES : (pair + 1) * LANES]
            tops, lows = [], []
            for i in (2 * pair, 2 * pair + 1):
                col, row = cum[:, i : i + 1], cumt[i : i + 1, :]
                top = jnp.exp2(jnp.where(mask, col[:half] - row[:, :half], -1e30))
                low_left = jnp.exp2(col[half:] - row[:, :half])
                low_right = jnp.exp2(jnp.where(mask, col[half:] - row[:, half:], -1e30))
                tops.append((top * k[:half, :half]).astype(bf16))
                low = jnp.concatenate(
                    [
                        (low_left * k[half:, :half]).astype(bf16),
                        (low_right * k[half:, half:]).astype(bf16),
                    ],
                    axis=1,
                )
                lows.append(low)
            tops = dot(jnp.concatenate(tops, axis=0), x_pair[:half], NN)
            lows = dot(jnp.concatenate(lows, axis=0), x_pair, NN)
            pieces.append(
                jnp.concatenate(
                    [jnp.where(left_lane, both[:half], both[half:]) for both in (tops, lows)],
                    axis=0,
                )
            )
        within = jnp.concatenate(pieces, axis=1)
        ssm = within + carried + skip[...] * act
        sig = sigmoid(gate)
        silu = gate * sig
        silu_o[...] = silu.astype(bf16)
        turned_o[...] = (ssm * (sig + silu * (1.0 - sig))).astype(bf16)
        u = ssm * silu
        u_o[...] = u.astype(bf16)
        gained = u * gate_gain[...]
        u_s[:, pl.ds(pl.multiple_of(step * WIDTH, WIDTH), WIDTH)] = gained
        ssq_s[...] += jnp.sum(u * u, axis=1, keepdims=True)
        branch_o[...] += dot(gained.astype(bf16), wo[...], NN)

    @pl.when(jnp.logical_and(step == GROUPS, valid))
    def _():
        r = lax.rsqrt(ssq_s[...] * (1.0 / DI) + EPS)
        r_o[...] = r
        r = r[:, 0:1]
        for g in range(GROUPS):
            cols = slice(g * WIDTH, (g + 1) * WIDTH)
            gout_o[:, cols] = (u_s[:, cols] * r).astype(bf16)
        branch = branch_o[...] * r
        branch_o[...] = branch
        out_o[...] = (chosen(flag[0, 0], own_ref, other_ref) + branch).astype(bf16)


def bwd_body(
    flag, own_ref, other_ref, own_grad, other_grad, ngain, branch, r_ref, wo, wg, wc, wbc, taps, taps_bc, head_rows, skip,
    gate_gain, spread, gather, silu_ref, turned_ref, u_ref, act_ref, slope_ref, cin, cin_bc, step_ref,
    tail_bc_in,
    state_in, adj_in, next_in, next_bc_in,
    gout_ref, gg_o, gc_o, gin_o, gin_low_o, adj_o, next_o, next_bc_o, chan_o, chan_bc_o, ngrad_o,
    head_o,
    acc_s, kt_s, wt_s, b_s, c_s, ct_s, sp_s, cum_s, cumt_s, db_s, dc_s, rows_s, cols_s,
    direct_s, fresh_s, carry_s, edge_s, dsilu_s, q_s,
):
    step = pl.program_id(0)
    length = own_ref.shape[0]
    half = length // 2
    valid = flag[0, 2] == 1

    def carried_in(ref):
        return jnp.where(flag[0, 3] == 1, ref[...], 0.0)

    @pl.when(jnp.logical_not(valid))
    def _():
        for ref in (chan_o, chan_bc_o, ngrad_o, head_o):
            ref[...] = jnp.zeros_like(ref)

    @pl.when(jnp.logical_and(step == 0, valid))
    def _():
        gout_ref[...] = chosen_grad(flag[0, 1], own_grad, other_grad).astype(bf16)
        tap_rows = taps_bc[...]
        shifted = earlier_rows(tail_bc_in[...], cin_bc[...].astype(f32))
        pre = conv_sum(tap_rows, shifted, tap_rows[CONV : CONV + 1])
        sig = sigmoid(pre)
        dsilu_s[...] = sig * (1.0 + pre * (1.0 - sig))
        act = (pre * sig).astype(bf16)
        b_rows, c_rows = act[:, :STATE], act[:, STATE:]
        b_s[...] = b_rows
        c_s[...] = c_rows
        ct_s[...] = c_rows.astype(f32).T.astype(bf16)
        kt_s[...] = dot(b_rows, c_rows, NT)
        dt = head_steps(step_ref[...], head_rows[...])
        cum = running_sum(dt * head_rows[1:2])
        total = cum[length - 1 : length]
        sp_s[0:length] = halves(dt)
        sp_s[length : 2 * length] = halves(jnp.exp(cum))
        sp_s[2 * length :] = halves(jnp.exp(total - cum))
        for g in range(GROUPS):
            cum_s[g] = cum[:, g * GROUP : (g + 1) * GROUP] * LOG2_E
        cumt_s[...] = (cum * LOG2_E).T
        for ref in (acc_s, wt_s, db_s, dc_s, rows_s, cols_s, direct_s, fresh_s, carry_s, edge_s):
            ref[...] = jnp.zeros_like(ref)
        rowdot = jnp.sum(branch[...] * gout_ref[...].astype(f32), axis=1, keepdims=True)
        q_s[...] = jnp.broadcast_to(rowdot * (1.0 / DI), q_s.shape) * r_ref[...] * r_ref[...]

    @pl.when(jnp.logical_and(step < GROUPS, valid))
    def _():
        grad_gated = dot(gout_ref[...], wo[...], NT)
        u = u_ref[...].astype(f32)
        scaled = r_ref[:, 0:1] * grad_gated
        gain_grad = jnp.sum(scaled * u, axis=0, keepdims=True)
        grad_u = scaled * gate_gain[...] - u * q_s[:, 0:1]
        grad_ssm = grad_u * silu_ref[...].astype(f32)
        grad_gate = (grad_u * turned_ref[...].astype(f32)).astype(bf16)
        gg_o[...] = grad_gate
        act = act_ref[...].astype(f32)
        where, pick = spread[...], gather[...]
        spreads = dot(sp_s[...], where, NN)
        dt, ec, w = (spreads[i * length : (i + 1) * length] for i in range(3))
        skip_grad = jnp.sum(act * grad_ssm, axis=0, keepdims=True)
        x_dt = act * dt
        x_low, g_low = x_dt.astype(bf16), grad_ssm.astype(bf16)
        g_ec = (grad_ssm * ec).astype(bf16)
        state, adj = state_in[...], carried_in(adj_in)
        state_low, adj_low = state.astype(bf16), adj.astype(bf16)
        from_adj = w * dot(b_s[...], adj_low, NN)
        carried = ec * dot(c_s[...], state_low, NN)
        db_s[...] += dot((x_dt * w).astype(bf16), adj_low, NT)
        dc_s[...] += dot(g_ec, state_low, NT)
        last = ec[length - 1 : length]
        adj_o[...] = last * adj + dot(ct_s[...], g_ec, NN)
        edge = last * jnp.sum(state * adj, axis=0, keepdims=True)
        edge_s[...] += dot(edge.astype(bf16), pick, NN)
        cum = cum_s[step]
        start = pl.multiple_of(step * GROUP, GROUP)
        cumt = cumt_s[pl.ds(start, GROUP), :]
        kt = kt_s[...]
        mask = lax.broadcasted_iota(jnp.int32, (half, half), 0) <= lax.broadcasted_iota(
            jnp.int32, (half, half), 1
        )
        left_lane = lax.broadcasted_iota(jnp.int32, (half, LANES), 1) < HEAD_DIM
        lane_id = lax.broadcasted_iota(jnp.int32, (1, LANES), 1)
        pieces, col_sums = [], []
        row_sums = rows_s[...]
        w_tl, w_tr, w_br = wt_s[:half, :half], wt_s[:half, half:], wt_s[half:, half:]
        for pair in range(GROUP // 2):
            lanes = slice(pair * LANES, (pair + 1) * LANES)
            x_pair, g_pair = x_low[:, lanes], g_low[:, lanes]
            x_heads = [
                jnp.where(mine, x_pair[rows], jnp.zeros_like(x_pair[rows]))
                for rows in (slice(0, half), slice(half, length))
                for mine in (left_lane, jnp.logical_not(left_lane))
            ]
            p_top = dot(jnp.concatenate(x_heads[:2], axis=0), g_pair, NT)
            p_low = dot(jnp.concatenate(x_heads[2:], axis=0), g_pair[half:], NT)
            tops, lows = [], []
            for i in (2 * pair, 2 * pair + 1):
                col, row = cum[:, i : i + 1], cumt[i : i + 1, :]
                l_tl = jnp.exp2(jnp.where(mask, row[:, :half] - col[:half], -1e30))
                l_tr = jnp.exp2(row[:, half:] - col[:half])
                l_br = jnp.exp2(jnp.where(mask, row[:, half:] - col[half:], -1e30))
                lk_tl, lk_tr, lk_br = (
                    l_tl * kt[:half, :half],
                    l_tr * kt[:half, half:],
                    l_br * kt[half:, half:],
                )
                tops.append(jnp.concatenate([lk_tl.astype(bf16), lk_tr.astype(bf16)], axis=1))
                lows.append(lk_br.astype(bf16))
                of_head = slice((i % 2) * half, (i % 2 + 1) * half)
                p_tl, p_tr, p_br = p_top[of_head, :half], p_top[of_head, half:], p_low[of_head]
                w_tl, w_tr, w_br = w_tl + l_tl * p_tl, w_tr + l_tr * p_tr, w_br + l_br * p_br
                z_tl, z_tr, z_br = lk_tl * p_tl, lk_tr * p_tr, lk_br * p_br
                sums = jnp.concatenate(
                    [
                        jnp.sum(z_tl + z_tr, axis=1, keepdims=True),
                        jnp.sum(z_br, axis=1, keepdims=True),
                    ],
                    axis=0,
                )
                row_sums = row_sums + jnp.where(lane_id == start + i, sums, 0.0)
                col_sums.append(
                    jnp.concatenate(
                        [
                            jnp.sum(z_tl, axis=0, keepdims=True),
                            jnp.sum(z_tr + z_br, axis=0, keepdims=True),
                        ],
                        axis=1,
                    )
                )
            tops = dot(jnp.concatenate(tops, axis=0), g_pair, NN)
            lows = dot(jnp.concatenate(lows, axis=0), g_pair[half:], NN)
            pieces.append(
                jnp.concatenate(
                    [jnp.where(left_lane, both[:half], both[half:]) for both in (tops, lows)],
                    axis=0,
                )
            )
        wt_s[:half, :half] = w_tl
        wt_s[:half, half:] = w_tr
        wt_s[half:, half:] = w_br
        rows_s[...] = row_sums
        cols_s[pl.ds(start, GROUP), :] = jnp.concatenate(col_sums, axis=0)
        mixed_grad = jnp.concatenate(pieces, axis=1) + from_adj
        products = [act * mixed_grad, x_dt * from_adj, grad_ssm * carried]
        picked = dot(jnp.concatenate([v.astype(bf16) for v in products], axis=0), pick, NN)
        direct_s[...] += picked[:length]
        fresh_s[...] += picked[length : 2 * length]
        carry_s[...] += picked[2 * length :]
        grad_pre = (dt * mixed_grad + skip[...] * grad_ssm) * slope_ref[...].astype(f32)
        next_o[...] = grad_pre[0:8]
        later = later_rows(grad_pre, carried_in(next_in))
        grad_conv = conv_sum(taps[...], later)
        grad_conv = grad_conv.astype(bf16)
        gc_o[:, pl.ds(pl.multiple_of(step * WIDTH, WIDTH), WIDTH)] = grad_conv
        conv_in = cin[...].astype(f32)
        sums = [jnp.sum(conv_in * rows, axis=0, keepdims=True) for rows in later]
        sums += [jnp.sum(grad_pre, axis=0, keepdims=True), gain_grad, skip_grad]
        chan_o[...] = jnp.concatenate(sums + [jnp.zeros_like(skip_grad)], axis=0)
        acc_s[...] += dot(grad_gate, wg[...], NT) + dot(grad_conv, wc[...], NT)

    @pl.when(jnp.logical_and(step == GROUPS, valid))
    def _():
        wt = wt_s[...].astype(bf16)
        grad_b = db_s[...] + dot(wt, c_s[...], NN)
        grad_c = dc_s[...] + dot(wt, b_s[...], TN)
        grad_pre = jnp.concatenate([grad_b, grad_c], axis=1) * dsilu_s[...]
        next_bc_o[...] = grad_pre[0:8]
        tap_rows = taps_bc[...]
        later = later_rows(grad_pre, carried_in(next_bc_in))
        grad_conv = conv_sum(tap_rows, later)
        conv_in = cin_bc[...].astype(f32)
        sums = [jnp.sum(conv_in * rows, axis=0, keepdims=True) for rows in later]
        sums += [jnp.sum(grad_pre, axis=0, keepdims=True)]
        chan_bc_o[...] = jnp.concatenate(sums + [jnp.zeros((3, BC), f32)], axis=0)
        dt = head_steps(step_ref[...], head_rows[...])
        rate = head_rows[1:2]
        ones = jnp.where(lower_mask(length, length), 1.0, 0.0).astype(f32)
        fresh = fresh_s[...]
        from_here = cols_s[...].T - rows_s[...] + carry_s[...]
        suffix = (
            dot(ones, from_here, TN, lax.Precision.HIGHEST)
            + dot(ones, fresh, NN, lax.Precision.HIGHEST)
            - fresh
            + edge_s[0:1]
        )
        decayed = rate * suffix
        grad_step = (direct_s[...] + decayed) * sigmoid(step_ref[...] + head_rows[0:1])
        head_o[...] = jnp.concatenate(
            [
                jnp.sum(grad_step, axis=0, keepdims=True),
                jnp.sum(dt * decayed, axis=0, keepdims=True),
                jnp.zeros((6, LANES), f32),
            ],
            axis=0,
        )
        low = jnp.concatenate([grad_conv.astype(bf16), grad_step.astype(bf16)], axis=1)
        gc_o[:, DI:] = low
        grad_normed = acc_s[...] + dot(low, wbc[...], NT)
        h = chosen(flag[0, 0], own_ref, other_ref)
        scale = lax.rsqrt(jnp.mean(h * h, axis=1, keepdims=True) + EPS)
        ngrad_o[...] = jnp.sum(grad_normed * h * scale, axis=0, keepdims=True)
        weighted = grad_normed * ngain[...]
        mean = jnp.mean(h * weighted, axis=1, keepdims=True)
        grad_in = gout_ref[...].astype(f32) + scale * weighted - h * (scale * scale * scale * mean)
        gin_o[...] = grad_in
        gin_low_o[...] = grad_in.astype(bf16)


def spread_table():
    table = np.zeros((2 * LANES, DI), np.float32)
    for head in range(HEADS):
        table[head, head * HEAD_DIM : (head + 1) * HEAD_DIM] = 1.0
        table[LANES + head, head * HEAD_DIM : (head + 1) * HEAD_DIM] = 1.0
    return table


def whole(shape):
    return pl.BlockSpec(shape, lambda i: (0,) * len(shape))


def by_group(rows, width=WIDTH, skip=0):
    return pl.BlockSpec((rows, width), lambda i: (0, jnp.minimum(i, GROUPS - 1) + skip))


def tail_of(rows, width, at):
    return pl.BlockSpec((rows, width), lambda i: (0, at // width))


def gather_table():
    table = np.zeros((GROUPS, WIDTH, LANES), np.float32)
    for group in range(GROUPS):
        for column in range(WIDTH):
            table[group, column, group * GROUP + column // HEAD_DIM] = 1.0
    return table.reshape(-1, LANES)


FLAGS = pl.BlockSpec(memory_space=pltpu.SMEM)


def fwd_call(flag, own, other, params, weights, state, tail, tail_bc):
    length = own.shape[0]
    win, wo = weights
    in_specs = [
        FLAGS, whole((length, D)), whole((length, D)), whole((1, D)), by_group(D), by_group(D, WIDTH, GROUPS), tail_of(D, TAIL, 2 * DI),
        pl.BlockSpec((WIDTH, D), lambda i: (jnp.minimum(i, GROUPS - 1), 0)),
        by_group(8), tail_of(8, BC, DI), whole((8, LANES)), by_group(1), by_group(1),
        by_group(2 * LANES), by_group(16), whole((16, BC)), by_group(STATE),
    ]
    out = [
        ((length, D), bf16, whole((length, D))),
        ((length, DI), bf16, by_group(length)),
        ((length, DI), bf16, by_group(length)),
        ((length, DI), bf16, by_group(length)),
        ((length, BC), bf16, whole((length, BC))),
        ((length, LANES), f32, whole((length, LANES))),
        ((length, DI), bf16, by_group(length)),
        ((length, DI), bf16, by_group(length)),
        ((length, DI), bf16, by_group(length)),
        ((STATE, DI), f32, by_group(STATE)),
        ((length, DI), bf16, whole((length, DI))),
        ((length, LANES), f32, whole((length, LANES))),
        ((length, D), f32, whole((length, D))),
        ((length, D), bf16, whole((length, D))),
        ((16, DI), bf16, by_group(16)),
        ((16, BC), bf16, whole((16, BC))),
    ]
    scratch = [
        ((length, DI), f32), ((length, LANES), f32), ((length, length), f32),
        ((length, STATE), bf16), ((STATE, length), bf16), ((3 * length, 2 * LANES), bf16),
        ((GROUPS, length, GROUP), f32),
        ((LANES, length), f32),
    ]
    return pl.pallas_call(
        fwd_body,
        grid=(GROUPS + 1,),
        in_specs=in_specs,
        out_specs=[spec for _, _, spec in out],
        out_shape=[jax.ShapeDtypeStruct(shape, dtype) for shape, dtype, _ in out],
        scratch_shapes=[pltpu.VMEM(shape, dtype) for shape, dtype in scratch],
        compiler_params=pltpu.CompilerParams(
            dimension_semantics=("arbitrary",), vmem_limit_bytes=VMEM_LIMIT
        ),
        cost_estimate=pl.CostEstimate(flops=12 * 10**9, bytes_accessed=45 * 10**6, transcendentals=5 * 10**6),
        name="layer_forward",
    )(
        flag, own, other, params["norm_gain"], win, win, win, wo, params["taps"], params["taps"],
        params["heads"], params["skip"], params["gate_gain"], params["spread"], tail, tail_bc, state,
    )


def bwd_call(flag, own_grad, other_grad, kept, params, weights, adj, ahead, ahead_bc):
    length = own_grad.shape[0]
    win, wo = weights
    rows_of_wo = pl.BlockSpec((WIDTH, D), lambda i: (jnp.minimum(i, GROUPS - 1), 0))
    pick = pl.BlockSpec((WIDTH, LANES), lambda i: (jnp.minimum(i, GROUPS - 1), 0))
    in_specs = [
        FLAGS, whole((length, D)), whole((length, D)), whole((length, D)), whole((length, D)),
        whole((1, D)), whole((length, D)),
        whole((length, LANES)), rows_of_wo, by_group(D), by_group(D, WIDTH, GROUPS), tail_of(D, TAIL, 2 * DI),
        by_group(8), tail_of(8, BC, DI), whole((8, LANES)), by_group(1), by_group(1),
        by_group(2 * LANES), pick, by_group(length), by_group(length), by_group(length),
        by_group(length), by_group(length), by_group(length), whole((length, BC)),
        whole((length, LANES)), whole((16, BC)),
        by_group(STATE), by_group(STATE), by_group(8), whole((8, BC)),
    ]
    out = [
        ((length, D), bf16, whole((length, D))),
        ((length, DI), bf16, by_group(length)),
        ((length, DI + TAIL), bf16, whole((length, DI + TAIL))),
        ((length, D), f32, whole((length, D))),
        ((length, D), bf16, whole((length, D))),
        ((STATE, DI), f32, by_group(STATE)),
        ((8, DI), f32, by_group(8)),
        ((8, BC), f32, whole((8, BC))),
        ((8, DI), f32, by_group(8)),
        ((8, BC), f32, whole((8, BC))),
        ((1, D), f32, whole((1, D))),
        ((8, LANES), f32, whole((8, LANES))),
    ]
    scratch = [
        ((length, D), f32), ((length, length), f32), ((length, length), f32),
        ((length, STATE), bf16), ((length, STATE), bf16), ((STATE, length), bf16),
        ((3 * length, 2 * LANES), bf16),
        ((GROUPS, length, GROUP), f32), ((LANES, length), f32), ((length, STATE), f32),
        ((length, STATE), f32), ((length, LANES), f32), ((LANES, length), f32),
        ((length, LANES), f32), ((length, LANES), f32), ((length, LANES), f32), ((1, LANES), f32),
        ((length, BC), f32), ((length, LANES), f32),
    ]
    return pl.pallas_call(
        bwd_body,
        grid=(GROUPS + 1,),
        in_specs=in_specs,
        out_specs=[spec for _, _, spec in out],
        out_shape=[jax.ShapeDtypeStruct(shape, dtype) for shape, dtype, _ in out],
        scratch_shapes=[pltpu.VMEM(shape, dtype) for shape, dtype in scratch],
        compiler_params=pltpu.CompilerParams(
            dimension_semantics=("arbitrary",), vmem_limit_bytes=VMEM_LIMIT
        ),
        cost_estimate=pl.CostEstimate(flops=25 * 10**9, bytes_accessed=55 * 10**6, transcendentals=8 * 10**6),
        name="layer_backward",
    )(
        flag, kept["own"], kept["other"], own_grad, other_grad, params["norm_gain"], kept["branch"], kept["r"], wo, win, win, win,
        params["taps"], params["taps"], params["heads"], params["skip"], params["gate_gain"],
        params["spread"], params["gather"], kept["silu"], kept["turned"], kept["u"], kept["act"],
        kept["slope"], kept["cin"], kept["cin_bc"], kept["step"], kept["tail_bc"], kept["state"], adj, ahead, ahead_bc,
    )


def xor_route(size, bit):
    return [(i, i ^ bit) for i in range(size)]


def bits_of(size):
    return [1 << b for b in range(size.bit_length() - 1)]


def gather_small(row):
    for axis in ("seq", "dp"):
        size, position = lax.axis_size(axis), lax.axis_index(axis)
        for bit in bits_of(size):
            other = lax.ppermute(row, axis, xor_route(size, bit))
            row = jnp.where(
                (position & bit) == 0,
                jnp.concatenate([row, other], axis=0),
                jnp.concatenate([other, row], axis=0),
            )
    return row


def exchanges():
    return [(axis, bit) for axis in ("dp", "seq") for bit in bits_of(lax.axis_size(axis))]


def exchange(value, axis, bit):
    return value + lax.ppermute(value, axis, xor_route(lax.axis_size(axis), bit))


def sum_small(value):
    for axis, bit in exchanges():
        value = exchange(value, axis, bit)
    return value


def direct_paths():
    return lax.axis_size("dp") == 4 and lax.axis_size("seq") == 4


RING = 8


def ring_place(position):
    return jnp.where(position < 4, position, 11 - position)


def ring_route(step):
    def device(position, core):
        y, z = (0, position) if position < 4 else (1, 7 - position)
        return (y * 2 + core) * 4 + z

    return [
        (device(p, core), device((p + step) % RING, core)) for p in range(RING) for core in range(2)
    ]


def around(value, step):
    return lax.ppermute(value, ("dp", "seq"), ring_route(step))


def across(value):
    return lax.ppermute(value, "dp", xor_route(4, 1))


def own_position():
    dp, z = lax.axis_index("dp"), lax.axis_index("seq")
    y = dp // 2
    return jnp.where(y == 0, z, 7 - z), dp % 2


def together(up, down):
    pairs = [lax.optimization_barrier(pair) for pair in zip(up, down)]
    return [a for a, _ in pairs], [b for _, b in pairs]


def gather_rows(shards):
    if not direct_paths():
        return [lax.all_gather(shard, ("dp", "seq"), axis=0, tiled=True) for shard in shards]
    position, core = own_position()
    held = [jnp.zeros((16,) + shard.shape, shard.dtype) for shard in shards]

    def place(held, pieces, offset, start=0):
        at = ring_place((position + offset) % RING)
        at = (at // 4) * 8 + at % 4
        others = [across(piece) for piece in pieces]
        for of_core, values in ((core, pieces), (1 - core, others)):
            held = [
                lax.dynamic_update_slice(whole, value[None], (at + of_core * 4, start * rows, 0))
                for whole, value, rows in zip(held, values, halves_of)
            ]
        return held

    halves_of = [shard.shape[0] // 2 for shard in shards]
    up, down = shards, shards
    held = place(held, shards, 0)
    for hop in range(1, 4):
        up, down = [around(v, 1) for v in up], [around(v, -1) for v in down]
        up, down = together(up, down)
        held = place(place(held, up, -hop), down, hop)
    up = [around(v[:rows], 1) for v, rows in zip(up, halves_of)]
    down = [around(v[rows:], -1) for v, rows in zip(down, halves_of)]
    held = place(place(held, up, 4), down, 4, 1)
    return [whole.reshape((-1,) + whole.shape[2:]) for whole in held]


def reduce_rows(chips, small, early):
    position, _ = own_position()
    hops = exchanges()

    def term(chip, offset):
        at = ring_place((position + offset) % RING)
        return lax.dynamic_index_in_dim(chip, at, 0, keepdims=False)

    half = [chip.shape[1] // 2 for chip in chips]
    up = [around(term(chip, 4)[:rows], 1) for chip, rows in zip(chips, half)]
    down = [around(term(chip, -4)[rows:], -1) for chip, rows in zip(chips, half)]
    small = exchange(small, *hops[0])
    up, down = together(up, down)
    up[0], small, early = lax.optimization_barrier((up[0], small, early))
    up = [jnp.pad(v, ((0, rows), (0, 0))) for v, rows in zip(up, half)]
    down = [jnp.pad(v, ((rows, 0), (0, 0))) for v, rows in zip(down, half)]
    for hop, offset in enumerate((3, 2, 1), 1):
        up = [
            around((term(chip, offset).astype(f32) + v.astype(f32)).astype(bf16), 1)
            for chip, v in zip(chips, up)
        ]
        down = [
            around((term(chip, -offset).astype(f32) + v.astype(f32)).astype(bf16), -1)
            for chip, v in zip(chips, down)
        ]
        small = exchange(small, *hops[hop])
        up, down = together(up, down)
        up[0], small = lax.optimization_barrier((up[0], small))
    sums = [
        term(chip, 0).astype(f32) + a.astype(f32) + b.astype(f32)
        for chip, a, b in zip(chips, up, down)
    ]
    return sums, small, early


def weight_grads(pairs, small, early, ready):
    def term(columns, right):
        return jnp.einsum("td,te->de", columns, right, preferred_element_type=f32)

    if not direct_paths():
        sums = [
            lax.optimization_barrier(
                lax.psum_scatter(term(left, right), ("dp", "seq"), scatter_dimension=0, tiled=True)
            )
            for left, right in pairs
        ]
        return sums, sum_small(small), early, ready
    core = lax.axis_index("dp") % 2

    def owned(left, right, which):
        quarter = left.shape[1] // 4
        parts = [left[:, i * quarter : (i + 1) * quarter] for i in range(4)]
        chosen = jnp.concatenate(
            [jnp.where(which == 0, parts[0], parts[1]), jnp.where(which == 0, parts[2], parts[3])],
            axis=1,
        )
        return term(chosen, right).astype(bf16).reshape(RING, quarter // 4, right.shape[1])

    arrived = [across(owned(left, right, 1 - core)) for left, right in pairs]
    left, ready = lax.optimization_barrier((pairs[0][0], ready))
    chips = [
        (owned(left, right, core).astype(f32) + other.astype(f32)).astype(bf16)
        for (_, right), other in zip(pairs, arrived)
    ]
    return *reduce_rows(chips, small, early), ready


def turn(value, shift, parts):
    size = lax.axis_size("seq")
    route = [(i, i - i % parts + (i % parts + shift) % parts) for i in range(size)]
    return lax.ppermute(value, "seq", route)


def in_order(arrived):
    parts = len(arrived)
    rank = lax.axis_index("seq") % parts
    arrived = jnp.stack(arrived)
    return [
        lax.dynamic_index_in_dim(arrived, (rank - k) % parts, 0, keepdims=False)
        for k in range(parts)
    ]


def token_blocks(tokens):
    parts, length = tokens.shape[0], tokens.shape[1]
    rank, section = lax.axis_index("seq") % parts, lax.axis_index("section")
    half = length // 2
    arrived = []
    for shift in range(1, parts):
        at = ((rank + shift) % parts, section * half, 0)
        piece = lax.dynamic_slice(tokens, at, (1, half, tokens.shape[2]))[0]
        arrived.append(turn(piece, shift, parts))
    handed = lax.ppermute(jnp.concatenate(arrived, axis=0), "section", [(1, 0)])
    blocks = [lax.dynamic_index_in_dim(tokens, rank, 0, keepdims=False)]
    for i, low in enumerate(arrived):
        blocks.append(jnp.concatenate([low, handed[i * half : (i + 1) * half]], axis=0))
    return in_order(blocks)


def cotangent_blocks(rows, late):
    parts = rows.shape[0]
    size = lax.axis_size("seq")
    rank = lax.axis_index("seq") % parts
    arrived = [lax.dynamic_index_in_dim(rows, rank, 0, keepdims=False)]
    for shift in range(1, parts):
        piece = lax.dynamic_index_in_dim(rows, (rank + shift) % parts, 0, keepdims=False)
        route = [
            (size + i, size + i - i % parts + (i % parts + shift) % parts) for i in range(size)
        ]
        arrived.append(lax.ppermute(piece, ("section", "seq"), route))
    arrived, _ = lax.optimization_barrier((arrived, late))
    return in_order(arrived)


def to_pieces(blocks, sent_type):
    parts = len(blocks)
    rank = lax.axis_index("seq") % parts
    stacked = jnp.stack(blocks)
    held = stacked
    pieces = []
    for shift in range(parts):
        piece = lax.dynamic_index_in_dim(stacked, (rank + shift) % parts, 0, keepdims=False)
        if shift:
            piece = turn(piece.astype(sent_type), shift, parts)
        pieces.append(piece)
    return stacked, pieces


def laid_out(held, pieces):
    parts = len(pieces)
    rank = lax.axis_index("seq") % parts
    for shift, piece in enumerate(pieces):
        piece = piece.astype(held.dtype)
        held = lax.dynamic_update_slice(held, piece[None], ((rank - shift) % parts, 0, 0))
    return held


KEPT = (
    "normed", "cin", "act", "slope", "cin_bc", "step", "silu", "turned", "u", "state_out", "gout", "r",
    "branch", "out",
    "tail_out", "tail_bc_out",
)
SKEW = 2


def flags(first, grad, valid, carried=True):
    values = [jnp.where(first, 1, 0), jnp.asarray(grad, jnp.int32)]
    values += [jnp.where(flag, 1, 0) for flag in (valid, carried)]
    return jnp.stack(values).astype(jnp.int32)[None]


def shards(
    tokens, cotangent, in_proj, out_proj, conv_weight, conv_bias, norm_gain, gate_gain, step_bias,
    log_decay, skip_gain,
):
    first = lax.axis_index("section") == 0
    seq = lax.axis_size("seq")
    parts, length = tokens.shape[0], tokens.shape[1]
    owned = in_proj.shape[1]
    tokens_in = token_blocks(tokens)

    shard = jnp.pad(in_proj[0], ((0, 0), (0, TAIL - BC - HEADS)))
    weights = (
        lax.all_gather(shard, ("dp", "seq"), axis=0, tiled=True),
        gather_rows([out_proj[0]])[0],
    )

    sizes = [CONV * conv_bias.shape[1], conv_bias.shape[1], norm_gain.shape[1], gate_gain.shape[1]]
    packed = jnp.concatenate([conv_weight[0].reshape(-1), conv_bias[0], norm_gain[0], gate_gain[0]])
    packed = gather_small(packed[None]).astype(f32)
    ends = np.cumsum(sizes)
    taps, shift, gain_in, gain_gate = (
        packed[:, end - size : end] for end, size in zip(ends, sizes)
    )
    taps = jnp.swapaxes(taps.reshape(-1, CONV, conv_bias.shape[1]), 0, 1).reshape(CONV, -1)
    taps = jnp.concatenate([taps, shift.reshape(1, -1), jnp.zeros((3, taps.shape[1]), f32)], axis=0)
    lanes = ((0, 0), (0, LANES - HEADS))
    params = {
        "norm_gain": gain_in.reshape(1, -1),
        "gate_gain": gain_gate.reshape(1, -1),
        "taps": taps,
        "heads": jnp.pad(
            jnp.concatenate([step_bias, -jnp.exp(log_decay), jnp.zeros((6, HEADS), f32)], axis=0),
            lanes,
        ),
        "skip": jnp.repeat(skip_gain, HEAD_DIM, axis=1),
        "spread": jnp.asarray(spread_table(), bf16),
        "gather": jnp.asarray(gather_table(), bf16),
    }

    ticks = parts + SKEW
    hops = seq // parts

    def forward(start):
        kept, received = [], [jnp.zeros((length, D), bf16)] * SKEW
        carry = start
        for tick in range(ticks):
            if tick == SKEW:
                carry = tuple(jnp.where(first, now, at) for now, at in zip(carry, start))
            own, other = tokens_in[min(tick, parts - 1)], received[tick]
            valid = jnp.where(first, tick < parts, tick >= SKEW)
            values = dict(zip(KEPT, fwd_call(flags(first, 0, valid), own, other, params, weights, *carry)))
            values.update(own=own, other=other, state=carry[0], tail=carry[1], tail_bc=carry[2])
            carry = (values["state_out"], values["tail_out"], values["tail_bc_out"])
            kept.append(values)
            if tick < parts:
                received.append(lax.ppermute(values["out"], "section", [(0, 1)]))
        return kept

    def backward(kept, start, before_last=None):
        early = None
        zeros = tuple(jnp.zeros_like(part) for part in start)
        carry = tuple(jnp.where(first, zero, at) for zero, at in zip(zeros, start))
        grads, received = [None] * ticks, [jnp.zeros((length, D), bf16)] * SKEW
        for tick in range(ticks):
            carried = jnp.logical_not(first) if tick == SKEW and hops == 1 else True
            if tick == SKEW and hops > 1:
                carry = tuple(jnp.where(first, at, now) for now, at in zip(carry, start))
            from_loss = loss_in[max(parts - 1 - tick, 0)]
            late = jnp.int32(2 if tick >= parts else 1)
            valid = jnp.where(first, tick >= SKEW, tick < parts)
            if before_last is not None and tick == ticks - 1:
                early = before_last(grads, received[tick])
                from_loss, early = lax.optimization_barrier((from_loss, early))
            at = ticks - 1 - tick
            names = (
                "out", "gate", "conv", "in", "in_low", "adj", "next", "next_bc", "chan", "chan_bc",
                "norm", "head",
            )
            values = dict(
                zip(
                    names,
                    bwd_call(
                        flags(first, jnp.where(first, 0, late), valid, carried),
                        from_loss,
                        received[tick],
                        kept[at],
                        params,
                        weights,
                        *carry,
                    ),
                )
            )
            carry = (values["adj"], values["next"], values["next_bc"])
            grads[at] = values
            if tick < parts:
                sent, received[-1] = lax.optimization_barrier((values["in_low"], received[-1]))
                received.append(lax.ppermute(sent, "section", [(1, 0)]))
        return grads, early

    start = (jnp.zeros((STATE, DI), f32), jnp.zeros((16, DI), bf16), jnp.zeros((16, BC), bf16))
    if hops > 1:

        def onward(_, start):
            kept = forward(start)
            ends = (
                tuple(kept[parts - 1][name] for name in ("state_out", "tail_out", "tail_bc_out")),
                tuple(kept[ticks - 1][name] for name in ("state_out", "tail_out", "tail_bc_out")),
            )
            route = [(i, i + parts) for i in range(seq - parts)]
            return tuple(
                lax.ppermute(jnp.where(first, a, b), "seq", route) for a, b in zip(*ends)
            )

        start = lax.fori_loop(0, hops - 1, onward, start)
    kept = forward(start)
    cotangent, _ = lax.optimization_barrier((cotangent, kept[0]["r"]))
    loss_in = cotangent_blocks(cotangent, kept[-1]["r"])
    activations = laid_out(
        *to_pieces(
            [jnp.where(first, kept[k]["out"], kept[k + SKEW]["out"]) for k in range(parts)], bf16
        )
    )[None]

    start = (jnp.zeros((STATE, DI), f32), jnp.zeros((8, DI), f32), jnp.zeros((8, BC), f32))
    if hops > 1:

        def back(_, start):
            grads, _ = backward(kept, start)
            ends = (
                tuple(grads[0][name] for name in ("adj", "next", "next_bc")),
                tuple(grads[SKEW][name] for name in ("adj", "next", "next_bc")),
            )
            route = [(i, i - parts) for i in range(parts, seq)]
            return tuple(
                lax.ppermute(jnp.where(first, a, b), "seq", route) for a, b in zip(*ends)
            )

        start = lax.fori_loop(0, hops - 1, back, start)
    def select(values, name):
        return jnp.concatenate(
            [jnp.where(first, values[k][name], values[k + SKEW][name]) for k in range(parts)], axis=0
        )

    def out_term(grads, received):
        branch_grads = [jnp.where(first, received, loss_in[0])] + [
            jnp.where(first, grads[k]["out"], grads[k + SKEW]["out"]) for k in range(1, parts)
        ]
        return jnp.einsum(
            "td,te->de",
            select(kept, "gout"),
            jnp.concatenate(branch_grads, axis=0),
            preferred_element_type=f32,
        ).astype(bf16)

    grads, term = backward(kept, start, out_term)
    grad_out_proj = lax.psum_scatter(
        term, ("dp", "seq"), scatter_dimension=0, tiled=True
    ).astype(f32)
    normed = select(kept, "normed")
    def total(name):
        return sum(values[name] for values in grads)

    channels = jnp.concatenate([total("chan"), total("chan_bc")], axis=1)
    head = total("head")
    last_row = jnp.concatenate([total("norm"), head[0:1], head[1:2]], axis=1)
    fill = channels.shape[1] - last_row.shape[1]
    small = (channels + jnp.pad(last_row, ((7, 0), (0, fill))))
    held, pieces = to_pieces(
        [jnp.where(first, grads[k]["in"], grads[k + SKEW]["in"]) for k in range(parts)], bf16
    )
    near = [pieces[1], pieces[-1]]
    (grad_gate, grad_conv), small, grad_out_proj, near = weight_grads(
        [(normed, select(grads, "gate")), (normed, select(grads, "conv"))],
        small,
        grad_out_proj,
        near,
    )
    pieces[1], pieces[-1] = near
    pieces, grad_gate = lax.optimization_barrier((pieces, grad_gate))
    input_grads = laid_out(held, pieces)[None]
    grad_in_proj = jnp.concatenate([grad_gate, grad_conv[:, : DI + BC + HEADS]], axis=1)[None]

    place = lax.axis_index("dp") * seq + lax.axis_index("seq")

    def mine(flat, width):
        return lax.dynamic_slice_in_dim(flat, place * width, width, axis=flat.ndim - 1)

    width = conv_bias.shape[1]
    return (
        activations,
        input_grads,
        grad_in_proj,
        grad_out_proj[None],
        mine(small[:CONV], width)[None],
        mine(small[CONV], width)[None],
        mine(small[7, :D], owned)[None],
        mine(small[5, :DI], gate_gain.shape[1])[None],
        small[7:8, D : D + HEADS],
        small[7:8, D + LANES : D + LANES + HEADS],
        small[6, :DI].reshape(HEADS, HEAD_DIM).sum(axis=1)[None],
    )


def solution(mesh):
    placed = (
        P("dp", "seq", None),
        P("dp", "seq", None),
        P("section", ("dp", "seq"), None),
        P("section", ("dp", "seq"), None),
        P("section", None, ("dp", "seq")),
        P("section", ("dp", "seq")),
        P("section", ("dp", "seq")),
        P("section", ("dp", "seq")),
        P("section", None),
        P("section", None),
        P("section", None),
    )
    return jax.shard_map(
        shards,
        mesh=mesh,
        in_specs=placed,
        out_specs=(
            P("section", "dp", "seq", None),
            P("section", "dp", "seq", None),
        )
        + placed[2:],
        check_vma=False,
    )
```

```python
import jax
import jax.numpy as jnp
import numpy as np
from jax import lax
from jax.experimental import pallas as pl
from jax.experimental.pallas import tpu as pltpu
from jax.sharding import PartitionSpec as P

D = 1536
HEADS = 48
HEAD_DIM = 64
STATE = 128
CONV = 4
DI = 3072
BC = 2 * STATE
TAIL = BC + 128
GROUP = 8
WIDTH = GROUP * HEAD_DIM
GROUPS = HEADS // GROUP
LANES = 128
EPS = 1e-05
LOG2_E = 1.4426950408889634
f32 = jnp.float32
bf16 = jnp.bfloat16
VMEM_LIMIT = 56 * 2**20
NN = ((1,), (0,))
NT = ((1,), (1,))
TN = ((0,), (0,))


def dot(a, b, dims, precision=None):
    return lax.dot_general(a, b, (dims, ((), ())), preferred_element_type=f32, precision=precision)


def halves(value):
    top = value.astype(bf16)
    rest = (value - top.astype(f32)).astype(bf16)
    return jnp.concatenate([top, rest], axis=1)


def lower_mask(rows, cols):
    return lax.broadcasted_iota(jnp.int32, (rows, cols), 0) >= lax.broadcasted_iota(
        jnp.int32, (rows, cols), 1
    )


def sigmoid(v):
    return 0.5 * jnp.tanh(0.5 * v) + 0.5


def head_steps(step_raw, head_rows):
    biased = step_raw + head_rows[0:1]
    return jnp.maximum(biased, 0.0) + jnp.log1p(jnp.exp(-jnp.abs(biased)))


def running_sum(value):
    length = value.shape[0]
    ones = jnp.where(lower_mask(length, length), 1.0, 0.0).astype(f32)
    return dot(ones, value, NN, lax.Precision.HIGHEST)


def earlier_rows(tail, rows):
    joined = jnp.concatenate([tail[8:16].astype(f32), rows], axis=0)
    shifted = [pltpu.roll(joined, shift, 0)[8:] for shift in range(CONV - 1, 0, -1)]
    return shifted + [rows]


def later_rows(rows, head):
    length = rows.shape[0]
    joined = jnp.concatenate([rows, head], axis=0)
    shifted = [pltpu.roll(joined, length + 8 - shift, 0)[:length] for shift in range(CONV - 1, 0, -1)]
    return shifted + [rows]


def conv_sum(taps, shifted, start=0.0):
    for j in range(CONV):
        start = start + shifted[j] * taps[j : j + 1]
    return start


def chosen(flag, own, other):
    return jnp.where(flag == 1, own[...].astype(f32), other[...].astype(f32))


def chosen_grad(flag, own, other):
    other_or_zero = jnp.where(flag == 0, other[...].astype(f32), 0.0)
    return jnp.where(flag == 1, own[...].astype(f32), other_or_zero)


def fwd_body(
    flag, own_ref, other_ref, ngain, wg, wc, wbc, wo, taps, taps_bc, head_rows, skip, gate_gain, spread, tail_in,
    tail_bc_in, state_in,
    normed_o, cin_o, act_o, slope_o, cin_bc_o, step_o, silu_o, turned_o, u_o, state_o, gout_o, r_o, branch_o, out_o,
    tail_o, tail_bc_o,
    u_s, ssq_s, k_s, c_s, bt_s, sp_s, cum_s, cumt_s,
):
    step = pl.program_id(0)
    length = own_ref.shape[0]
    half = length // 2
    valid = flag[0, 2] == 1

    @pl.when(jnp.logical_and(step == 0, valid))
    def _():
        h = chosen(flag[0, 0], own_ref, other_ref)
        scale = lax.rsqrt(jnp.mean(h * h, axis=1, keepdims=True) + EPS)
        normed = (h * scale * ngain[...]).astype(bf16)
        normed_o[...] = normed
        projected = dot(normed, wbc[...], NN)
        step_raw = projected[:, BC:]
        step_o[...] = step_raw
        conv_in = projected[:, :BC].astype(bf16)
        cin_bc_o[...] = conv_in
        tail_bc_o[...] = conv_in[length - 16 :]
        tap_rows = taps_bc[...]
        shifted = earlier_rows(tail_bc_in[...], conv_in.astype(f32))
        pre = conv_sum(tap_rows, shifted, tap_rows[CONV : CONV + 1])
        act = (pre * sigmoid(pre)).astype(bf16)
        b_rows, c_rows = act[:, :STATE], act[:, STATE:]
        c_s[...] = c_rows
        bt_s[...] = b_rows.astype(f32).T.astype(bf16)
        k_s[...] = dot(c_rows, b_rows, NT)
        dt = head_steps(step_raw, head_rows[...])
        cum = running_sum(dt * head_rows[1:2])
        total = cum[length - 1 : length]
        sp_s[0:length] = halves(dt)
        sp_s[length : 2 * length] = halves(jnp.exp(cum))
        sp_s[2 * length :] = halves(dt * jnp.exp(total - cum))
        for g in range(GROUPS):
            cum_s[g] = cum[:, g * GROUP : (g + 1) * GROUP] * LOG2_E
        cumt_s[...] = (cum * LOG2_E).T
        ssq_s[...] = jnp.zeros_like(ssq_s)
        branch_o[...] = jnp.zeros_like(branch_o)

    @pl.when(jnp.logical_and(step < GROUPS, valid))
    def _():
        normed = normed_o[...]
        gate = dot(normed, wg[...], NN)
        conv_in = dot(normed, wc[...], NN).astype(bf16)
        cin_o[...] = conv_in
        tail_o[...] = conv_in[length - 16 :]
        tap_rows = taps[...]
        shifted = earlier_rows(tail_in[...], conv_in.astype(f32))
        pre = conv_sum(tap_rows, shifted, tap_rows[CONV : CONV + 1])
        sig = sigmoid(pre)
        act = pre * sig
        slope_o[...] = (sig + act * (1.0 - sig)).astype(bf16)
        act_o[...] = act.astype(bf16)
        act = act_o[...].astype(f32)
        where = spread[...]
        spreads = dot(sp_s[...], where, NN)
        x_dt = (act * spreads[:length]).astype(bf16)
        x_w = (act * spreads[2 * length :]).astype(bf16)
        ec = spreads[length : 2 * length]
        state = state_in[...]
        state_o[...] = ec[length - 1 : length] * state + dot(bt_s[...], x_w, NN)
        carried = dot(c_s[...], state.astype(bf16), NN) * ec
        cum = cum_s[step]
        cumt = cumt_s[pl.ds(pl.multiple_of(step * GROUP, GROUP), GROUP), :]
        k = k_s[...]
        mask = lower_mask(half, half)
        left_lane = lax.broadcasted_iota(jnp.int32, (half, LANES), 1) < HEAD_DIM
        pieces = []
        for pair in range(GROUP // 2):
            x_pair = x_dt[:, pair * LANES : (pair + 1) * LANES]
            tops, lows = [], []
            for i in (2 * pair, 2 * pair + 1):
                col, row = cum[:, i : i + 1], cumt[i : i + 1, :]
                top = jnp.exp2(jnp.where(mask, col[:half] - row[:, :half], -1e30))
                low_left = jnp.exp2(col[half:] - row[:, :half])
                low_right = jnp.exp2(jnp.where(mask, col[half:] - row[:, half:], -1e30))
                tops.append((top * k[:half, :half]).astype(bf16))
                low = jnp.concatenate(
                    [
                        (low_left * k[half:, :half]).astype(bf16),
                        (low_right * k[half:, half:]).astype(bf16),
                    ],
                    axis=1,
                )
                lows.append(low)
            tops = dot(jnp.concatenate(tops, axis=0), x_pair[:half], NN)
            lows = dot(jnp.concatenate(lows, axis=0), x_pair, NN)
            pieces.append(
                jnp.concatenate(
                    [jnp.where(left_lane, both[:half], both[half:]) for both in (tops, lows)],
                    axis=0,
                )
            )
        within = jnp.concatenate(pieces, axis=1)
        ssm = within + carried + skip[...] * act
        sig = sigmoid(gate)
        silu = gate * sig
        silu_o[...] = silu.astype(bf16)
        turned_o[...] = (ssm * (sig + silu * (1.0 - sig))).astype(bf16)
        u = ssm * silu
        u_o[...] = u.astype(bf16)
        gained = u * gate_gain[...]
        u_s[:, pl.ds(pl.multiple_of(step * WIDTH, WIDTH), WIDTH)] = gained
        ssq_s[...] += jnp.sum(u * u, axis=1, keepdims=True)
        branch_o[...] += dot(gained.astype(bf16), wo[...], NN)

    @pl.when(jnp.logical_and(step == GROUPS, valid))
    def _():
        r = lax.rsqrt(ssq_s[...] * (1.0 / DI) + EPS)
        r_o[...] = r
        r = r[:, 0:1]
        for g in range(GROUPS):
            cols = slice(g * WIDTH, (g + 1) * WIDTH)
            gout_o[:, cols] = (u_s[:, cols] * r).astype(bf16)
        branch = branch_o[...] * r
        branch_o[...] = branch
        out_o[...] = (chosen(flag[0, 0], own_ref, other_ref) + branch).astype(bf16)


def bwd_body(
    flag, own_ref, other_ref, own_grad, other_grad, ngain, branch, r_ref, wo, wg, wc, wbc, taps, taps_bc, head_rows, skip,
    gate_gain, spread, gather, silu_ref, turned_ref, u_ref, act_ref, slope_ref, cin, cin_bc, step_ref,
    tail_bc_in,
    state_in, adj_in, next_in, next_bc_in,
    gout_ref, gg_o, gc_o, gin_o, gin_low_o, adj_o, next_o, next_bc_o, chan_o, chan_bc_o, ngrad_o,
    head_o,
    acc_s, kt_s, wt_s, b_s, c_s, ct_s, sp_s, cum_s, cumt_s, db_s, dc_s, rows_s, cols_s,
    direct_s, fresh_s, carry_s, edge_s, dsilu_s, q_s,
):
    step = pl.program_id(0)
    length = own_ref.shape[0]
    half = length // 2
    valid = flag[0, 2] == 1

    def carried_in(ref):
        return jnp.where(flag[0, 3] == 1, ref[...], 0.0)

    @pl.when(jnp.logical_not(valid))
    def _():
        for ref in (chan_o, chan_bc_o, ngrad_o, head_o):
            ref[...] = jnp.zeros_like(ref)

    @pl.when(jnp.logical_and(step == 0, valid))
    def _():
        gout_ref[...] = chosen_grad(flag[0, 1], own_grad, other_grad).astype(bf16)
        tap_rows = taps_bc[...]
        shifted = earlier_rows(tail_bc_in[...], cin_bc[...].astype(f32))
        pre = conv_sum(tap_rows, shifted, tap_rows[CONV : CONV + 1])
        sig = sigmoid(pre)
        dsilu_s[...] = sig * (1.0 + pre * (1.0 - sig))
        act = (pre * sig).astype(bf16)
        b_rows, c_rows = act[:, :STATE], act[:, STATE:]
        b_s[...] = b_rows
        c_s[...] = c_rows
        ct_s[...] = c_rows.astype(f32).T.astype(bf16)
        kt_s[...] = dot(b_rows, c_rows, NT)
        dt = head_steps(step_ref[...], head_rows[...])
        cum = running_sum(dt * head_rows[1:2])
        total = cum[length - 1 : length]
        sp_s[0:length] = halves(dt)
        sp_s[length : 2 * length] = halves(jnp.exp(cum))
        sp_s[2 * length :] = halves(jnp.exp(total - cum))
        for g in range(GROUPS):
            cum_s[g] = cum[:, g * GROUP : (g + 1) * GROUP] * LOG2_E
        cumt_s[...] = (cum * LOG2_E).T
        for ref in (acc_s, wt_s, db_s, dc_s, rows_s, cols_s, direct_s, fresh_s, carry_s, edge_s):
            ref[...] = jnp.zeros_like(ref)
        rowdot = jnp.sum(branch[...] * gout_ref[...].astype(f32), axis=1, keepdims=True)
        q_s[...] = jnp.broadcast_to(rowdot * (1.0 / DI), q_s.shape) * r_ref[...] * r_ref[...]

    @pl.when(jnp.logical_and(step < GROUPS, valid))
    def _():
        grad_gated = dot(gout_ref[...], wo[...], NT)
        u = u_ref[...].astype(f32)
        scaled = r_ref[:, 0:1] * grad_gated
        gain_grad = jnp.sum(scaled * u, axis=0, keepdims=True)
        grad_u = scaled * gate_gain[...] - u * q_s[:, 0:1]
        grad_ssm = grad_u * silu_ref[...].astype(f32)
        grad_gate = (grad_u * turned_ref[...].astype(f32)).astype(bf16)
        gg_o[...] = grad_gate
        act = act_ref[...].astype(f32)
        where, pick = spread[...], gather[...]
        spreads = dot(sp_s[...], where, NN)
        dt, ec, w = (spreads[i * length : (i + 1) * length] for i in range(3))
        skip_grad = jnp.sum(act * grad_ssm, axis=0, keepdims=True)
        x_dt = act * dt
        x_low, g_low = x_dt.astype(bf16), grad_ssm.astype(bf16)
        g_ec = (grad_ssm * ec).astype(bf16)
        state, adj = state_in[...], carried_in(adj_in)
        state_low, adj_low = state.astype(bf16), adj.astype(bf16)
        from_adj = w * dot(b_s[...], adj_low, NN)
        carried = ec * dot(c_s[...], state_low, NN)
        db_s[...] += dot((x_dt * w).astype(bf16), adj_low, NT)
        dc_s[...] += dot(g_ec, state_low, NT)
        last = ec[length - 1 : length]
        adj_o[...] = last * adj + dot(ct_s[...], g_ec, NN)
        edge = last * jnp.sum(state * adj, axis=0, keepdims=True)
        edge_s[...] += dot(edge.astype(bf16), pick, NN)
        cum = cum_s[step]
        start = pl.multiple_of(step * GROUP, GROUP)
        cumt = cumt_s[pl.ds(start, GROUP), :]
        kt = kt_s[...]
        mask = lax.broadcasted_iota(jnp.int32, (half, half), 0) <= lax.broadcasted_iota(
            jnp.int32, (half, half), 1
        )
        left_lane = lax.broadcasted_iota(jnp.int32, (half, LANES), 1) < HEAD_DIM
        lane_id = lax.broadcasted_iota(jnp.int32, (1, LANES), 1)
        pieces, col_sums = [], []
        row_sums = rows_s[...]
        w_tl, w_tr, w_br = wt_s[:half, :half], wt_s[:half, half:], wt_s[half:, half:]
        for pair in range(GROUP // 2):
            lanes = slice(pair * LANES, (pair + 1) * LANES)
            x_pair, g_pair = x_low[:, lanes], g_low[:, lanes]
            x_heads = [
                jnp.where(mine, x_pair[rows], jnp.zeros_like(x_pair[rows]))
                for rows in (slice(0, half), slice(half, length))
                for mine in (left_lane, jnp.logical_not(left_lane))
            ]
            p_top = dot(jnp.concatenate(x_heads[:2], axis=0), g_pair, NT)
            p_low = dot(jnp.concatenate(x_heads[2:], axis=0), g_pair[half:], NT)
            tops, lows = [], []
            for i in (2 * pair, 2 * pair + 1):
                col, row = cum[:, i : i + 1], cumt[i : i + 1, :]
                l_tl = jnp.exp2(jnp.where(mask, row[:, :half] - col[:half], -1e30))
                l_tr = jnp.exp2(row[:, half:] - col[:half])
                l_br = jnp.exp2(jnp.where(mask, row[:, half:] - col[half:], -1e30))
                lk_tl, lk_tr, lk_br = (
                    l_tl * kt[:half, :half],
                    l_tr * kt[:half, half:],
                    l_br * kt[half:, half:],
                )
                tops.append(jnp.concatenate([lk_tl.astype(bf16), lk_tr.astype(bf16)], axis=1))
                lows.append(lk_br.astype(bf16))
                of_head = slice((i % 2) * half, (i % 2 + 1) * half)
                p_tl, p_tr, p_br = p_top[of_head, :half], p_top[of_head, half:], p_low[of_head]
                w_tl, w_tr, w_br = w_tl + l_tl * p_tl, w_tr + l_tr * p_tr, w_br + l_br * p_br
                z_tl, z_tr, z_br = lk_tl * p_tl, lk_tr * p_tr, lk_br * p_br
                sums = jnp.concatenate(
                    [
                        jnp.sum(z_tl + z_tr, axis=1, keepdims=True),
                        jnp.sum(z_br, axis=1, keepdims=True),
                    ],
                    axis=0,
                )
                row_sums = row_sums + jnp.where(lane_id == start + i, sums, 0.0)
                col_sums.append(
                    jnp.concatenate(
                        [
                            jnp.sum(z_tl, axis=0, keepdims=True),
                            jnp.sum(z_tr + z_br, axis=0, keepdims=True),
                        ],
                        axis=1,
                    )
                )
            tops = dot(jnp.concatenate(tops, axis=0), g_pair, NN)
            lows = dot(jnp.concatenate(lows, axis=0), g_pair[half:], NN)
            pieces.append(
                jnp.concatenate(
                    [jnp.where(left_lane, both[:half], both[half:]) for both in (tops, lows)],
                    axis=0,
                )
            )
        wt_s[:half, :half] = w_tl
        wt_s[:half, half:] = w_tr
        wt_s[half:, half:] = w_br
        rows_s[...] = row_sums
        cols_s[pl.ds(start, GROUP), :] = jnp.concatenate(col_sums, axis=0)
        mixed_grad = jnp.concatenate(pieces, axis=1) + from_adj
        products = [act * mixed_grad, x_dt * from_adj, grad_ssm * carried]
        picked = dot(jnp.concatenate([v.astype(bf16) for v in products], axis=0), pick, NN)
        direct_s[...] += picked[:length]
        fresh_s[...] += picked[length : 2 * length]
        carry_s[...] += picked[2 * length :]
        grad_pre = (dt * mixed_grad + skip[...] * grad_ssm) * slope_ref[...].astype(f32)
        next_o[...] = grad_pre[0:8]
        later = later_rows(grad_pre, carried_in(next_in))
        grad_conv = conv_sum(taps[...], later)
        grad_conv = grad_conv.astype(bf16)
        gc_o[:, pl.ds(pl.multiple_of(step * WIDTH, WIDTH), WIDTH)] = grad_conv
        conv_in = cin[...].astype(f32)
        sums = [jnp.sum(conv_in * rows, axis=0, keepdims=True) for rows in later]
        sums += [jnp.sum(grad_pre, axis=0, keepdims=True), gain_grad, skip_grad]
        chan_o[...] = jnp.concatenate(sums + [jnp.zeros_like(skip_grad)], axis=0)
        acc_s[...] += dot(grad_gate, wg[...], NT) + dot(grad_conv, wc[...], NT)

    @pl.when(jnp.logical_and(step == GROUPS, valid))
    def _():
        wt = wt_s[...].astype(bf16)
        grad_b = db_s[...] + dot(wt, c_s[...], NN)
        grad_c = dc_s[...] + dot(wt, b_s[...], TN)
        grad_pre = jnp.concatenate([grad_b, grad_c], axis=1) * dsilu_s[...]
        next_bc_o[...] = grad_pre[0:8]
        tap_rows = taps_bc[...]
        later = later_rows(grad_pre, carried_in(next_bc_in))
        grad_conv = conv_sum(tap_rows, later)
        conv_in = cin_bc[...].astype(f32)
        sums = [jnp.sum(conv_in * rows, axis=0, keepdims=True) for rows in later]
        sums += [jnp.sum(grad_pre, axis=0, keepdims=True)]
        chan_bc_o[...] = jnp.concatenate(sums + [jnp.zeros((3, BC), f32)], axis=0)
        dt = head_steps(step_ref[...], head_rows[...])
        rate = head_rows[1:2]
        ones = jnp.where(lower_mask(length, length), 1.0, 0.0).astype(f32)
        fresh = fresh_s[...]
        from_here = cols_s[...].T - rows_s[...] + carry_s[...]
        suffix = (
            dot(ones, from_here, TN, lax.Precision.HIGHEST)
            + dot(ones, fresh, NN, lax.Precision.HIGHEST)
            - fresh
            + edge_s[0:1]
        )
        decayed = rate * suffix
        grad_step = (direct_s[...] + decayed) * sigmoid(step_ref[...] + head_rows[0:1])
        head_o[...] = jnp.concatenate(
            [
                jnp.sum(grad_step, axis=0, keepdims=True),
                jnp.sum(dt * decayed, axis=0, keepdims=True),
                jnp.zeros((6, LANES), f32),
            ],
            axis=0,
        )
        low = jnp.concatenate([grad_conv.astype(bf16), grad_step.astype(bf16)], axis=1)
        gc_o[:, DI:] = low
        grad_normed = acc_s[...] + dot(low, wbc[...], NT)
        h = chosen(flag[0, 0], own_ref, other_ref)
        scale = lax.rsqrt(jnp.mean(h * h, axis=1, keepdims=True) + EPS)
        ngrad_o[...] = jnp.sum(grad_normed * h * scale, axis=0, keepdims=True)
        weighted = grad_normed * ngain[...]
        mean = jnp.mean(h * weighted, axis=1, keepdims=True)
        grad_in = gout_ref[...].astype(f32) + scale * weighted - h * (scale * scale * scale * mean)
        gin_o[...] = grad_in
        gin_low_o[...] = grad_in.astype(bf16)


def spread_table():
    table = np.zeros((2 * LANES, DI), np.float32)
    for head in range(HEADS):
        table[head, head * HEAD_DIM : (head + 1) * HEAD_DIM] = 1.0
        table[LANES + head, head * HEAD_DIM : (head + 1) * HEAD_DIM] = 1.0
    return table


def whole(shape):
    return pl.BlockSpec(shape, lambda i: (0,) * len(shape))


def by_group(rows, width=WIDTH, skip=0):
    return pl.BlockSpec((rows, width), lambda i: (0, jnp.minimum(i, GROUPS - 1) + skip))


def tail_of(rows, width, at):
    return pl.BlockSpec((rows, width), lambda i: (0, at // width))


def gather_table():
    table = np.zeros((GROUPS, WIDTH, LANES), np.float32)
    for group in range(GROUPS):
        for column in range(WIDTH):
            table[group, column, group * GROUP + column // HEAD_DIM] = 1.0
    return table.reshape(-1, LANES)


FLAGS = pl.BlockSpec(memory_space=pltpu.SMEM)


def fwd_call(flag, own, other, params, weights, state, tail, tail_bc):
    length = own.shape[0]
    win, wo = weights
    in_specs = [
        FLAGS, whole((length, D)), whole((length, D)), whole((1, D)), by_group(D), by_group(D, WIDTH, GROUPS), tail_of(D, TAIL, 2 * DI),
        pl.BlockSpec((WIDTH, D), lambda i: (jnp.minimum(i, GROUPS - 1), 0)),
        by_group(8), tail_of(8, BC, DI), whole((8, LANES)), by_group(1), by_group(1),
        by_group(2 * LANES), by_group(16), whole((16, BC)), by_group(STATE),
    ]
    out = [
        ((length, D), bf16, whole((length, D))),
        ((length, DI), bf16, by_group(length)),
        ((length, DI), bf16, by_group(length)),
        ((length, DI), bf16, by_group(length)),
        ((length, BC), bf16, whole((length, BC))),
        ((length, LANES), f32, whole((length, LANES))),
        ((length, DI), bf16, by_group(length)),
        ((length, DI), bf16, by_group(length)),
        ((length, DI), bf16, by_group(length)),
        ((STATE, DI), f32, by_group(STATE)),
        ((length, DI), bf16, whole((length, DI))),
        ((length, LANES), f32, whole((length, LANES))),
        ((length, D), f32, whole((length, D))),
        ((length, D), bf16, whole((length, D))),
        ((16, DI), bf16, by_group(16)),
        ((16, BC), bf16, whole((16, BC))),
    ]
    scratch = [
        ((length, DI), f32), ((length, LANES), f32), ((length, length), f32),
        ((length, STATE), bf16), ((STATE, length), bf16), ((3 * length, 2 * LANES), bf16),
        ((GROUPS, length, GROUP), f32),
        ((LANES, length), f32),
    ]
    return pl.pallas_call(
        fwd_body,
        grid=(GROUPS + 1,),
        in_specs=in_specs,
        out_specs=[spec for _, _, spec in out],
        out_shape=[jax.ShapeDtypeStruct(shape, dtype) for shape, dtype, _ in out],
        scratch_shapes=[pltpu.VMEM(shape, dtype) for shape, dtype in scratch],
        compiler_params=pltpu.CompilerParams(
            dimension_semantics=("arbitrary",), vmem_limit_bytes=VMEM_LIMIT
        ),
        cost_estimate=pl.CostEstimate(flops=12 * 10**9, bytes_accessed=45 * 10**6, transcendentals=5 * 10**6),
        name="layer_forward",
    )(
        flag, own, other, params["norm_gain"], win, win, win, wo, params["taps"], params["taps"],
        params["heads"], params["skip"], params["gate_gain"], params["spread"], tail, tail_bc, state,
    )


def bwd_call(flag, own_grad, other_grad, kept, params, weights, adj, ahead, ahead_bc):
    length = own_grad.shape[0]
    win, wo = weights
    rows_of_wo = pl.BlockSpec((WIDTH, D), lambda i: (jnp.minimum(i, GROUPS - 1), 0))
    pick = pl.BlockSpec((WIDTH, LANES), lambda i: (jnp.minimum(i, GROUPS - 1), 0))
    in_specs = [
        FLAGS, whole((length, D)), whole((length, D)), whole((length, D)), whole((length, D)),
        whole((1, D)), whole((length, D)),
        whole((length, LANES)), rows_of_wo, by_group(D), by_group(D, WIDTH, GROUPS), tail_of(D, TAIL, 2 * DI),
        by_group(8), tail_of(8, BC, DI), whole((8, LANES)), by_group(1), by_group(1),
        by_group(2 * LANES), pick, by_group(length), by_group(length), by_group(length),
        by_group(length), by_group(length), by_group(length), whole((length, BC)),
        whole((length, LANES)), whole((16, BC)),
        by_group(STATE), by_group(STATE), by_group(8), whole((8, BC)),
    ]
    out = [
        ((length, D), bf16, whole((length, D))),
        ((length, DI), bf16, by_group(length)),
        ((length, DI + TAIL), bf16, whole((length, DI + TAIL))),
        ((length, D), f32, whole((length, D))),
        ((length, D), bf16, whole((length, D))),
        ((STATE, DI), f32, by_group(STATE)),
        ((8, DI), f32, by_group(8)),
        ((8, BC), f32, whole((8, BC))),
        ((8, DI), f32, by_group(8)),
        ((8, BC), f32, whole((8, BC))),
        ((1, D), f32, whole((1, D))),
        ((8, LANES), f32, whole((8, LANES))),
    ]
    scratch = [
        ((length, D), f32), ((length, length), f32), ((length, length), f32),
        ((length, STATE), bf16), ((length, STATE), bf16), ((STATE, length), bf16),
        ((3 * length, 2 * LANES), bf16),
        ((GROUPS, length, GROUP), f32), ((LANES, length), f32), ((length, STATE), f32),
        ((length, STATE), f32), ((length, LANES), f32), ((LANES, length), f32),
        ((length, LANES), f32), ((length, LANES), f32), ((length, LANES), f32), ((1, LANES), f32),
        ((length, BC), f32), ((length, LANES), f32),
    ]
    return pl.pallas_call(
        bwd_body,
        grid=(GROUPS + 1,),
        in_specs=in_specs,
        out_specs=[spec for _, _, spec in out],
        out_shape=[jax.ShapeDtypeStruct(shape, dtype) for shape, dtype, _ in out],
        scratch_shapes=[pltpu.VMEM(shape, dtype) for shape, dtype in scratch],
        compiler_params=pltpu.CompilerParams(
            dimension_semantics=("arbitrary",), vmem_limit_bytes=VMEM_LIMIT
        ),
        cost_estimate=pl.CostEstimate(flops=25 * 10**9, bytes_accessed=55 * 10**6, transcendentals=8 * 10**6),
        name="layer_backward",
    )(
        flag, kept["own"], kept["other"], own_grad, other_grad, params["norm_gain"], kept["branch"], kept["r"], wo, win, win, win,
        params["taps"], params["taps"], params["heads"], params["skip"], params["gate_gain"],
        params["spread"], params["gather"], kept["silu"], kept["turned"], kept["u"], kept["act"],
        kept["slope"], kept["cin"], kept["cin_bc"], kept["step"], kept["tail_bc"], kept["state"], adj, ahead, ahead_bc,
    )


def xor_route(size, bit):
    return [(i, i ^ bit) for i in range(size)]


def bits_of(size):
    return [1 << b for b in range(size.bit_length() - 1)]


def gather_small(row):
    for axis in ("seq", "dp"):
        size, position = lax.axis_size(axis), lax.axis_index(axis)
        for bit in bits_of(size):
            other = lax.ppermute(row, axis, xor_route(size, bit))
            row = jnp.where(
                (position & bit) == 0,
                jnp.concatenate([row, other], axis=0),
                jnp.concatenate([other, row], axis=0),
            )
    return row


def exchanges():
    return [(axis, bit) for axis in ("dp", "seq") for bit in bits_of(lax.axis_size(axis))]


def exchange(value, axis, bit):
    return value + lax.ppermute(value, axis, xor_route(lax.axis_size(axis), bit))


def sum_small(value):
    for axis, bit in exchanges():
        value = exchange(value, axis, bit)
    return value


def direct_paths():
    return lax.axis_size("dp") == 4 and lax.axis_size("seq") == 4


RING = 8


def ring_place(position):
    return jnp.where(position < 4, position, 11 - position)


def ring_route(step):
    def device(position, core):
        y, z = (0, position) if position < 4 else (1, 7 - position)
        return (y * 2 + core) * 4 + z

    return [
        (device(p, core), device((p + step) % RING, core)) for p in range(RING) for core in range(2)
    ]


def around(value, step):
    return lax.ppermute(value, ("dp", "seq"), ring_route(step))


def across(value):
    return lax.ppermute(value, "dp", xor_route(4, 1))


def own_position():
    dp, z = lax.axis_index("dp"), lax.axis_index("seq")
    y = dp // 2
    return jnp.where(y == 0, z, 7 - z), dp % 2


def together(up, down):
    pairs = [lax.optimization_barrier(pair) for pair in zip(up, down)]
    return [a for a, _ in pairs], [b for _, b in pairs]


def gather_rows(shards):
    if not direct_paths():
        return [lax.all_gather(shard, ("dp", "seq"), axis=0, tiled=True) for shard in shards]
    position, core = own_position()
    held = [jnp.zeros((16,) + shard.shape, shard.dtype) for shard in shards]

    def place(held, pieces, offset, start=0):
        at = ring_place((position + offset) % RING)
        at = (at // 4) * 8 + at % 4
        others = [across(piece) for piece in pieces]
        for of_core, values in ((core, pieces), (1 - core, others)):
            held = [
                lax.dynamic_update_slice(whole, value[None], (at + of_core * 4, start * rows, 0))
                for whole, value, rows in zip(held, values, halves_of)
            ]
        return held

    halves_of = [shard.shape[0] // 2 for shard in shards]
    up, down = shards, shards
    held = place(held, shards, 0)
    for hop in range(1, 4):
        up, down = [around(v, 1) for v in up], [around(v, -1) for v in down]
        up, down = together(up, down)
        held = place(place(held, up, -hop), down, hop)
    up = [around(v[:rows], 1) for v, rows in zip(up, halves_of)]
    down = [around(v[rows:], -1) for v, rows in zip(down, halves_of)]
    held = place(place(held, up, 4), down, 4, 1)
    return [whole.reshape((-1,) + whole.shape[2:]) for whole in held]


def reduce_rows(chips, small, early):
    position, _ = own_position()
    hops = exchanges()

    def term(chip, offset):
        at = ring_place((position + offset) % RING)
        return lax.dynamic_index_in_dim(chip, at, 0, keepdims=False)

    half = [chip.shape[1] // 2 for chip in chips]
    up = [around(term(chip, 4)[:rows], 1) for chip, rows in zip(chips, half)]
    down = [around(term(chip, -4)[rows:], -1) for chip, rows in zip(chips, half)]
    small = exchange(small, *hops[0])
    up, down = together(up, down)
    up[0], small, early = lax.optimization_barrier((up[0], small, early))
    up = [jnp.pad(v, ((0, rows), (0, 0))) for v, rows in zip(up, half)]
    down = [jnp.pad(v, ((rows, 0), (0, 0))) for v, rows in zip(down, half)]
    for hop, offset in enumerate((3, 2, 1), 1):
        up = [
            around((term(chip, offset).astype(f32) + v.astype(f32)).astype(bf16), 1)
            for chip, v in zip(chips, up)
        ]
        down = [
            around((term(chip, -offset).astype(f32) + v.astype(f32)).astype(bf16), -1)
            for chip, v in zip(chips, down)
        ]
        small = exchange(small, *hops[hop])
        up, down = together(up, down)
        up[0], small = lax.optimization_barrier((up[0], small))
    sums = [
        term(chip, 0).astype(f32) + a.astype(f32) + b.astype(f32)
        for chip, a, b in zip(chips, up, down)
    ]
    return sums, small, early


def weight_grads(pairs, small, early, ready):
    def term(columns, right):
        return jnp.einsum("td,te->de", columns, right, preferred_element_type=f32)

    if not direct_paths():
        sums = [
            lax.optimization_barrier(
                lax.psum_scatter(term(left, right), ("dp", "seq"), scatter_dimension=0, tiled=True)
            )
            for left, right in pairs
        ]
        return sums, sum_small(small), early, ready
    core = lax.axis_index("dp") % 2

    def owned(left, right, which):
        quarter = left.shape[1] // 4
        parts = [left[:, i * quarter : (i + 1) * quarter] for i in range(4)]
        chosen = jnp.concatenate(
            [jnp.where(which == 0, parts[0], parts[1]), jnp.where(which == 0, parts[2], parts[3])],
            axis=1,
        )
        return term(chosen, right).astype(bf16).reshape(RING, quarter // 4, right.shape[1])

    arrived = [across(owned(left, right, 1 - core)) for left, right in pairs]
    left, ready = lax.optimization_barrier((pairs[0][0], ready))
    chips = [
        (owned(left, right, core).astype(f32) + other.astype(f32)).astype(bf16)
        for (_, right), other in zip(pairs, arrived)
    ]
    return *reduce_rows(chips, small, early), ready


def turn(value, shift, parts):
    size = lax.axis_size("seq")
    route = [(i, i - i % parts + (i % parts + shift) % parts) for i in range(size)]
    return lax.ppermute(value, "seq", route)


def in_order(arrived):
    parts = len(arrived)
    rank = lax.axis_index("seq") % parts
    arrived = jnp.stack(arrived)
    return [
        lax.dynamic_index_in_dim(arrived, (rank - k) % parts, 0, keepdims=False)
        for k in range(parts)
    ]


def token_blocks(tokens):
    parts, length = tokens.shape[0], tokens.shape[1]
    rank, section = lax.axis_index("seq") % parts, lax.axis_index("section")
    half = length // 2
    arrived = []
    for shift in range(1, parts):
        at = ((rank + shift) % parts, section * half, 0)
        piece = lax.dynamic_slice(tokens, at, (1, half, tokens.shape[2]))[0]
        arrived.append(turn(piece, shift, parts))
    handed = lax.ppermute(jnp.concatenate(arrived, axis=0), "section", [(1, 0)])
    blocks = [lax.dynamic_index_in_dim(tokens, rank, 0, keepdims=False)]
    for i, low in enumerate(arrived):
        blocks.append(jnp.concatenate([low, handed[i * half : (i + 1) * half]], axis=0))
    return in_order(blocks)


def cotangent_blocks(rows, late):
    parts = rows.shape[0]
    size = lax.axis_size("seq")
    rank = lax.axis_index("seq") % parts
    arrived = [lax.dynamic_index_in_dim(rows, rank, 0, keepdims=False)]
    for shift in range(1, parts):
        piece = lax.dynamic_index_in_dim(rows, (rank + shift) % parts, 0, keepdims=False)
        route = [
            (size + i, size + i - i % parts + (i % parts + shift) % parts) for i in range(size)
        ]
        arrived.append(lax.ppermute(piece, ("section", "seq"), route))
    arrived, _ = lax.optimization_barrier((arrived, late))
    return in_order(arrived)


def to_pieces(blocks, sent_type):
    parts = len(blocks)
    rank = lax.axis_index("seq") % parts
    stacked = jnp.stack(blocks)
    held = stacked
    pieces = []
    for shift in range(parts):
        piece = lax.dynamic_index_in_dim(stacked, (rank + shift) % parts, 0, keepdims=False)
        if shift:
            piece = turn(piece.astype(sent_type), shift, parts)
        pieces.append(piece)
    return stacked, pieces


def laid_out(held, pieces):
    parts = len(pieces)
    rank = lax.axis_index("seq") % parts
    for shift in sorted(range(parts), key=lambda shift: 1 < shift < parts - 1):
        piece = pieces[shift].astype(held.dtype)
        held = lax.dynamic_update_slice(held, piece[None], ((rank - shift) % parts, 0, 0))
    return held


KEPT = (
    "normed", "cin", "act", "slope", "cin_bc", "step", "silu", "turned", "u", "state_out", "gout", "r",
    "branch", "out",
    "tail_out", "tail_bc_out",
)
SKEW = 2


def flags(first, grad, valid, carried=True):
    values = [jnp.where(first, 1, 0), jnp.asarray(grad, jnp.int32)]
    values += [jnp.where(flag, 1, 0) for flag in (valid, carried)]
    return jnp.stack(values).astype(jnp.int32)[None]


def shards(
    tokens, cotangent, in_proj, out_proj, conv_weight, conv_bias, norm_gain, gate_gain, step_bias,
    log_decay, skip_gain,
):
    first = lax.axis_index("section") == 0
    seq = lax.axis_size("seq")
    parts, length = tokens.shape[0], tokens.shape[1]
    owned = in_proj.shape[1]
    tokens_in = token_blocks(tokens)

    shard = jnp.pad(in_proj[0], ((0, 0), (0, TAIL - BC - HEADS)))
    weights = (
        lax.all_gather(shard, ("dp", "seq"), axis=0, tiled=True),
        gather_rows([out_proj[0]])[0],
    )

    sizes = [CONV * conv_bias.shape[1], conv_bias.shape[1], norm_gain.shape[1], gate_gain.shape[1]]
    packed = jnp.concatenate([conv_weight[0].reshape(-1), conv_bias[0], norm_gain[0], gate_gain[0]])
    packed = gather_small(packed[None]).astype(f32)
    ends = np.cumsum(sizes)
    taps, shift, gain_in, gain_gate = (
        packed[:, end - size : end] for end, size in zip(ends, sizes)
    )
    taps = jnp.swapaxes(taps.reshape(-1, CONV, conv_bias.shape[1]), 0, 1).reshape(CONV, -1)
    taps = jnp.concatenate([taps, shift.reshape(1, -1), jnp.zeros((3, taps.shape[1]), f32)], axis=0)
    lanes = ((0, 0), (0, LANES - HEADS))
    params = {
        "norm_gain": gain_in.reshape(1, -1),
        "gate_gain": gain_gate.reshape(1, -1),
        "taps": taps,
        "heads": jnp.pad(
            jnp.concatenate([step_bias, -jnp.exp(log_decay), jnp.zeros((6, HEADS), f32)], axis=0),
            lanes,
        ),
        "skip": jnp.repeat(skip_gain, HEAD_DIM, axis=1),
        "spread": jnp.asarray(spread_table(), bf16),
        "gather": jnp.asarray(gather_table(), bf16),
    }

    ticks = parts + SKEW
    hops = seq // parts

    def forward(start):
        kept, received = [], [jnp.zeros((length, D), bf16)] * SKEW
        carry = start
        for tick in range(ticks):
            if tick == SKEW:
                carry = tuple(jnp.where(first, now, at) for now, at in zip(carry, start))
            own, other = tokens_in[min(tick, parts - 1)], received[tick]
            valid = jnp.where(first, tick < parts, tick >= SKEW)
            values = dict(zip(KEPT, fwd_call(flags(first, 0, valid), own, other, params, weights, *carry)))
            values.update(own=own, other=other, state=carry[0], tail=carry[1], tail_bc=carry[2])
            carry = (values["state_out"], values["tail_out"], values["tail_bc_out"])
            kept.append(values)
            if tick < parts:
                received.append(lax.ppermute(values["out"], "section", [(0, 1)]))
        return kept

    def backward(kept, start, before_last=None):
        early = None
        zeros = tuple(jnp.zeros_like(part) for part in start)
        carry = tuple(jnp.where(first, zero, at) for zero, at in zip(zeros, start))
        grads, received = [None] * ticks, [jnp.zeros((length, D), bf16)] * SKEW
        for tick in range(ticks):
            carried = jnp.logical_not(first) if tick == SKEW and hops == 1 else True
            if tick == SKEW and hops > 1:
                carry = tuple(jnp.where(first, at, now) for now, at in zip(carry, start))
            from_loss = loss_in[max(parts - 1 - tick, 0)]
            late = jnp.int32(2 if tick >= parts else 1)
            valid = jnp.where(first, tick >= SKEW, tick < parts)
            if before_last is not None and tick == ticks - 1:
                early = before_last(grads, received[tick])
                from_loss, early = lax.optimization_barrier((from_loss, early))
            at = ticks - 1 - tick
            names = (
                "out", "gate", "conv", "in", "in_low", "adj", "next", "next_bc", "chan", "chan_bc",
                "norm", "head",
            )
            values = dict(
                zip(
                    names,
                    bwd_call(
                        flags(first, jnp.where(first, 0, late), valid, carried),
                        from_loss,
                        received[tick],
                        kept[at],
                        params,
                        weights,
                        *carry,
                    ),
                )
            )
            carry = (values["adj"], values["next"], values["next_bc"])
            grads[at] = values
            if tick < parts:
                sent, received[-1] = lax.optimization_barrier((values["in_low"], received[-1]))
                received.append(lax.ppermute(sent, "section", [(1, 0)]))
        return grads, early

    start = (jnp.zeros((STATE, DI), f32), jnp.zeros((16, DI), bf16), jnp.zeros((16, BC), bf16))
    if hops > 1:

        def onward(_, start):
            kept = forward(start)
            ends = (
                tuple(kept[parts - 1][name] for name in ("state_out", "tail_out", "tail_bc_out")),
                tuple(kept[ticks - 1][name] for name in ("state_out", "tail_out", "tail_bc_out")),
            )
            route = [(i, i + parts) for i in range(seq - parts)]
            return tuple(
                lax.ppermute(jnp.where(first, a, b), "seq", route) for a, b in zip(*ends)
            )

        start = lax.fori_loop(0, hops - 1, onward, start)
    kept = forward(start)
    cotangent, _ = lax.optimization_barrier((cotangent, kept[0]["r"]))
    loss_in = cotangent_blocks(cotangent, kept[-1]["r"])
    activations = laid_out(
        *to_pieces(
            [jnp.where(first, kept[k]["out"], kept[k + SKEW]["out"]) for k in range(parts)], bf16
        )
    )[None]

    start = (jnp.zeros((STATE, DI), f32), jnp.zeros((8, DI), f32), jnp.zeros((8, BC), f32))
    if hops > 1:

        def back(_, start):
            grads, _ = backward(kept, start)
            ends = (
                tuple(grads[0][name] for name in ("adj", "next", "next_bc")),
                tuple(grads[SKEW][name] for name in ("adj", "next", "next_bc")),
            )
            route = [(i, i - parts) for i in range(parts, seq)]
            return tuple(
                lax.ppermute(jnp.where(first, a, b), "seq", route) for a, b in zip(*ends)
            )

        start = lax.fori_loop(0, hops - 1, back, start)
    def select(values, name):
        return jnp.concatenate(
            [jnp.where(first, values[k][name], values[k + SKEW][name]) for k in range(parts)], axis=0
        )

    def out_term(grads, received):
        branch_grads = [jnp.where(first, received, loss_in[0])] + [
            jnp.where(first, grads[k]["out"], grads[k + SKEW]["out"]) for k in range(1, parts)
        ]
        return jnp.einsum(
            "td,te->de",
            select(kept, "gout"),
            jnp.concatenate(branch_grads, axis=0),
            preferred_element_type=f32,
        ).astype(bf16)

    grads, term = backward(kept, start, out_term)
    grad_out_proj = lax.psum_scatter(
        term, ("dp", "seq"), scatter_dimension=0, tiled=True
    ).astype(f32)
    normed = select(kept, "normed")
    def total(name):
        return sum(values[name] for values in grads)

    channels = jnp.concatenate([total("chan"), total("chan_bc")], axis=1)
    head = total("head")
    last_row = jnp.concatenate([total("norm"), head[0:1], head[1:2]], axis=1)
    fill = channels.shape[1] - last_row.shape[1]
    small = (channels + jnp.pad(last_row, ((7, 0), (0, fill))))
    held, pieces = to_pieces(
        [jnp.where(first, grads[k]["in"], grads[k + SKEW]["in"]) for k in range(parts)], bf16
    )
    near = [pieces[1], pieces[-1]]
    (grad_gate, grad_conv), small, grad_out_proj, near = weight_grads(
        [(normed, select(grads, "gate")), (normed, select(grads, "conv"))],
        small,
        grad_out_proj,
        near,
    )
    pieces[1], pieces[-1] = near
    pieces[2:-1], grad_gate = lax.optimization_barrier((pieces[2:-1], grad_gate))
    input_grads = laid_out(held, pieces)[None]
    grad_in_proj = jnp.concatenate([grad_gate, grad_conv[:, : DI + BC + HEADS]], axis=1)[None]

    place = lax.axis_index("dp") * seq + lax.axis_index("seq")

    def mine(flat, width):
        return lax.dynamic_slice_in_dim(flat, place * width, width, axis=flat.ndim - 1)

    width = conv_bias.shape[1]
    return (
        activations,
        input_grads,
        grad_in_proj,
        grad_out_proj[None],
        mine(small[:CONV], width)[None],
        mine(small[CONV], width)[None],
        mine(small[7, :D], owned)[None],
        mine(small[5, :DI], gate_gain.shape[1])[None],
        small[7:8, D : D + HEADS],
        small[7:8, D + LANES : D + LANES + HEADS],
        small[6, :DI].reshape(HEADS, HEAD_DIM).sum(axis=1)[None],
    )


def solution(mesh):
    placed = (
        P("dp", "seq", None),
        P("dp", "seq", None),
        P("section", ("dp", "seq"), None),
        P("section", ("dp", "seq"), None),
        P("section", None, ("dp", "seq")),
        P("section", ("dp", "seq")),
        P("section", ("dp", "seq")),
        P("section", ("dp", "seq")),
        P("section", None),
        P("section", None),
        P("section", None),
    )
    return jax.shard_map(
        shards,
        mesh=mesh,
        in_specs=placed,
        out_specs=(
            P("section", "dp", "seq", None),
            P("section", "dp", "seq", None),
        )
        + placed[2:],
        check_vma=False,
    )
```
